128 devices in a mesh: seq: 8 (over x, z_lo), fsdp: 16 (over y, z_hi, core).
Axes of the slice: x: 4, y: 4, z: 4 (z_hi: 2, z_lo: 2; z = z_hi * 2 + z_lo), core: 2. Of those that a mesh axis runs over, the one named last changes fastest.
Arguments:
- inputs: bfloat16 [2, 16, 2048, 1024], P(None, 'fsdp', 'seq'), may hold values from -6 to 6
- cotangent: bfloat16 [2, 16, 2048, 1024], P(None, 'fsdp', 'seq'), may hold values from -6 to 6
- doc_lengths: int32 [2, 16, 4], P(None, 'fsdp'), may hold values from 1 to 1536, 2048 in all within a row
- present: int32 [2, 16, 2048], P(None, 'fsdp'), may hold values 0 or 1
- w_qkv: float32 [1024, 3072], P('fsdp', 'seq'), may hold values from -0.1875 to 0.1875
- m_qkv: float32 [1024, 3072], P('fsdp', 'seq'), may hold values from -160 to 160
- v_qkv: float32 [1024, 3072], P('fsdp', 'seq'), may hold values from 1310.72 to 13107.2
- w_out: float32 [1024, 1024], P('fsdp', 'seq'), may hold values from -2 to 2
- m_out: float32 [1024, 1024], P('fsdp', 'seq'), may hold values from -48 to 48
- v_out: float32 [1024, 1024], P('fsdp', 'seq'), may hold values from 131.072 to 1310.72
- w_up: float32 [1024, 4096], P('fsdp', 'seq'), may hold values from -0.1875 to 0.1875
- m_up: float32 [1024, 4096], P('fsdp', 'seq'), may hold values from -80 to 80
- v_up: float32 [1024, 4096], P('fsdp', 'seq'), may hold values from 327.68 to 3276.8
- w_down: float32 [4096, 1024], P('fsdp', 'seq'), may hold values from -0.09375 to 0.09375
- m_down: float32 [4096, 1024], P('fsdp', 'seq'), may hold values from -80 to 80
- v_down: float32 [4096, 1024], P('fsdp', 'seq'), may hold values from 327.68 to 3276.8
- vector: float32 [13312], replicated, may hold values from -2 to 2, as said below
- m_vector: float32 [13312], replicated, may hold values from -160 to 160
- v_vector: float32 [13312], replicated, may hold values from 1310.72 to 13107.2
Outputs:
- outputs: float32 [2, 16, 2048, 1024], P(None, 'fsdp', 'seq')
- grad_inputs: float32 [2, 16, 2048, 1024], P(None, 'fsdp', 'seq')
- new_m_qkv: float32 [1024, 3072], P('fsdp', 'seq')
- new_v_qkv: float32 [1024, 3072], P('fsdp', 'seq')
- new_w_qkv: float32 [1024, 3072], P('fsdp', 'seq')
- new_m_out: float32 [1024, 1024], P('fsdp', 'seq')
- new_v_out: float32 [1024, 1024], P('fsdp', 'seq')
- new_w_out: float32 [1024, 1024], P('fsdp', 'seq')
- new_m_up: float32 [1024, 4096], P('fsdp', 'seq')
- new_v_up: float32 [1024, 4096], P('fsdp', 'seq')
- new_w_up: float32 [1024, 4096], P('fsdp', 'seq')
- new_m_down: float32 [4096, 1024], P('fsdp', 'seq')
- new_v_down: float32 [4096, 1024], P('fsdp', 'seq')
- new_w_down: float32 [4096, 1024], P('fsdp', 'seq')
- new_m_vector: float32 [13312], replicated
- new_v_vector: float32 [13312], replicated
- new_vector: float32 [13312], replicated
The draws below stay inside these ranges and needn't reach their ends.
Inputs may be any that keep to these rules, and one draw needn't show every extreme that they name: `vector`: entries of the two norms' gains lie within 0.4 to 1.6, all biases within -2 to 2.
All inputs are finite; a program needn't handle non-finite values. No bound on the sum of `present` on one device may be relied on, other than what follows from the above.
Results may differ from the reference program's by a relative error of at most 0.011.
Values may be sent and summed in bfloat16 or wider, within the bound.
A program may use at most 320 MiB of HBM per device.

```python
import math
import jax
import jax.numpy as jnp
import numpy as np
from jax import lax

D = 1024
HEADS = 16
HEAD = 64
FF = 4096
ROT = 16
WINDOW = 1024
NDOC = 4
MB = 2
STEP = 10
SEQS = 16
LEN = 2048
NTOK = 65536
VEC = 13312


def draw_vector(key, part):
    key = jax.random.fold_in(key, 7)
    draws_normal = jnp.clip(jax.random.normal(key, (VEC,), jnp.float32), -4.0, 4.0)
    positions = jnp.arange(VEC)
    is_gain = (positions < D) | (positions >= 2 * D) & (positions < 3 * D)
    return jnp.where(is_gain, 1.0 + 0.15 * draws_normal, 0.5 * draws_normal)


def set_ends(values, key, least, largest):
    longest = values.shape.index(max(values.shape))
    spots = []
    for shift in (0, 1):
        where = [jax.random.randint(jax.random.fold_in(key, axis), (), 0, length) for axis, length in enumerate(values.shape)]
        where[longest] = (where[longest] + shift) % values.shape[longest]
        spots.append(tuple(where))
    return values.at[spots[0]].set(least).at[spots[1]].set(largest)


def level_of(key, shape, shards, low, largest):
    loudness = 1.0
    for axis_at, blocks in shards:
        steps = jax.random.uniform(jax.random.fold_in(jax.random.fold_in(key, 6), axis_at), (blocks,), jnp.float32, low / len(shards), largest / len(shards))
        loudness = loudness * jnp.repeat(jnp.exp(steps), shape[axis_at] // blocks).reshape((-1,) + (1,) * (len(shape) - 1 - axis_at))
    return loudness


def split_up(amount, total, limit, skew):
    portions = [(1 << 20) // math.isqrt(grade ** skew) + 1 for grade in range(2, amount + 1)]
    spare, holding = total - limit - (amount - 1), [1] * (amount - 1)
    while spare > 0:
        free = [i for i in range(amount - 1) if holding[i] < limit]
        mass, remaining = sum([portions[i] for i in free]), spare
        for i in free:
            more = min(limit - holding[i], max(1, remaining * portions[i] // mass), spare)
            holding[i] = holding[i] + more
            spare = spare - more
    return np.array([limit] + holding)


def ragged(rng, number_of, total, bound, lean):
    if number_of == 2:
        one = jax.random.randint(rng, (), max(1, total - bound), min(bound, total - 1) + 1)
        return jnp.stack([one, total - one])
    lengths = jnp.asarray(split_up(number_of, total, bound, lean), jnp.int32)
    couples = (number_of - 1) // 2
    source_of, sink = lengths[1:1 + 2 * couples:2], lengths[2:2 + 2 * couples:2]
    room = jnp.minimum(source_of - 1, bound - sink)
    passed = jax.random.randint(jax.random.fold_in(rng, 1), (couples,), 0, 1 << 20) % (room + 1)
    lengths = lengths.at[1:1 + 2 * couples:2].set(source_of - passed).at[2:2 + 2 * couples:2].set(sink + passed)
    return lengths[jax.random.permutation(jax.random.fold_in(rng, 2), number_of)]


def noise(key, extent, scale, reach, split=(), kind=jnp.bfloat16):
    entries = scale * jax.random.normal(key, extent, jnp.float32)
    if split:
        entries = entries * level_of(key, extent, split, -0.22, 0.18)
    return jnp.clip(entries, -reach, reach).astype(kind)


def setup_inputs(seed: int = 0) -> dict:
    key_of = jax.random.split(jax.random.key(seed), 20)
    inputs = noise(key_of[0], (MB, SEQS, LEN, D), 1.0, 6.0, ((1, 16), (2, 8)))
    cotangent = noise(key_of[1], (MB, SEQS, LEN, D), 1.0, 6.0, ((1, 16), (2, 8)))
    doc_lengths = jax.vmap(lambda own: ragged(own, NDOC, LEN, LEN * 3 // 4, 2))(jax.random.split(key_of[2], MB * SEQS)).reshape((MB, SEQS, NDOC)).astype(jnp.int32)
    present = set_ends((jax.random.randint(key_of[3], (MB, SEQS, LEN), 0, 16) < 15).astype(jnp.int32), jax.random.fold_in(key_of[3], 1), 0, 1)
    w_qkv = noise(key_of[4], (D, 3 * D), D ** -0.5, 0.1875, ((0, 16), (1, 8)), jnp.float32)
    m_qkv = noise(key_of[5], (D, 3 * D), (0.1 * NTOK ** 0.5), 160.0, ((0, 16), (1, 8)), jnp.float32)
    v_qkv = jnp.clip(jnp.exp(math.log(13107.2) - 2.3025851 * jax.random.uniform(key_of[6], (D, 3 * D), jnp.float32) ** level_of(key_of[6], (D, 3 * D), ((0, 16), (1, 8)), -0.2, 0.2)), 1310.72, 13107.2)
    w_out = noise(key_of[7], (D, D), (max(1, D * 16 // LEN)) ** -0.5, 2.0, ((0, 16), (1, 8)), jnp.float32)
    m_out = noise(key_of[8], (D, D), (0.03 * NTOK ** 0.5), 48.0, ((0, 16), (1, 8)), jnp.float32)
    v_out = jnp.clip(jnp.exp(math.log(1310.72) - 2.30258502 * jax.random.uniform(key_of[9], (D, D), jnp.float32) ** level_of(key_of[9], (D, D), ((0, 16), (1, 8)), -0.2, 0.2)), 131.072, 1310.72)
    w_up = noise(key_of[10], (D, FF), D ** -0.5, 0.1875, ((0, 16), (1, 8)), jnp.float32)
    m_up = noise(key_of[11], (D, FF), (0.05 * NTOK ** 0.5), 80.0, ((0, 16), (1, 8)), jnp.float32)
    v_up = jnp.clip(jnp.exp(math.log(3276.8) - 2.3025851 * jax.random.uniform(key_of[12], (D, FF), jnp.float32) ** level_of(key_of[12], (D, FF), ((0, 16), (1, 8)), -0.2, 0.2)), 327.68, 3276.8)
    w_down = noise(key_of[13], (FF, D), FF ** -0.5, 0.09375, ((0, 16), (1, 8)), jnp.float32)
    m_down = noise(key_of[14], (FF, D), (0.05 * NTOK ** 0.5), 80.0, ((0, 16), (1, 8)), jnp.float32)
    v_down = jnp.clip(jnp.exp(math.log(3276.8) - 2.3025851 * jax.random.uniform(key_of[15], (FF, D), jnp.float32) ** level_of(key_of[15], (FF, D), ((0, 16), (1, 8)), -0.2, 0.2)), 327.68, 3276.8)
    vector = draw_vector(jax.random.fold_in(key_of[19], 71), 0)
    m_vector = noise(key_of[17], (VEC,), (0.1 * NTOK ** 0.5), 160.0, (), jnp.float32)
    v_vector = jnp.clip(jnp.exp(jax.random.uniform(key_of[18], (VEC,), jnp.float32, math.log(1310.72), math.log(13107.2))), 1310.72, 13107.2)
    return {"inputs": inputs, "cotangent": cotangent, "doc_lengths": doc_lengths, "present": present, "w_qkv": w_qkv, "m_qkv": m_qkv, "v_qkv": v_qkv, "w_out": w_out, "m_out": m_out, "v_out": v_out, "w_up": w_up, "m_up": m_up, "v_up": v_up, "w_down": w_down, "m_down": m_down, "v_down": v_down, "vector": vector, "m_vector": m_vector, "v_vector": v_vector}


BETA_ONE = 0.9
BETA_TWO = 0.95
ADAM_EPS = 1e-08
DECAY = 0.01
NORM_EPS = 1e-05
VECTOR_RATE = 0.5
BIG_NEG = -1e+30
HIGHEST = lax.Precision.HIGHEST

@jax.custom_vjp
def low(v):
    return lax.optimization_barrier(v.astype(jnp.bfloat16)).astype(jnp.float32)

@jax.custom_vjp
def low_back(v):
    return v

def low_keep(v):
    return (low(v), None)

def low_pass(kept, grad):
    return (grad,)

def back_keep(v):
    return (v, None)

def back_low(kept, grad):
    return (low(grad),)
low.defvjp(low_keep, low_pass)
low_back.defvjp(back_keep, back_low)

def split_vector(vector):
    return (vector[0:D], vector[D:2 * D], vector[2 * D:3 * D], vector[3 * D:4 * D], vector[4 * D:7 * D], vector[7 * D:8 * D], vector[8 * D:8 * D + FF], vector[8 * D + FF:9 * D + FF])

def layer_norm(values, gain, shift):
    row_mean = lax.optimization_barrier(jnp.mean(values, axis=-1, keepdims=True))
    centred = values - row_mean
    row_var = lax.optimization_barrier(jnp.mean(centred * centred, axis=-1, keepdims=True))
    return centred * lax.rsqrt(row_var + NORM_EPS) * gain + shift

def rotate(values, rot_dims):
    length = values.shape[0]
    half_dims = rot_dims // 2
    inverse = 10000.0 ** (-(jnp.arange(half_dims, dtype=jnp.float32) * 2.0) / rot_dims)
    angles = jnp.arange(length, dtype=jnp.float32)[:, None] * inverse[None, :]
    cosine = jnp.cos(angles)[:, None, :]
    sine_part = jnp.sin(angles)[:, None, :]
    lower_half = values[..., :half_dims]
    upper_half = values[..., half_dims:rot_dims]
    return jnp.concatenate([lower_half * cosine - upper_half * sine_part, upper_half * cosine + lower_half * sine_part, values[..., rot_dims:]], axis=-1)

def allowed_mask(query_pos, key_pos, query_doc, key_doc, key_live):
    is_causal = key_pos[None, :] <= query_pos[:, None]
    in_window = query_pos[:, None] - key_pos[None, :] < WINDOW
    same_doc = query_doc[:, None] == key_doc[None, :]
    on_diagonal = query_pos[:, None] == key_pos[None, :]
    return is_causal & in_window & same_doc & (key_live[None, :] > 0) | on_diagonal

def attention(query, keys, values, doc_ids, live):
    length = query.shape[0]
    block = min(512, length)
    scale = HEAD ** (-0.5)
    positions = jnp.arange(length)
    outputs = []
    for block_index in range(length // block):
        query_start = block_index * block
        key_end = query_start + block
        key_start = max(0, key_end - block - WINDOW)
        allowed = allowed_mask(positions[query_start:key_end], positions[key_start:key_end], doc_ids[query_start:key_end], doc_ids[key_start:key_end], live[key_start:key_end])

        def one_block(query_part, key_part, value_part):
            scores = jnp.einsum('qhd,khd->hqk', query_part, key_part, precision=HIGHEST) * scale
            scores = low_back(scores)
            scores = jnp.where(allowed[None], scores, BIG_NEG)
            top_score = lax.optimization_barrier(jnp.max(scores, axis=-1, keepdims=True))
            log_total = top_score + jnp.log(lax.optimization_barrier(jnp.sum(jnp.exp(scores - top_score), axis=-1, keepdims=True)))
            probs = low(jnp.exp(scores - log_total))
            return jnp.einsum('hqk,khd->qhd', probs, value_part, precision=HIGHEST)
        outputs.append(jax.checkpoint(one_block)(query[query_start:key_end], keys[key_start:key_end], values[key_start:key_end]))
    return jnp.concatenate(outputs, axis=0)

def layer(w_qkv, w_out, w_up, w_down, vector, rows_x, doc_ids, live):
    length = rows_x.shape[0]
    gain_one, shift_one, gain_two, shift_two, bias_qkv, bias_out, bias_up, bias_down = split_vector(vector)
    h_one = low(layer_norm(rows_x, gain_one, shift_one))
    h_two = low(layer_norm(rows_x, gain_two, shift_two))
    joined = low(low_back(jnp.dot(h_one, low(w_qkv), precision=HIGHEST) + bias_qkv))
    heads = joined.reshape(length, 3, HEADS, HEAD)
    query = low(rotate(heads[:, 0], ROT))
    keys = low(rotate(heads[:, 1], ROT))
    mixed = attention(query, keys, heads[:, 2], doc_ids, live)
    mixed = low(low_back(mixed.reshape(length, D)))
    attn_out = jnp.dot(mixed, low(w_out), precision=HIGHEST) + bias_out
    upper = low_back(jnp.dot(h_two, low(w_up), precision=HIGHEST) + bias_up)
    active = low(jax.nn.gelu(upper, approximate=False))
    return rows_x + attn_out + jnp.dot(active, low(w_down), precision=HIGHEST) + bias_down

def adam(weight, first, second, grad, rate):
    first_new = BETA_ONE * first + (1.0 - BETA_ONE) * grad
    second_new = BETA_TWO * second + (1.0 - BETA_TWO) * grad * grad
    first_hat = first_new / (1.0 - BETA_ONE ** STEP)
    second_hat = second_new / (1.0 - BETA_TWO ** STEP)
    weight_new = weight - rate * (first_hat / (jnp.sqrt(second_hat) + ADAM_EPS) + DECAY * weight)
    return (first_new, second_new, weight_new)

def reference(inputs, cotangent, doc_lengths, present, w_qkv, m_qkv, v_qkv, w_out, m_out, v_out, w_up, m_up, v_up, w_down, m_down, v_down, vector, m_vector, v_vector):
    count = MB * SEQS
    flat_x = inputs.reshape(count, LEN, D).astype(jnp.float32)
    flat_cot = cotangent.reshape(count, LEN, D).astype(jnp.float32)
    ends = jnp.cumsum(doc_lengths.reshape(count, NDOC), axis=-1)
    positions = jnp.arange(LEN).astype(jnp.int32)
    doc_ids = lax.optimization_barrier(jnp.sum((positions[None, :, None] >= ends[:, None, :NDOC - 1]).astype(jnp.int32), axis=-1))
    live_all = present.reshape(count, LEN)
    masters = (w_qkv, w_out, w_up, w_down, vector)

    def one_sequence(carry, items):
        rows_x, rows_cot, seq_doc, seq_live = items

        def forward(wq_arg, wo_arg, wu_arg, wd_arg, vec_arg, x_arg):
            return layer(wq_arg, wo_arg, wu_arg, wd_arg, vec_arg, x_arg, seq_doc, seq_live)
        result, puller = jax.vjp(forward, w_qkv, w_out, w_up, w_down, vector, rows_x)
        grads = puller(rows_cot)
        new_carry = tuple((total + piece for total, piece in zip(carry, grads[:5])))
        return (new_carry, (result, grads[5]))
    start = tuple((jnp.zeros_like(master) for master in masters))
    totals, (results, grad_x) = lax.scan(one_sequence, start, (flat_x, flat_cot, doc_ids, live_all))
    out_rate = max(1, D * 16 // LEN) ** (-0.5)
    new_qkv = adam(w_qkv, m_qkv, v_qkv, totals[0], D ** (-0.5))
    new_out = adam(w_out, m_out, v_out, totals[1], out_rate)
    new_up = adam(w_up, m_up, v_up, totals[2], D ** (-0.5))
    new_down = adam(w_down, m_down, v_down, totals[3], FF ** (-0.5))
    new_vec = adam(vector, m_vector, v_vector, totals[4], VECTOR_RATE)
    return (results.reshape(MB, SEQS, LEN, D), grad_x.reshape(MB, SEQS, LEN, D), new_qkv[0], new_qkv[1], new_qkv[2], new_out[0], new_out[1], new_out[2], new_up[0], new_up[1], new_up[2], new_down[0], new_down[1], new_down[2], new_vec[0], new_vec[1], new_vec[2])
```

```python
import math

import jax
import jax.numpy as jnp
from jax import lax
from jax.experimental import pallas as pl
from jax.experimental.pallas import tpu as pltpu
from jax.sharding import Mesh
from jax.sharding import PartitionSpec as P

D = 1024
HEADS = 16
HEAD = 64
FF = 4096
ROT = 16
WINDOW = 1024
NDOC = 4
STEP = 10
VEC = 13312
MB = 2
ROWS = 256
LEN = 2048
BETA_ONE = 0.9
BETA_TWO = 0.95
ADAM_EPS = 1e-08
DECAY = 0.01
NORM_EPS = 1e-05
VECTOR_RATE = 0.5
BIG_NEG = -1e30
MESH = pl.DeviceIdType.MESH
MIB = 2**20
F32 = jnp.float32
BF16 = jnp.bfloat16

SEQ = ("x", "zl")
FSDP = ("y", "zh", "c")
LEAD = (4, 2, 4, 2)
ORDERS = (("x", "y", "z"), ("y", "z", "x"), ("z", "x", "y"))
QO_ROWS = (((0, 48), (48, 48)), ((96, 32), (128, 32)), ((160, 48), (208, 48)))
UD_ROWS = (((0, 48), (48, 32)), ((80, 48), (128, 48)), ((176, 48), (224, 32)))


def dot_nn(a, b):
    return lax.dot_general(a, b, (((1,), (0,)), ((), ())), preferred_element_type=F32)


def dot_nt(a, b):
    return lax.dot_general(a, b, (((1,), (1,)), ((), ())), preferred_element_type=F32)


def dot_tn(a, b):
    return lax.dot_general(a, b, (((0,), (0,)), ((), ())), preferred_element_type=F32)


def place():
    zl, zh = lax.axis_index("zl"), lax.axis_index("zh")
    return {
        "x": lax.axis_index("x"),
        "y": lax.axis_index("y"),
        "z": zh * 2 + zl,
        "c": lax.axis_index("c"),
    }


def device(at):
    return (at["x"], lax.rem(at["z"], 2), at["y"], at["z"] // 2, at["c"])


def stepped(me, axis, by):
    at = dict(me)
    at[axis] = lax.rem(me[axis] + by + 4, 4)
    return at


def slot(sel):
    z = sel["z"]
    if isinstance(z, slice):
        return (sel["x"], slice(None), sel["y"], slice(None))
    return (sel["x"], lax.rem(z, 2), sel["y"], z // 2)


def greet(targets):
    bar = pltpu.get_barrier_semaphore()
    for t in targets:
        pl.semaphore_signal(bar, inc=1, device_id=t, device_id_type=MESH)
    pl.semaphore_wait(bar, len(targets))


def ring_neighbours(me):
    return [device(stepped(me, a, s)) for a in "xyz" for s in (1, -1)]


def run_all(gens):
    live = list(gens)
    while live:
        nxt = []
        for g in live:
            try:
                next(g)
                nxt.append(g)
            except StopIteration:
                pass
        live = nxt


class Sems:
    def __init__(self, send, recv):
        self.send, self.recv, self.at, self.copies = send, recv, 0, []

    def push(self, src, dst, to):
        k = self.at
        self.at += 1
        cp = pltpu.make_async_remote_copy(
            src_ref=src,
            dst_ref=dst,
            send_sem=self.send.at[k],
            recv_sem=self.recv.at[k],
            device_id=to,
            device_id_type=MESH,
        )
        cp.start()
        self.copies.append(cp)
        return k

    def arrived(self, k, dst, to):
        pltpu.make_async_remote_copy(
            src_ref=dst,
            dst_ref=dst,
            send_sem=self.send.at[k],
            recv_sem=self.recv.at[k],
            device_id=to,
            device_id_type=MESH,
        ).wait_recv()

    def drain(self):
        for cp in self.copies:
            cp.wait_send()


def ring_gather(ref, order, halves, sems, me):
    h1, h2 = halves
    known = set()
    for a in order:
        i = me[a]
        up, down = device(stepped(me, a, 1)), device(stepped(me, a, -1))

        def block(v, half):
            sel = {b: (slice(None) if b in known else me[b]) for b in "xyz"}
            sel[a] = v
            return ref.at[slot(sel) + (pl.ds(*half), slice(None))]

        left, right, far = lax.rem(i + 3, 4), lax.rem(i + 1, 4), lax.rem(i + 2, 4)
        r1 = sems.push(block(i, h1), block(i, h1), up)
        l2 = sems.push(block(i, h2), block(i, h2), down)
        r2 = sems.push(block(i, h2), block(i, h2), up)
        l1 = sems.push(block(i, h1), block(i, h1), down)
        yield
        sems.arrived(r1, block(left, h1), up)
        rf = sems.push(block(left, h1), block(left, h1), up)
        sems.arrived(l2, block(right, h2), down)
        lf = sems.push(block(right, h2), block(right, h2), down)
        yield
        sems.arrived(r2, block(left, h2), up)
        sems.arrived(l1, block(right, h1), down)
        sems.arrived(rf, block(far, h1), up)
        sems.arrived(lf, block(far, h2), down)
        known.add(a)


def free_dims(sel):
    dims = []
    for n, v in zip(LEAD, slot(sel)):
        if isinstance(v, slice):
            dims.append(n)
    return dims


def each_cell(sel, body):
    lead = slot(sel)
    dims = free_dims(sel)
    count = math.prod(dims)

    def at(n):
        free = []
        for d in reversed(dims):
            free.append(lax.rem(n, d))
            n = n // d
        free = free[::-1]
        full, k = [], 0
        for v in lead:
            if isinstance(v, slice):
                full.append(free[k])
                k += 1
            else:
                full.append(v)
        return tuple(full), tuple(free)

    if count == 1:
        body(*at(0))
    else:

        @pl.loop(0, count)
        def _(n):
            body(*at(n))


def ring_scatter(ref, order, halves, bufs, sems, me, out):
    h1, h2 = halves
    done = set()
    for n, a in enumerate(order):
        i = me[a]
        up, down = device(stepped(me, a, 1)), device(stepped(me, a, -1))

        def sel(v):
            s = {b: (me[b] if b in done else slice(None)) for b in "xyz"}
            s[a] = v
            return s

        def block(v, half):
            return ref.at[slot(sel(v)) + (pl.ds(*half), slice(None))]

        def add(v, half, terms, final):
            def body(full, free):
                rows = (pl.ds(*half), slice(None))
                total = ref[full + rows].astype(F32)
                for t in terms:
                    total += t[free].astype(F32)
                if final:
                    out[rows] = total
                else:
                    ref[full + rows] = total.astype(BF16)

            each_cell(sel(v), body)

        left, right, far = lax.rem(i + 3, 4), lax.rem(i + 1, 4), lax.rem(i + 2, 4)
        ra, rb, rc, la, lb, lc = bufs[n]
        c0 = sems.push(block(far, h1), ra, up)
        c1 = sems.push(block(far, h2), la, down)
        c2 = sems.push(block(right, h2), rb, up)
        c3 = sems.push(block(left, h1), lb, down)
        yield
        sems.arrived(c0, ra, up)
        add(right, h1, [ra], False)
        c4 = sems.push(block(right, h1), rc, up)
        sems.arrived(c1, la, down)
        add(left, h2, [la], False)
        c5 = sems.push(block(left, h2), lc, down)
        yield
        last = n == 2
        sems.arrived(c3, lb, down)
        sems.arrived(c4, rc, up)
        add(i, h1, [lb, rc], last)
        sems.arrived(c2, rb, up)
        sems.arrived(c5, lc, down)
        add(i, h2, [rb, lc], last)
        done.add(a)


def scatter_shapes(order, halves, lanes):
    dims = {"x": (4,), "y": (4,), "z": (2, 2)}
    left = ["x", "y", "z"]
    shapes = []
    for a in order:
        left.remove(a)
        lead = []
        if "x" in left:
            lead.append(4)
        if "z" in left:
            lead.append(2)
        if "y" in left:
            lead.append(4)
        if "z" in left:
            lead.append(2)
        n1, n2 = halves[0][1], halves[1][1]
        shapes += [tuple(lead) + (r, lanes) for r in (n1, n2, n1, n2, n1, n2)]
    return shapes


def gather_kernel(qo_ref, ud_ref, gqo, gud, send, recv, local):
    me = place()
    own = slot(me)
    c1 = pltpu.make_async_copy(qo_ref, gqo.at[own], local.at[0])
    c2 = pltpu.make_async_copy(ud_ref, gud.at[own], local.at[1])
    c1.start()
    c2.start()
    greet(ring_neighbours(me))
    c1.wait()
    c2.wait()
    sems = Sems(send, recv)
    run_all(
        [ring_gather(gqo, o, h, sems, me) for o, h in zip(ORDERS, QO_ROWS)]
        + [ring_gather(gud, o, h, sems, me) for o, h in zip(ORDERS, UD_ROWS)]
    )
    sems.drain()


def gather_weights(qo, ud):
    n = 6 * 3 * 6
    return pl.pallas_call(
        gather_kernel,
        name="gather_weights",
        out_shape=(
            jax.ShapeDtypeStruct(LEAD + (256, 128), BF16),
            jax.ShapeDtypeStruct(LEAD + (256, 256), BF16),
        ),
        in_specs=[pl.BlockSpec(memory_space=pl.ANY)] * 2,
        out_specs=[pl.BlockSpec(memory_space=pl.ANY)] * 2,
        scratch_shapes=[
            pltpu.SemaphoreType.DMA((n,)),
            pltpu.SemaphoreType.DMA((n,)),
            pltpu.SemaphoreType.DMA((2,)),
        ],
        compiler_params=pltpu.CompilerParams(collective_id=0, has_side_effects=True),
    )(qo, ud)


def scatter_kernel(pqo, pud, oqo, oud, vqo, vud, *rest):
    bufs, (send, recv, local) = rest[:-3], rest[-3:]
    me = place()
    c1 = pltpu.make_async_copy(pqo, vqo, local.at[0])
    c2 = pltpu.make_async_copy(pud, vud, local.at[1])
    c1.start()
    c2.start()
    greet(ring_neighbours(me))
    sems = Sems(send, recv)
    gens, at = [], 0
    c2.wait()
    c1.wait()
    for ref, rows, out in ((vud, UD_ROWS, oud), (vqo, QO_ROWS, oqo)):
        for o, h in zip(ORDERS, rows):
            mine = [bufs[at + 6 * n : at + 6 * n + 6] for n in range(3)]
            mine = [(b[0], b[1], b[2], b[3], b[4], b[5]) for b in mine]
            mine = [(ra, rb, rc, la, lb, lc) for (ra, rb, rc, la, lb, lc) in mine]
            gens.append(ring_scatter(ref, o, h, mine, sems, me, out))
            at += 18
    run_all(gens)
    sems.drain()


def scatter_buffers():
    shapes = []
    for rows, lanes in ((UD_ROWS, 256), (QO_ROWS, 128)):
        for o, h in zip(ORDERS, rows):
            n1, n2 = h[0][1], h[1][1]
            raw = scatter_shapes(o, h, lanes)
            for s in range(3):
                lead = raw[6 * s][:-2]
                for r in (n1, n2, n1, n2, n1, n2):
                    shapes.append(lead + (r, lanes))
    return shapes


def scatter_grads(pqo, pud):
    n = 6 * 3 * 6
    return pl.pallas_call(
        scatter_kernel,
        name="scatter_grads",
        out_shape=(
            jax.ShapeDtypeStruct((256, 128), F32),
            jax.ShapeDtypeStruct((256, 256), F32),
        ),
        in_specs=[pl.BlockSpec(memory_space=pl.ANY)] * 2,
        out_specs=[pl.BlockSpec(memory_space=pltpu.VMEM)] * 2,
        scratch_shapes=[
            pltpu.VMEM(LEAD + (256, 128), BF16),
            pltpu.VMEM(LEAD + (256, 256), BF16),
        ]
        + [pltpu.VMEM(s, BF16) for s in scatter_buffers()]
        + [
            pltpu.SemaphoreType.DMA((n,)),
            pltpu.SemaphoreType.DMA((n,)),
            pltpu.SemaphoreType.DMA((2,)),
        ],
        compiler_params=pltpu.CompilerParams(
            collective_id=1, has_side_effects=True, vmem_limit_bytes=56 * MIB
        ),
    )(pqo, pud)


def peers(me):
    out = []
    zl = lax.rem(me["z"], 2)
    for k in range(1, 8):
        at = dict(me)
        at["x"] = lax.rem(me["x"] + k // 2, 4)
        at["z"] = me["z"] - zl + lax.rem(zl + k % 2, 2)
        out.append(at)
    return out


def group_index(at):
    return at["x"] * 2 + lax.rem(at["z"], 2)


def exchange_kernel(to_heads, src, dst, send, recv, local):
    me = place()
    mine = group_index(me)

    def out_of(j):
        if to_heads:
            return src.at[j]
        return src.at[:, :, pl.ds(pl.multiple_of(j * ROWS, ROWS), ROWS), :]

    def into(j):
        if to_heads:
            return dst.at[:, :, pl.ds(pl.multiple_of(j * ROWS, ROWS), ROWS), :]
        return dst.at[j]

    own = pltpu.make_async_copy(out_of(mine), into(mine), local)
    own.start()
    others = peers(me)
    greet([device(p) for p in others])
    sems = Sems(send, recv)
    for p in others:
        sems.push(out_of(group_index(p)), into(mine), device(p))
    for k in range(7):
        frm = dict(me)
        zl = lax.rem(me["z"], 2)
        frm["x"] = lax.rem(me["x"] + 4 - (k + 1) // 2, 4)
        frm["z"] = me["z"] - zl + lax.rem(zl + (k + 1) % 2, 2)
        sems.arrived(k, into(group_index(frm)), device(frm))
    sems.drain()
    own.wait()


def exchange(array, to_heads):
    shape = (4, MB, LEN, 128) if to_heads else (8, 4, MB, ROWS, 128)

    def body(*refs):
        exchange_kernel(to_heads, *refs)

    return pl.pallas_call(
        body,
        name="to_heads" if to_heads else "to_tokens",
        out_shape=jax.ShapeDtypeStruct(shape, BF16),
        in_specs=[pl.BlockSpec(memory_space=pl.ANY)],
        out_specs=pl.BlockSpec(memory_space=pl.ANY),
        scratch_shapes=[
            pltpu.SemaphoreType.DMA((7,)),
            pltpu.SemaphoreType.DMA((7,)),
            pltpu.SemaphoreType.DMA,
        ],
        compiler_params=pltpu.CompilerParams(
            collective_id=2 if to_heads else 3, has_side_effects=True
        ),
    )(array)


def norm_parts(x):
    mean = jnp.mean(x, axis=-1, keepdims=True)
    cen = x - mean
    var = jnp.mean(cen * cen, axis=-1, keepdims=True)
    rstd = lax.rsqrt(var + NORM_EPS)
    return cen * rstd, rstd


def rope(v, table, sign):
    ahead = pltpu.roll(v, 128 - 8, 1)
    behind = pltpu.roll(v, 8, 1)
    return v * table[0] + sign * (ahead * table[1] + behind * table[2])


def pre_kernel(x_ref, g_ref, gqo, norms, bqkv, table_ref, h1_ref, h2_ref, s_ref, wt, wo):
    step = pl.program_id(0)

    @pl.when(step == 0)
    def _():
        for k in range(8):
            for r in range(8):
                cell = gqo[k // 2, k % 2, r // 2, r % 2]
                wt[k * 192 : (k + 1) * 192, r * 128 : (r + 1) * 128] = cell[:192]
                wo[r * 64 : (r + 1) * 64, k * 128 : (k + 1) * 128] = cell[192:]

    x = x_ref[0].astype(F32)
    xhat, _ = norm_parts(x)
    h1 = (xhat * norms[0:1] + norms[1:2]).astype(BF16)
    h1_ref[0] = h1
    h2_ref[0] = (xhat * norms[2:3] + norms[3:4]).astype(BF16)
    qkv = (dot_nt(h1, wt[...]) + bqkv[...]).astype(BF16)
    do = dot_nt(g_ref[0], wo[...]).astype(BF16)
    table = [jnp.concatenate([table_ref[i]] * MB, axis=0) for i in range(3)]
    for p in range(4):
        for a in range(4):
            if a < 3:
                piece = qkv[:, a * 512 + p * 128 : a * 512 + (p + 1) * 128]
            else:
                piece = do[:, p * 128 : (p + 1) * 128]
            if a < 2:
                piece = rope(piece.astype(F32), table, 1.0).astype(BF16)
            s_ref[p, 0, a] = piece.reshape(MB, ROWS, 128)


def pre(x, g, gqo, norms, bqkv, table):
    return pl.pallas_call(
        pre_kernel,
        name="pre",
        grid=(2,),
        out_shape=(
            jax.ShapeDtypeStruct((2, 512, D), BF16),
            jax.ShapeDtypeStruct((2, 512, D), BF16),
            jax.ShapeDtypeStruct((4, 2, 4, MB, ROWS, 128), BF16),
            jax.ShapeDtypeStruct((1536, D), BF16),
            jax.ShapeDtypeStruct((512, D), BF16),
        ),
        in_specs=[
            pl.BlockSpec((1, 512, D), lambda s: (s, 0, 0)),
            pl.BlockSpec((1, 512, D), lambda s: (s, 0, 0)),
            pl.BlockSpec(LEAD + (256, 128), lambda s: (0,) * 6),
            pl.BlockSpec((4, D), lambda s: (0, 0)),
            pl.BlockSpec((1, 1536), lambda s: (0, 0)),
            pl.BlockSpec((3, ROWS, 128), lambda s: (0, 0, 0)),
        ],
        out_specs=[
            pl.BlockSpec((1, 512, D), lambda s: (s, 0, 0)),
            pl.BlockSpec((1, 512, D), lambda s: (s, 0, 0)),
            pl.BlockSpec((4, 1, 4, MB, ROWS, 128), lambda s: (0, s, 0, 0, 0, 0)),
            pl.BlockSpec((1536, D), lambda s: (0, 0)),
            pl.BlockSpec((512, D), lambda s: (0, 0)),
        ],
        compiler_params=pltpu.CompilerParams(vmem_limit_bytes=56 * MIB),
    )(x, g, gqo, norms, bqkv, table)


def attention_kernel(r_ref, lo_ref, jeff_ref, table_ref, t_ref, dk, dv):
    scale = HEAD**-0.5
    lane = lax.broadcasted_iota(jnp.int32, (ROWS, 128), 1)
    first = lane < HEAD
    dk[...] = jnp.zeros_like(dk)
    dv[...] = jnp.zeros_like(dv)

    def pair(v):
        zero = jnp.zeros_like(v)
        return jnp.concatenate([jnp.where(first, v, zero), jnp.where(first, zero, v)], axis=0)

    def merge(v):
        return jnp.where(first, v[:ROWS], v[ROWS:])

    def one(q0, k0, width):
        qs, ks = pl.ds(q0, ROWS), pl.ds(k0, width)
        q = pair(r_ref[0, 0, qs])
        do = pair(r_ref[3, 0, qs])
        k, v = r_ref[1, 0, ks], r_ref[2, 0, ks]
        lo = lo_ref[0, qs]
        jeff = jeff_ref[0, :, ks]
        i = q0 + lax.broadcasted_iota(jnp.int32, (ROWS, width), 0)
        j = k0 + lax.broadcasted_iota(jnp.int32, (ROWS, width), 1)
        ok = ((jeff <= i) & (jeff >= lo)) | (i == j)
        ok = jnp.concatenate([ok, ok], axis=0)
        s = jnp.where(ok, dot_nt(q, k) * scale, BIG_NEG)
        top = jnp.max(s, axis=-1, keepdims=True)
        e = jnp.exp(s - top)
        prob = e * (1.0 / jnp.sum(e, axis=-1, keepdims=True))
        low = prob.astype(BF16)
        o = dot_nn(low, v)
        delta = jnp.sum(o * do.astype(F32), axis=-1, keepdims=True)
        ds = (prob * (dot_nt(do, v) - delta)).astype(BF16)
        t_ref[0, 0, qs] = merge(o).astype(BF16)
        dq = merge(dot_nn(ds, k)) * scale
        table = [table_ref[n, qs] for n in range(3)]
        t_ref[1, 0, qs] = rope(dq, table, -1.0).astype(BF16)
        dk[ks] += dot_tn(ds, q)
        dv[ks] += dot_tn(low, do)

    for n in range(4):
        one(n * ROWS, 0, (n + 1) * ROWS)

    @pl.loop(4, 8)
    def _(n):
        one(
            pl.multiple_of(n * ROWS, ROWS),
            pl.multiple_of((n - 4) * ROWS, ROWS),
            5 * ROWS,
        )

    table = [table_ref[n] for n in range(3)]
    t_ref[2, 0] = rope(dk[...] * scale, table, -1.0).astype(BF16)
    t_ref[3, 0] = dv[...].astype(BF16)


def attention(r, lo, jeff, table):
    return pl.pallas_call(
        attention_kernel,
        name="attention",
        grid=(MB,),
        out_shape=jax.ShapeDtypeStruct((4, MB, LEN, 128), BF16),
        in_specs=[
            pl.BlockSpec((4, 1, LEN, 128), lambda m: (0, m, 0, 0)),
            pl.BlockSpec((1, LEN, 1), lambda m: (m, 0, 0)),
            pl.BlockSpec((1, 1, LEN), lambda m: (m, 0, 0)),
            pl.BlockSpec((3, LEN, 128), lambda m: (0, 0, 0)),
        ],
        out_specs=pl.BlockSpec((4, 1, LEN, 128), lambda m: (0, m, 0, 0)),
        scratch_shapes=[pltpu.VMEM((LEN, 128), F32), pltpu.VMEM((LEN, 128), F32)],
        compiler_params=pltpu.CompilerParams(vmem_limit_bytes=56 * MIB),
    )(r, lo, jeff, table)


def ff_kernel(h_ref, g_ref, u_ref, d_ref, b_ref, y_ref, dh_ref, p_ref, db_ref):
    n = pl.program_id(0)
    h, g = h_ref[...], g_ref[...]
    wu = u_ref[0, 0].reshape(D, 256)
    wd = d_ref[:, :, 0, 0].reshape(D, 256)
    u = dot_nn(h, wu) + b_ref[0]
    ga = dot_nn(g, wd)
    cdf = 0.5 + 0.5 * lax.erf(u * (0.5**0.5))
    pdf = jnp.exp(-0.5 * u * u) * ((2.0 * math.pi) ** -0.5)
    act = (u * cdf).astype(BF16)
    du = (ga * (cdf + u * pdf)).astype(BF16)
    y = dot_nt(act, wd)
    dh = dot_nt(du, wu)

    @pl.when(n == 0)
    def _():
        y_ref[...] = y
        dh_ref[...] = dh

    @pl.when(n > 0)
    def _():
        y_ref[...] += y
        dh_ref[...] += dh

    db_ref[0] = jnp.sum(du.astype(F32), axis=0, keepdims=True)
    p_ref[n // 2, lax.rem(n, 2), :, :, 0:128] = (
        dot_tn(h, du).astype(BF16).reshape(4, 2, 128, 256)
    )
    p_ref[:, :, n // 2, lax.rem(n, 2), 128:256] = (
        dot_tn(g, act).astype(BF16).reshape(4, 2, 128, 256)
    )


def feed_forward(h, g, gud, bias):
    return pl.pallas_call(
        ff_kernel,
        name="feed_forward",
        grid=(8,),
        out_shape=(
            jax.ShapeDtypeStruct((1024, D), F32),
            jax.ShapeDtypeStruct((1024, D), F32),
            jax.ShapeDtypeStruct(LEAD + (256, 256), BF16),
            jax.ShapeDtypeStruct((8, 1, 256), F32),
        ),
        in_specs=[
            pl.BlockSpec((1024, D), lambda n: (0, 0)),
            pl.BlockSpec((1024, D), lambda n: (0, 0)),
            pl.BlockSpec((1, 1, 4, 2, 128, 256), lambda n: (n // 2, n % 2, 0, 0, 0, 0)),
            pl.BlockSpec((4, 2, 1, 1, 128, 256), lambda n: (0, 0, n // 2, n % 2, 1, 0)),
            pl.BlockSpec((1, 1, 256), lambda n: (n, 0, 0)),
        ],
        out_specs=[
            pl.BlockSpec((1024, D), lambda n: (0, 0)),
            pl.BlockSpec((1024, D), lambda n: (0, 0)),
            pl.BlockSpec(LEAD + (256, 256), lambda n: (0,) * 6),
            pl.BlockSpec((1, 1, 256), lambda n: (n, 0, 0)),
        ],
        compiler_params=pltpu.CompilerParams(vmem_limit_bytes=60 * MIB),
    )(h, g, gud, gud, bias)


def post_kernel(
    x_ref, g_ref, h_ref, u_ref, wt, wo, y_ref, dh2_ref, norms, yo_ref, dx_ref, p_ref, vec_ref, dbq_ref, dwt, dwo
):
    step = pl.program_id(0)
    g = g_ref[0]

    def heads(a):
        return jnp.concatenate([u_ref[p, 0, a].reshape(512, 128) for p in range(4)], axis=1)

    o = heads(0)
    dqkv = jnp.concatenate([heads(1), heads(2), heads(3)], axis=1)
    yo_ref[0] = y_ref[0] + dot_nn(o, wo[...])
    dh1 = dot_nn(dqkv, wt[...])
    dh2 = dh2_ref[0]
    xhat, _ = norm_parts(x_ref[0].astype(F32))
    dx_ref[0] = dh1 * norms[0:1] + dh2 * norms[2:3]
    sums = jnp.concatenate(
        [
            jnp.sum(dh1 * xhat, axis=0, keepdims=True),
            jnp.sum(dh1, axis=0, keepdims=True),
            jnp.sum(dh2 * xhat, axis=0, keepdims=True),
            jnp.sum(dh2, axis=0, keepdims=True),
            jnp.sum(g.astype(F32), axis=0, keepdims=True) * jnp.where(step == 0, 1.0, 0.0),
        ],
        axis=0,
    )
    bias = jnp.sum(dqkv.astype(F32), axis=0, keepdims=True)
    tq, to = dot_tn(dqkv, h_ref[0]), dot_tn(o, g)

    @pl.when(step == 0)
    def _():
        vec_ref[...] = sums
        dbq_ref[...] = bias
        dwt[...] = tq
        dwo[...] = to

    @pl.when(step == 1)
    def _():
        vec_ref[...] += sums
        dbq_ref[...] += bias
        dwt[...] += tq
        dwo[...] += to
        for k in range(8):
            for r in range(8):
                p_ref[k // 2, k % 2, r // 2, r % 2, 0:192] = dwt[
                    k * 192 : (k + 1) * 192, r * 128 : (r + 1) * 128
                ].astype(BF16)
                p_ref[k // 2, k % 2, r // 2, r % 2, 192:256] = dwo[
                    r * 64 : (r + 1) * 64, k * 128 : (k + 1) * 128
                ].astype(BF16)


def post(x, g, h1, u, wt, wo, y, dh2, norms):
    tok = pl.BlockSpec((1, 512, D), lambda s: (s, 0, 0))

    def whole(*shape):
        return pl.BlockSpec(shape, lambda s: (0,) * len(shape))

    return pl.pallas_call(
        post_kernel,
        name="post",
        grid=(2,),
        out_shape=(
            jax.ShapeDtypeStruct((2, 512, D), F32),
            jax.ShapeDtypeStruct((2, 512, D), F32),
            jax.ShapeDtypeStruct(LEAD + (256, 128), BF16),
            jax.ShapeDtypeStruct((5, D), F32),
            jax.ShapeDtypeStruct((1, 1536), F32),
        ),
        in_specs=[
            tok,
            tok,
            tok,
            pl.BlockSpec((4, 1, 4, MB, ROWS, 128), lambda s: (0, s, 0, 0, 0, 0)),
            whole(1536, D),
            whole(512, D),
            tok,
            tok,
            whole(4, D),
        ],
        out_specs=[tok, tok, whole(*LEAD, 256, 128), whole(5, D), whole(1, 1536)],
        scratch_shapes=[pltpu.VMEM((1536, D), F32), pltpu.VMEM((512, D), F32)],
        compiler_params=pltpu.CompilerParams(vmem_limit_bytes=60 * MIB),
    )(x, g, h1, u, wt, wo, y, dh2, norms)


def adam(weight, first, second, grad, rate):
    first_new = BETA_ONE * first + (1.0 - BETA_ONE) * grad
    second_new = BETA_TWO * second + (1.0 - BETA_TWO) * grad * grad
    first_hat = first_new / (1.0 - BETA_ONE**STEP)
    second_hat = second_new / (1.0 - BETA_TWO**STEP)
    weight_new = weight - rate * (first_hat / (jnp.sqrt(second_hat) + ADAM_EPS) + DECAY * weight)
    return (first_new, second_new, weight_new)


def swap(array):
    return lax.ppermute(array, "c", [(0, 1), (1, 0)])


def rope_table(positions):
    half = ROT // 2
    inverse = 10000.0 ** (-(jnp.arange(half, dtype=F32) * 2.0) / ROT)
    angles = positions.astype(F32)[:, None] * inverse[None, :]
    cos, sin = jnp.cos(angles), jnp.sin(angles)
    n = positions.shape[0]
    rest = HEAD - ROT
    one, zero = jnp.ones((n, rest), F32), jnp.zeros((n, rest), F32)
    none = jnp.zeros((n, half), F32)
    cols = [
        jnp.concatenate([cos, cos, one], axis=1),
        jnp.concatenate([-sin, none, zero], axis=1),
        jnp.concatenate([none, sin, zero], axis=1),
    ]
    return jnp.stack([jnp.concatenate([c, c], axis=1) for c in cols])


def pick(array, axis, core):
    return lax.dynamic_index_in_dim(array, core, axis, keepdims=False)


def by_core(own, other, core):
    return jnp.where(core == 0, jnp.stack([own, other]), jnp.stack([other, own]))


def shards(
    inputs, cotangent, doc_lengths, present,
    w_qkv, m_qkv, v_qkv, w_out, m_out, v_out, w_up, m_up, v_up, w_down, m_down, v_down,
    vector, m_vector, v_vector,
):
    core = lax.axis_index("c")
    seq = lax.axis_index(SEQ)
    zl = lax.axis_index("zl")

    wq = w_qkv.astype(BF16).reshape(64, 3, 2, HEAD)
    wu = w_up.astype(BF16).reshape(64, 2, 256)
    away = jnp.concatenate(
        [pick(wq, 2, 1 - core).reshape(-1), pick(wu, 1, 1 - core).reshape(-1)]
    )
    came = swap(away.reshape(-1, 128)).reshape(-1)
    nq = 64 * 192
    wq = by_core(pick(wq, 2, core), came[:nq].reshape(64, 3, HEAD), core)
    wu = by_core(pick(wu, 1, core), came[nq:].reshape(64, 256), core)
    qo = jnp.concatenate(
        [wq.transpose(2, 3, 0, 1).reshape(192, 128), w_out.astype(BF16)], axis=0
    )
    ud = jnp.concatenate([wu.reshape(128, 256), w_down.astype(BF16).T], axis=0)

    x_own, g_own = inputs.reshape(512, D), cotangent.reshape(512, D)
    x_oth, g_oth = swap(x_own), swap(g_own)
    x = jnp.stack([x_own, x_oth])
    g = jnp.stack([g_own, g_oth])

    positions = jnp.arange(LEN, dtype=jnp.int32)
    ends = jnp.cumsum(doc_lengths[:, 0], axis=-1)[:, : NDOC - 1]
    starts = jnp.max(
        jnp.where(ends[:, None, :] <= positions[None, :, None], ends[:, None, :], 0), axis=-1
    )
    lo = jnp.maximum(starts, positions[None] - (WINDOW - 1))
    jeff = jnp.where(present[:, 0] > 0, positions[None], LEN)
    masks = jnp.stack([lo, jeff])
    masks = jnp.where(zl == 0, masks, swap(masks))

    norms = vector[: 4 * D].reshape(4, D)
    bias_qkv = pick(vector[4 * D : 7 * D].reshape(24, 2, HEAD), 1, core).reshape(1, 1536)
    bias_out = vector[7 * D : 8 * D]
    bias_up = pick(vector[8 * D : 8 * D + FF].reshape(8, 2, 256), 1, core).reshape(8, 1, 256)
    bias_down = vector[8 * D + FF :]

    gqo, gud = gather_weights(qo, ud)
    table = rope_table(seq * ROWS + jnp.arange(ROWS, dtype=jnp.int32))
    h1, h2, sent, wt, wo = pre(x, g, gqo, norms, bias_qkv, table)
    r = exchange(sent.reshape(8, 4, MB, ROWS, 128), True)
    t = attention(r, masks[0][:, :, None], masks[1][:, None, :], rope_table(positions))
    u = exchange(t, False).reshape(4, 2, 4, MB, ROWS, 128)
    y, dh2, pud, dbu = feed_forward(h2.reshape(1024, D), g.reshape(1024, D), gud, bias_up)
    y, dxh, pqo, sums, dbq = post(
        x, g, h1, u, wt, wo, y.reshape(2, 512, D), dh2.reshape(2, 512, D), norms
    )

    other = swap(jnp.stack([y[1], dxh[1]]).astype(BF16)).astype(F32)
    xf = x_own.astype(F32)
    outputs = xf + y[0] + other[0] + (bias_out + bias_down)
    dxh = dxh[0] + other[1]
    xhat, rstd = norm_parts(xf)
    grad_inputs = g_own.astype(F32) + rstd * (
        dxh
        - jnp.mean(dxh, axis=-1, keepdims=True)
        - xhat * jnp.mean(dxh * xhat, axis=-1, keepdims=True)
    )

    oqo, oud = scatter_grads(pqo, pud)
    tq = oqo[:192].reshape(3, HEAD, 2, 64).transpose(2, 3, 0, 1)
    tu = oud[:128].reshape(2, 64, 256)
    away = jnp.concatenate(
        [pick(tq, 0, 1 - core).reshape(-1), pick(tu, 0, 1 - core).reshape(-1)]
    )
    came = swap(away.reshape(-1, 128)).reshape(-1)
    grad_qkv = by_core(pick(tq, 0, core), came[:nq].reshape(64, 3, HEAD), core)
    grad_qkv = grad_qkv.transpose(1, 2, 0, 3).reshape(64, 384)
    grad_up = by_core(pick(tu, 0, core), came[nq:].reshape(64, 256), core)
    grad_up = grad_up.transpose(1, 0, 2).reshape(64, 512)
    grad_out = oqo[192:]
    grad_down = oud[128:].T

    mine = jnp.arange(2) == core
    vec = jnp.concatenate(
        [
            sums[:4].reshape(-1),
            jnp.where(mine[None, :, None], dbq.reshape(24, 1, HEAD), 0.0).reshape(-1),
            sums[4],
            jnp.where(mine[None, :, None], dbu.reshape(8, 1, 256), 0.0).reshape(-1),
            sums[4],
        ]
    )
    vec = lax.psum(vec, SEQ + FSDP)

    out_rate = max(1, D * 16 // LEN) ** -0.5
    new_qkv = adam(w_qkv, m_qkv, v_qkv, grad_qkv, D**-0.5)
    new_out = adam(w_out, m_out, v_out, grad_out, out_rate)
    new_up = adam(w_up, m_up, v_up, grad_up, D**-0.5)
    new_down = adam(w_down, m_down, v_down, grad_down, FF**-0.5)
    new_vec = adam(vector, m_vector, v_vector, vec, VECTOR_RATE)
    shape = (MB, 1, ROWS, D)
    return (
        outputs.reshape(shape),
        grad_inputs.reshape(shape),
        *new_qkv,
        *new_out,
        *new_up,
        *new_down,
        *new_vec,
    )


def solution(mesh):
    finer = Mesh(mesh.devices.reshape(4, 2, 4, 2, 2), SEQ + FSDP)
    tokens = P(None, FSDP, SEQ, None)
    weight = P(FSDP, SEQ)
    in_specs = (tokens, tokens, P(None, FSDP, None), P(None, FSDP, None)) + (weight,) * 12 + (P(),) * 3
    out_specs = (tokens, tokens) + (weight,) * 12 + (P(),) * 3
    return jax.shard_map(
        shards, mesh=finer, in_specs=in_specs, out_specs=out_specs, check_vma=False
    )
```

```python
import math

import jax
import jax.numpy as jnp
import numpy as np
from jax import lax
from jax.experimental import pallas as pl
from jax.experimental.pallas import tpu as pltpu
from jax.sharding import Mesh
from jax.sharding import PartitionSpec as P

D = 1024
HEADS = 16
HEAD = 64
FF = 4096
ROT = 16
WINDOW = 1024
NDOC = 4
STEP = 10
VEC = 13312
MB = 2
ROWS = 256
LEN = 2048
BETA_ONE = 0.9
BETA_TWO = 0.95
ADAM_EPS = 1e-08
DECAY = 0.01
NORM_EPS = 1e-05
VECTOR_RATE = 0.5
BIG_NEG = -1e30
MESH = pl.DeviceIdType.MESH
MIB = 2**20
F32 = jnp.float32
BF16 = jnp.bfloat16

SEQ = ("x", "zl")
FSDP = ("y", "zh", "c")
LEAD = (4, 2, 4, 2)
ORDERS = (("x", "y", "z"), ("y", "z", "x"), ("z", "x", "y"))
PART_ROWS = (
    (((0, 48), (48, 48)), ((96, 32), (128, 32)), ((160, 48), (208, 48))),
    (((0, 48), (48, 32)), ((80, 48), (128, 48)), ((176, 48), (224, 32))),
    (((0, 48), (48, 32)), ((80, 48), (128, 48)), ((176, 48), (224, 32))),
)
SLOT = (256, 128)


def dot_nn(a, b):
    return lax.dot_general(a, b, (((1,), (0,)), ((), ())), preferred_element_type=F32)


def dot_nt(a, b):
    return lax.dot_general(a, b, (((1,), (1,)), ((), ())), preferred_element_type=F32)


def dot_tn(a, b):
    return lax.dot_general(a, b, (((0,), (0,)), ((), ())), preferred_element_type=F32)


def place():
    zl, zh = lax.axis_index("zl"), lax.axis_index("zh")
    return {
        "x": lax.axis_index("x"),
        "y": lax.axis_index("y"),
        "z": zh * 2 + zl,
        "c": lax.axis_index("c"),
    }


def device(at):
    return (at["x"], lax.rem(at["z"], 2), at["y"], at["z"] // 2, at["c"])


def stepped(me, axis, by):
    at = dict(me)
    at[axis] = lax.rem(me[axis] + by + 4, 4)
    return at


def slot(sel):
    z = sel["z"]
    if isinstance(z, slice):
        return (sel["x"], slice(None), sel["y"], slice(None))
    return (sel["x"], lax.rem(z, 2), sel["y"], z // 2)


def greet(targets):
    bar = pltpu.get_barrier_semaphore()
    for t in targets:
        pl.semaphore_signal(bar, inc=1, device_id=t, device_id_type=MESH)
    pl.semaphore_wait(bar, len(targets))


def ring_neighbours(me):
    return [device(stepped(me, a, s)) for a in "xyz" for s in (1, -1)]


class Steps:
    def __init__(self, gens):
        self.live = list(gens)

    def step(self):
        still = []
        for g in self.live:
            if next(g, "end") != "end":
                still.append(g)
        self.live = still

    def finish(self):
        while self.live:
            self.step()


class Sems:
    def __init__(self, send, recv, at=0):
        self.send, self.recv, self.at, self.copies = send, recv, at, []

    def push(self, src, dst, to):
        k = self.at
        self.at += 1
        cp = pltpu.make_async_remote_copy(
            src_ref=src,
            dst_ref=dst,
            send_sem=self.send.at[k],
            recv_sem=self.recv.at[k],
            device_id=to,
            device_id_type=MESH,
        )
        cp.start()
        self.copies.append(cp)
        return k

    def arrived(self, k, dst, to):
        pltpu.make_async_remote_copy(
            src_ref=dst,
            dst_ref=dst,
            send_sem=self.send.at[k],
            recv_sem=self.recv.at[k],
            device_id=to,
            device_id_type=MESH,
        ).wait_recv()

    def drain(self):
        for cp in self.copies:
            cp.wait_send()
        self.copies = []


def other_core(me):
    at = dict(me)
    at["c"] = 1 - me["c"]
    return device(at)


def ring_gather(ref, order, halves, sems, me):
    h1, h2 = halves
    known = set()
    for a in order:
        i = me[a]
        up, down = device(stepped(me, a, 1)), device(stepped(me, a, -1))

        def block(v, half):
            sel = {b: (slice(None) if b in known else me[b]) for b in "xyz"}
            sel[a] = v
            return ref.at[slot(sel) + (pl.ds(*half), slice(None))]

        left, right, far = lax.rem(i + 3, 4), lax.rem(i + 1, 4), lax.rem(i + 2, 4)
        r1 = sems.push(block(i, h1), block(i, h1), up)
        l2 = sems.push(block(i, h2), block(i, h2), down)
        r2 = sems.push(block(i, h2), block(i, h2), up)
        l1 = sems.push(block(i, h1), block(i, h1), down)
        yield 0
        sems.arrived(r1, block(left, h1), up)
        rf = sems.push(block(left, h1), block(left, h1), up)
        sems.arrived(l2, block(right, h2), down)
        lf = sems.push(block(right, h2), block(right, h2), down)
        yield 0
        sems.arrived(r2, block(left, h2), up)
        sems.arrived(l1, block(right, h1), down)
        sems.arrived(rf, block(far, h1), up)
        sems.arrived(lf, block(far, h2), down)
        known.add(a)


def free_dims(sel):
    dims = []
    for n, v in zip(LEAD, slot(sel)):
        if isinstance(v, slice):
            dims.append(n)
    return dims


def each_cell(sel, body):
    lead = slot(sel)
    dims = free_dims(sel)
    count = math.prod(dims)

    def at(n):
        free = []
        for d in reversed(dims):
            free.append(lax.rem(n, d))
            n = n // d
        free = free[::-1]
        full, k = [], 0
        for v in lead:
            if isinstance(v, slice):
                full.append(free[k])
                k += 1
            else:
                full.append(v)
        return tuple(full), tuple(free)

    if count == 1:
        body(*at(0))
    else:

        @pl.loop(0, count)
        def _(n):
            body(*at(n))


def ring_scatter(ref, order, halves, bufs, sems, me, out):
    h1, h2 = halves
    done = set()
    for n, a in enumerate(order):
        i = me[a]
        up, down = device(stepped(me, a, 1)), device(stepped(me, a, -1))

        def sel(v):
            s = {b: (me[b] if b in done else slice(None)) for b in "xyz"}
            s[a] = v
            return s

        def block(v, half):
            return ref.at[slot(sel(v)) + (pl.ds(*half), slice(None))]

        def add(v, half, terms, final):
            def body(full, free):
                rows = (pl.ds(*half), slice(None))
                total = ref[full + rows].astype(F32)
                for t in terms:
                    total += t[free].astype(F32)
                if final:
                    out[rows] = total
                else:
                    ref[full + rows] = total.astype(BF16)

            each_cell(sel(v), body)

        left, right, far = lax.rem(i + 3, 4), lax.rem(i + 1, 4), lax.rem(i + 2, 4)
        ra, rb, rc, la, lb, lc = bufs[n]
        c0 = sems.push(block(far, h1), ra, up)
        c1 = sems.push(block(far, h2), la, down)
        c2 = sems.push(block(right, h2), rb, up)
        c3 = sems.push(block(left, h1), lb, down)
        yield 0
        sems.arrived(c0, ra, up)
        add(right, h1, [ra], False)
        c4 = sems.push(block(right, h1), rc, up)
        sems.arrived(c1, la, down)
        add(left, h2, [la], False)
        c5 = sems.push(block(left, h2), lc, down)
        yield 0
        last = n == 2
        sems.arrived(c3, lb, down)
        sems.arrived(c4, rc, up)
        add(i, h1, [lb, rc], last)
        sems.arrived(c2, rb, up)
        sems.arrived(c5, lc, down)
        add(i, h2, [rb, lc], last)
        done.add(a)


def scatter_shapes(order, halves, lanes):
    dims = {"x": (4,), "y": (4,), "z": (2, 2)}
    left = ["x", "y", "z"]
    shapes = []
    for a in order:
        left.remove(a)
        lead = []
        if "x" in left:
            lead.append(4)
        if "z" in left:
            lead.append(2)
        if "y" in left:
            lead.append(4)
        if "z" in left:
            lead.append(2)
        n1, n2 = halves[0][1], halves[1][1]
        shapes += [tuple(lead) + (r, lanes) for r in (n1, n2, n1, n2, n1, n2)]
    return shapes


def scatter_buffers(phases):
    shapes = []
    for ph in phases:
        for o, h in zip(ORDERS, PART_ROWS[ph]):
            shapes += scatter_shapes(o, h, 128)
    return shapes


def start_scatter(refs, phases, bufs, sems, me, outs):
    gens, at = [], 0
    for ref, ph, out in zip(refs, phases, outs):
        for o, h in zip(ORDERS, PART_ROWS[ph]):
            mine = [bufs[at + 6 * n : at + 6 * n + 6] for n in range(3)]
            gens.append(ring_scatter(ref, o, h, mine, sems, me, out))
            at += 18
    return Steps(gens)


def peers(me):
    out = []
    zl = lax.rem(me["z"], 2)
    for k in range(1, 8):
        at = dict(me)
        at["x"] = lax.rem(me["x"] + k // 2, 4)
        at["z"] = me["z"] - zl + lax.rem(zl + k % 2, 2)
        out.append(at)
    return out


def group_index(at):
    return at["x"] * 2 + lax.rem(at["z"], 2)


def own_rows(j):
    return pl.ds(pl.multiple_of(j * ROWS, ROWS), ROWS)


def to_tokens_kernel(src, dst, send, recv, local):
    me = place()
    mine = group_index(me)
    own = pltpu.make_async_copy(src.at[:, :, own_rows(mine)], dst.at[mine], local)
    own.start()
    others = peers(me)
    greet([device(p) for p in others])
    sems = Sems(send, recv)
    for p in others:
        sems.push(src.at[:, :, own_rows(group_index(p))], dst.at[mine], device(p))
    zl = lax.rem(me["z"], 2)
    for k in range(7):
        frm = dict(me)
        frm["x"] = lax.rem(me["x"] + 4 - (k + 1) // 2, 4)
        frm["z"] = me["z"] - zl + lax.rem(zl + (k + 1) % 2, 2)
        sems.arrived(k, dst.at[group_index(frm)], device(frm))
    sems.drain()
    own.wait()


def to_tokens(array):
    return pl.pallas_call(
        to_tokens_kernel,
        name="to_tokens",
        out_shape=jax.ShapeDtypeStruct((8, 4, MB, ROWS, 128), BF16),
        in_specs=[pl.BlockSpec(memory_space=pl.ANY)],
        out_specs=pl.BlockSpec(memory_space=pl.ANY),
        scratch_shapes=[
            pltpu.SemaphoreType.DMA((7,)),
            pltpu.SemaphoreType.DMA((7,)),
            pltpu.SemaphoreType.DMA,
        ],
        compiler_params=pltpu.CompilerParams(collective_id=3, has_side_effects=True),
    )(array)


def norm_parts(x):
    mean = jnp.mean(x, axis=-1, keepdims=True)
    cen = x - mean
    var = jnp.mean(cen * cen, axis=-1, keepdims=True)
    rstd = lax.rsqrt(var + NORM_EPS)
    return cen * rstd, rstd


def rope(v, table, sign):
    lane = lax.rem(lax.broadcasted_iota(jnp.int32, v.shape, 1), HEAD)
    turned = jnp.where(lane < ROT // 2, pltpu.roll(v, 128 - ROT // 2, 1), pltpu.roll(v, ROT // 2, 1))
    return v * table[0] + (sign * turned) * table[1]


def forward_kernel(
    x_own, g_own, wq_in, wo_in, wu_in, wd_in, norms, bqkv, bup, table,
    r_out, h1_out, y_out, dh_out, db_out, p_out, wt_out, wo_out, x_oth, g_oth,
    xs, gs, gt, h1, h2, h2t, cells, wt, wo, sent, tab, wqs, awq, awu, cwq, cwu,
    send, recv, heads_send, heads_recv, local,
):
    me = place()
    core, zl, zh = me["c"], lax.rem(me["z"], 2), me["z"] // 2
    seq = group_index(me)
    partner = other_core(me)

    def load(src, dst, k):
        cp = pltpu.make_async_copy(src, dst, local.at[k])
        cp.start()
        return cp

    got_x = load(x_own, xs.at[0], 0)
    got_g = load(g_own, gs.at[0:512], 1)
    got_t = load(table.at[:, own_rows(seq)], tab, 2)

    wqs[...] = wq_in[...].T.astype(BF16).reshape(3, 2, HEAD, 64)
    gone = wqs[:, 1 - core].reshape(192, 64)
    awq[...] = jnp.concatenate([gone[:96], gone[96:]], axis=1)
    wu = wu_in[...].astype(BF16)
    awu[...] = jnp.where(core == 0, wu[:, 256:], wu[:, :256])
    others = [p for p in peers(me)]
    greet(
        [device(stepped(me, a, s)) for a in "xyz" for s in (1, -1)]
        + [partner]
        + [device(p) for k, p in enumerate(others) if k + 1 not in (1, 2, 6)]
    )
    sems = Sems(send, recv)
    kq = sems.push(awq, cwq, partner)
    ku = sems.push(awu, cwu, partner)
    kx = sems.push(x_own, x_oth, partner)
    kg = sems.push(g_own, g_oth, partner)
    own = slot(me)
    kept = wqs[:, core].reshape(192, 64)
    kept_u = jnp.where(core == 0, wu[:, :256], wu[:, 256:])
    wd = wd_in[...].T.astype(BF16)
    sems.arrived(kq, cwq, partner)
    came = jnp.concatenate([cwq[:, :64], cwq[:, 64:]], axis=0)
    cells[(0,) + own + (slice(0, 192),)] = jnp.where(
        core == 0,
        jnp.concatenate([kept, came], axis=1),
        jnp.concatenate([came, kept], axis=1),
    )
    cells[(0,) + own + (slice(192, 256),)] = wo_in[...].astype(BF16)
    sems.arrived(ku, cwu, partner)
    came_u = cwu[...]
    both = jnp.where(
        core == 0,
        jnp.concatenate([kept_u, came_u], axis=0),
        jnp.concatenate([came_u, kept_u], axis=0),
    )
    for f in range(2):
        cells[(1 + f,) + own + (slice(0, 128),)] = both[:, f * 128 : (f + 1) * 128]
        cells[(1 + f,) + own + (slice(128, 256),)] = wd[:, f * 128 : (f + 1) * 128]
    ring_sems = [Sems(send, recv, 4 + 54 * ph) for ph in range(3)]
    ring = [
        Steps(
            [
                ring_gather(cells.at[ph], o, h, ring_sems[ph], me)
                for o, h in zip(ORDERS, PART_ROWS[ph])
            ]
        )
        for ph in range(3)
    ]

    def normalise(s):
        @pl.loop(0, 4)
        def _(k):
            rows = pl.ds(pl.multiple_of(k * 128, 128), 128)
            at = pl.ds(pl.multiple_of(s * 512 + k * 128, 128), 128)
            xhat, _ = norm_parts(xs[s, rows].astype(F32))
            h1[at] = (xhat * norms[0:1] + norms[1:2]).astype(BF16)
            h2[at] = (xhat * norms[2:3] + norms[3:4]).astype(BF16)

    def turn(src, dst):
        @pl.loop(0, 4)
        def _(k):
            at = pl.ds(pl.multiple_of(k * 256, 256), 256)
            dst[:, at] = src[at].T

    for ph in range(3):
        ring[ph].step()
    got_x.wait()
    normalise(0)
    for ph in range(3):
        ring[ph].step()
    for ph in range(3):
        ring[ph].step()
    sems.arrived(kx, x_oth, partner)
    got_x = load(x_oth, xs.at[1], 0)
    for ph in range(3):
        ring[ph].step()
    ring[0].step()
    sems.arrived(kg, g_oth, partner)
    got_g.wait()
    got_g = load(g_oth, gs.at[512:1024], 1)
    got_x.wait()
    normalise(1)
    kept_h = load(h1, h1_out, 3)
    ring[0].step()
    ring[1].step()
    turn(h2, h2t)
    ring[0].finish()

    for k in range(8):
        for r in range(8):
            cell = cells[0, k // 2, k % 2, r // 2, r % 2]
            wt[k * 192 : (k + 1) * 192, r * 128 : (r + 1) * 128] = cell[:192]
            wo[r * 64 : (r + 1) * 64, k * 128 : (k + 1) * 128] = cell[192:]
    kept_w = [load(wt, wt_out, 4), load(wo, wo_out, 5)]
    got_g.wait()
    got_t.wait()

    def project(s):
        rows = slice(s * 512, (s + 1) * 512)
        do = dot_nt(gs[rows], wo[...]).astype(BF16)
        turns = [jnp.concatenate([tab[i]] * MB, axis=0) for i in range(2)]
        for a in range(4):
            if a < 3:
                part = dot_nt(h1[rows], wt[a * 512 : (a + 1) * 512])
                part = (part + bqkv[:, a * 512 : (a + 1) * 512]).astype(BF16)
            else:
                part = do
            for p in range(4):
                piece = part[:, p * 128 : (p + 1) * 128]
                if a < 2:
                    piece = rope(piece.astype(F32), turns, 1.0).astype(BF16)
                sent[p, s, a] = piece.reshape(MB, ROWS, 128)

    def heads_copy(s, dx):
        to = dict(me)
        to["x"] = lax.rem(me["x"] + dx, 4)
        to["z"] = zh * 2 + s
        return pltpu.make_async_remote_copy(
            src_ref=sent.at[to["x"], s],
            dst_ref=r_out.at[:, :, own_rows(seq)],
            send_sem=heads_send.at[s * 4 + dx],
            recv_sem=heads_recv.at[zl * 4 + dx],
            device_id=device(to),
            device_id_type=MESH,
        )

    own_heads = pltpu.make_async_copy(
        sent.at[me["x"], zl], r_out.at[:, :, own_rows(seq)], local.at[6]
    )

    def ship(s):
        for dx in (2, 1, 3):
            heads_copy(s, dx).start()

        @pl.when(zl == s)
        def _():
            own_heads.start()

        @pl.when(zl != s)
        def _():
            heads_copy(s, 0).start()

    project(0)
    ship(0)
    ring[1].step()
    ring[2].step()
    project(1)
    ship(1)
    turn(gs, gt)

    y_out[...] = jnp.zeros_like(y_out)
    dh_out[...] = jnp.zeros_like(dh_out)

    def feed(f, m):
        u_at = [(1 + f, m, k, slice(None), slice(None), slice(0, 128)) for k in range(2)]
        d_at = [(1 + f, slice(None), slice(None), m, k, slice(128, 256)) for k in range(2)]
        wu = jnp.concatenate([cells[i].reshape(D, 128) for i in u_at], axis=1)
        wd = jnp.concatenate([cells[i].reshape(D, 128) for i in d_at], axis=1)
        u = dot_nn(h2[...], wu) + bup[f, m]
        ga = dot_nn(gs[...], wd)
        cdf = 0.5 + 0.5 * lax.erf(u * (0.5**0.5))
        pdf = jnp.exp(-0.5 * u * u) * ((2.0 * math.pi) ** -0.5)
        act = (u * cdf).astype(BF16)
        du = (ga * (cdf + u * pdf)).astype(BF16)
        db_out[f, m] = jnp.sum(du.astype(F32), axis=0, keepdims=True)
        for k in range(4):
            rows = slice(k * 256, (k + 1) * 256)
            y_out[rows] += dot_nt(act[rows], wd)
            dh_out[rows] += dot_nt(du[rows], wu)
        dwu = dot_nn(h2t[...], du).astype(BF16)
        dwd = dot_nn(gt[...], act).astype(BF16)
        for k in range(2):
            lanes = slice(k * 128, (k + 1) * 128)
            cells[u_at[k]] = dwu[:, lanes].reshape(4, 2, 128, 128)
            cells[d_at[k]] = dwd[:, lanes].reshape(4, 2, 128, 128)

    for f in range(2):
        ring[1 + f].finish()
        ring_sems[1 + f].drain()

        @pl.loop(0, 2)
        def _(m):
            feed(f, m)

        if f == 0:
            ring[2].step()

        @pl.loop(2, 4)
        def _(m):
            feed(f, m)

        kept_w.append(load(cells.at[1 + f], p_out.at[f], 7 + f))

    for s in range(2):
        for dx in (2, 1, 3):
            heads_copy(s, dx).wait_send()

        @pl.when(zl != s)
        def _():
            heads_copy(s, 0).wait_send()

    for src_zl in range(2):
        for dx in range(4):
            frm = lax.rem(me["x"] + 4 - dx, 4) * 2 + src_zl

            def wait(src_zl=src_zl, dx=dx, frm=frm):
                there = dict(me)
                there["x"] = lax.rem(me["x"] + 4 - dx, 4)
                there["z"] = zh * 2 + src_zl
                pltpu.make_async_remote_copy(
                    src_ref=r_out.at[:, :, own_rows(frm)],
                    dst_ref=r_out.at[:, :, own_rows(frm)],
                    send_sem=heads_send.at[0],
                    recv_sem=heads_recv.at[src_zl * 4 + dx],
                    device_id=device(there),
                    device_id_type=MESH,
                ).wait_recv()

            if dx:
                wait()
            else:
                pl.when(zl != src_zl)(wait)

    own_heads.wait()
    ring_sems[0].drain()
    sems.drain()
    kept_h.wait()
    for cp in kept_w:
        cp.wait()


def forward(x, g, weights, norms, bqkv, bup, table):
    any_spec = pl.BlockSpec(memory_space=pl.ANY)
    vmem = pl.BlockSpec(memory_space=pltpu.VMEM)
    n = 3 * 3 * 18 + 4
    return pl.pallas_call(
        forward_kernel,
        name="forward",
        out_shape=(
            jax.ShapeDtypeStruct((4, MB, LEN, 128), BF16),
            jax.ShapeDtypeStruct((1024, D), BF16),
            jax.ShapeDtypeStruct((1024, D), F32),
            jax.ShapeDtypeStruct((1024, D), F32),
            jax.ShapeDtypeStruct((2, 4, 1, 256), F32),
            jax.ShapeDtypeStruct((2,) + LEAD + SLOT, BF16),
            jax.ShapeDtypeStruct((1536, D), BF16),
            jax.ShapeDtypeStruct((512, D), BF16),
            jax.ShapeDtypeStruct((512, D), BF16),
            jax.ShapeDtypeStruct((512, D), BF16),
        ),
        in_specs=[any_spec] * 2 + [vmem] * 7 + [any_spec],
        out_specs=[any_spec] * 2 + [vmem] * 3 + [any_spec] * 5,
        scratch_shapes=[
            pltpu.VMEM((2, 512, D), BF16),
            pltpu.VMEM((1024, D), BF16),
            pltpu.VMEM((D, 1024), BF16),
            pltpu.VMEM((1024, D), BF16),
            pltpu.VMEM((1024, D), BF16),
            pltpu.VMEM((D, 1024), BF16),
            pltpu.VMEM((3,) + LEAD + SLOT, BF16),
            pltpu.VMEM((1536, D), BF16),
            pltpu.VMEM((512, D), BF16),
            pltpu.VMEM((4, 2, 4, MB, ROWS, 128), BF16),
            pltpu.VMEM((2, ROWS, 128), F32),
            pltpu.VMEM((3, 2, HEAD, 64), BF16),
            pltpu.VMEM((96, 128), BF16),
            pltpu.VMEM((64, 256), BF16),
            pltpu.VMEM((96, 128), BF16),
            pltpu.VMEM((64, 256), BF16),
            pltpu.SemaphoreType.DMA((n,)),
            pltpu.SemaphoreType.DMA((n,)),
            pltpu.SemaphoreType.DMA((8,)),
            pltpu.SemaphoreType.DMA((8,)),
            pltpu.SemaphoreType.DMA((9,)),
        ],
        compiler_params=pltpu.CompilerParams(
            collective_id=0, has_side_effects=True, vmem_limit_bytes=62 * MIB
        ),
    )(x, g, *weights, norms, bqkv, bup, table)


def attention_kernel(
    r_ref, docs, live, table_ref, p_hbm, t_ref, out_ref, dk, dv, cells, *rest
):
    bufs, (send, recv, local) = rest[:-3], rest[-3:]
    me = place()
    got = pltpu.make_async_copy(p_hbm, cells, local)
    got.start()
    greet(ring_neighbours(me))
    got.wait()
    sems = Sems(send, recv)
    ring = start_scatter(
        [cells.at[0], cells.at[1]], (1, 2), bufs, sems, me, [out_ref.at[0], out_ref.at[1]]
    )
    ring.step()
    scale = HEAD**-0.5
    lane = lax.broadcasted_iota(jnp.int32, (ROWS, 128), 1)
    first = lane < HEAD

    def pair(v):
        zero = jnp.zeros_like(v)
        return jnp.concatenate([jnp.where(first, v, zero), jnp.where(first, zero, v)], axis=0)

    def merge(v):
        return jnp.where(first, v[:ROWS], v[ROWS:])

    def one(b, q0, k0, width):
        qs, ks = pl.ds(q0, ROWS), pl.ds(k0, width)
        q = pair(r_ref[0, b, qs])
        do = pair(r_ref[3, b, qs])
        k, v = r_ref[1, b, ks], r_ref[2, b, ks]
        row = q0 + lax.broadcasted_iota(jnp.int32, (ROWS, 1), 0)
        lo, end = row - (WINDOW - 1), 0
        for d in range(NDOC - 1):
            end = end + docs[b, d]
            lo = jnp.where(row >= end, jnp.maximum(lo, end), lo)
        col = k0 + lax.broadcasted_iota(jnp.int32, (1, width), 1)
        jeff = jnp.where(live[b, :, ks] > 0, col, LEN)
        i = q0 + lax.broadcasted_iota(jnp.int32, (ROWS, width), 0)
        j = k0 + lax.broadcasted_iota(jnp.int32, (ROWS, width), 1)
        ok = ((jeff <= i) & (jeff >= lo)) | (i == j)
        ok = jnp.concatenate([ok, ok], axis=0)
        s = jnp.where(ok, dot_nt(q, k) * scale, BIG_NEG)
        top = jnp.max(s, axis=-1, keepdims=True)
        e = jnp.exp(s - top)
        prob = e * (1.0 / jnp.sum(e, axis=-1, keepdims=True))
        low = prob.astype(BF16)
        o = dot_nn(low, v)
        delta = jnp.sum(o * do.astype(F32), axis=-1, keepdims=True)
        ds = (prob * (dot_nt(do, v) - delta)).astype(BF16)
        t_ref[0, b, qs] = merge(o).astype(BF16)
        dq = merge(dot_nn(ds, k)) * scale
        table = [table_ref[n, qs] for n in range(2)]
        t_ref[1, b, qs] = rope(dq, table, -1.0).astype(BF16)
        dk[ks] += dot_tn(ds, q)
        dv[ks] += dot_tn(low, do)

    for b in range(MB):
        dk[...] = jnp.zeros_like(dk)
        dv[...] = jnp.zeros_like(dv)
        for n in range(4):
            one(b, n * ROWS, 0, (n + 1) * ROWS)
            ring.step()
        for begin in (4, 6):

            @pl.loop(begin, begin + 2)
            def _(n):
                one(
                    b,
                    pl.multiple_of(n * ROWS, ROWS),
                    pl.multiple_of((n - 4) * ROWS, ROWS),
                    5 * ROWS,
                )

            ring.step()

        table = [table_ref[n] for n in range(2)]
        t_ref[2, b] = rope(dk[...] * scale, table, -1.0).astype(BF16)
        t_ref[3, b] = dv[...].astype(BF16)
    ring.finish()
    sems.drain()


def attention(r, docs, live, table, p):
    vmem = pl.BlockSpec(memory_space=pltpu.VMEM)
    n = 2 * 3 * 18
    return pl.pallas_call(
        attention_kernel,
        name="attention",
        out_shape=(
            jax.ShapeDtypeStruct((4, MB, LEN, 128), BF16),
            jax.ShapeDtypeStruct((2,) + SLOT, F32),
        ),
        in_specs=[
            vmem,
            pl.BlockSpec(memory_space=pltpu.SMEM),
            vmem,
            vmem,
            pl.BlockSpec(memory_space=pl.ANY),
        ],
        out_specs=[vmem] * 2,
        scratch_shapes=[
            pltpu.VMEM((LEN, 128), F32),
            pltpu.VMEM((LEN, 128), F32),
            pltpu.VMEM((2,) + LEAD + SLOT, BF16),
        ]
        + [pltpu.VMEM(s, BF16) for s in scatter_buffers((1, 2))]
        + [
            pltpu.SemaphoreType.DMA((n,)),
            pltpu.SemaphoreType.DMA((n,)),
            pltpu.SemaphoreType.DMA,
        ],
        compiler_params=pltpu.CompilerParams(
            collective_id=1, has_side_effects=True, vmem_limit_bytes=62 * MIB
        ),
    )(r, docs, live, table, p)


def vector_sum(vecs, sems, me):
    for n, a in enumerate("xyz"):
        i = me[a]
        ks = []
        for by in (1, 2, 3):
            ks.append(sems.push(vecs.at[n, i], vecs.at[n, i], device(stepped(me, a, by))))
        yield 0
        for k, by in zip(ks, (1, 2, 3)):
            frm = stepped(me, a, -by)
            sems.arrived(k, vecs.at[n, frm[a]], device(frm))
        total = vecs[n, 0] + vecs[n, 1] + vecs[n, 2] + vecs[n, 3]
        if n < 2:
            vecs[n + 1, me["xyz"[n + 1]]] = total
        else:
            vecs[3, me["c"]] = total


def backward_kernel(
    x_own, g_own, x_oth, g_oth, h_in, u_in, wt_in, wo_in, y_in, dh_in, norms, db_in, ud_in,
    y_out, dx_out, e_out, w_out, v_out,
    xs, gs, hs, us, wt, wo, ys, dhs, dqkv, os, cells, e_send, slots, vecs, *rest,
):
    bufs, (send, recv, local) = rest[:-3], rest[-3:]
    me = place()
    core = me["c"]
    partner = other_core(me)

    def load(src, dst, k):
        cp = pltpu.make_async_copy(src, dst, local.at[k])
        cp.start()
        return cp

    first = [
        load(u_in, us, 0),
        load(h_in, hs, 1),
        load(g_own, gs.at[0:512], 2),
        load(g_oth, gs.at[512:1024], 3),
    ]
    second = [
        load(wt_in, wt, 4),
        load(wo_in, wo, 5),
        load(x_own, xs.at[0], 6),
        load(x_oth, xs.at[1], 7),
        load(dh_in, dhs, 8),
        load(y_in, ys, 9),
    ]
    greet(
        ring_neighbours(me)
        + [partner]
        + [device(stepped(me, a, 2)) for a in "xyz"]
    )
    sems = Sems(send, recv)
    for cp in first:
        cp.wait()
    for s in range(2):
        rows = slice(s * 512, (s + 1) * 512)
        for p in range(4):
            for a in range(4):
                piece = us[p, s, a].reshape(512, 128)
                if a == 0:
                    os[rows, p * 128 : (p + 1) * 128] = piece
                else:
                    at = (a - 1) * 512 + p * 128
                    dqkv[rows, at : at + 128] = piece
    for m in range(4):
        part = dot_tn(dqkv[:, m * 384 : (m + 1) * 384], hs[...]).astype(BF16)
        for k in range(2):
            for r in range(8):
                cells[m, k, r // 2, r % 2, 0:192] = part[
                    k * 192 : (k + 1) * 192, r * 128 : (r + 1) * 128
                ]
    part = dot_tn(os[...], gs[...]).astype(BF16)
    for k in range(8):
        for r in range(8):
            cells[k // 2, k % 2, r // 2, r % 2, 192:256] = part[
                r * 64 : (r + 1) * 64, k * 128 : (k + 1) * 128
            ]
    slots[core, 1:3] = ud_in[...]
    ring = start_scatter([cells], (0,), bufs, sems, me, [slots.at[core, 0]])
    ring.step()
    for cp in second:
        cp.wait()
    sums = jnp.zeros((5, D), F32)
    for s in (1, 0):
        rows = slice(s * 512, (s + 1) * 512)
        y = ys[rows] + dot_nn(os[rows], wo[...])
        dh1 = dot_nn(dqkv[rows], wt[...])
        dh2 = dhs[rows]
        xhat, _ = norm_parts(xs[s].astype(F32))
        dx = dh1 * norms[0:1] + dh2 * norms[2:3]
        sums += jnp.concatenate(
            [
                jnp.sum(dh1 * xhat, axis=0, keepdims=True),
                jnp.sum(dh1, axis=0, keepdims=True),
                jnp.sum(dh2 * xhat, axis=0, keepdims=True),
                jnp.sum(dh2, axis=0, keepdims=True),
                jnp.sum(gs[rows].astype(F32), axis=0, keepdims=True) * (1.0 - s),
            ],
            axis=0,
        )
        if s == 1:
            e_send[0] = y.astype(BF16)
            e_send[1] = dx.astype(BF16)
            ke = sems.push(e_send, e_out, partner)
        else:
            y_out[...] = y
            dx_out[...] = dx
        ring.step()
    bias = jnp.sum(dqkv[...].astype(F32), axis=0, keepdims=True)
    vecs[0, me["x"]] = jnp.zeros((16, D), F32)
    vecs[0, me["x"], 0:5] = sums
    vecs[0, me["x"], 5:6] = bias[:, :1024]
    vecs[0, me["x"], 6:7, 0:512] = bias[:, 1024:]
    vecs[0, me["x"], 8:16, 0:256] = db_in[...]
    line = Steps([vector_sum(vecs, sems, me)])
    line.step()
    while ring.live or line.live:
        ring.step()
        line.step()
    kw = sems.push(slots.at[core], slots.at[core], partner)
    kv = sems.push(vecs.at[3, core], vecs.at[3, core], partner)
    sems.arrived(ke, e_out, partner)
    sems.arrived(kw, slots.at[1 - core], partner)
    sems.arrived(kv, vecs.at[3, 1 - core], partner)
    w_out[...] = slots[...]
    v_out[...] = vecs[3, 0:2]
    sems.drain()


def backward(x, g, x_oth, g_oth, h1, u, wt, wo, y, dh, norms, db, ud):
    any_spec = pl.BlockSpec(memory_space=pl.ANY)
    vmem = pl.BlockSpec(memory_space=pltpu.VMEM)
    n = 3 * 18 + 9 + 3
    return pl.pallas_call(
        backward_kernel,
        name="backward",
        out_shape=(
            jax.ShapeDtypeStruct((512, D), F32),
            jax.ShapeDtypeStruct((512, D), F32),
            jax.ShapeDtypeStruct((2, 512, D), BF16),
            jax.ShapeDtypeStruct((2, 3) + SLOT, F32),
            jax.ShapeDtypeStruct((2, 16, D), F32),
        ),
        in_specs=[any_spec] * 10 + [vmem] * 3,
        out_specs=[vmem] * 2 + [any_spec] + [vmem] * 2,
        scratch_shapes=[
            pltpu.VMEM((2, 512, D), BF16),
            pltpu.VMEM((1024, D), BF16),
            pltpu.VMEM((1024, D), BF16),
            pltpu.VMEM((4, 2, 4, MB, ROWS, 128), BF16),
            pltpu.VMEM((1536, D), BF16),
            pltpu.VMEM((512, D), BF16),
            pltpu.VMEM((1024, D), F32),
            pltpu.VMEM((1024, D), F32),
            pltpu.VMEM((1024, 1536), BF16),
            pltpu.VMEM((1024, 512), BF16),
            pltpu.VMEM(LEAD + SLOT, BF16),
            pltpu.VMEM((2, 512, D), BF16),
            pltpu.VMEM((2, 3) + SLOT, F32),
            pltpu.VMEM((4, 4, 16, D), F32),
        ]
        + [pltpu.VMEM(s, BF16) for s in scatter_buffers((0,))]
        + [
            pltpu.SemaphoreType.DMA((n,)),
            pltpu.SemaphoreType.DMA((n,)),
            pltpu.SemaphoreType.DMA((10,)),
        ],
        compiler_params=pltpu.CompilerParams(
            collective_id=2, has_side_effects=True, vmem_limit_bytes=62 * MIB
        ),
    )(x, g, x_oth, g_oth, h1, u, wt, wo, y, dh, norms, db, ud)


def adam(weight, first, second, grad, rate):
    first_new = BETA_ONE * first + (1.0 - BETA_ONE) * grad
    second_new = BETA_TWO * second + (1.0 - BETA_TWO) * grad * grad
    first_hat = first_new / (1.0 - BETA_ONE**STEP)
    second_hat = second_new / (1.0 - BETA_TWO**STEP)
    weight_new = weight - rate * (first_hat / (jnp.sqrt(second_hat) + ADAM_EPS) + DECAY * weight)
    return (first_new, second_new, weight_new)


def swap(array):
    return lax.ppermute(array, "c", [(0, 1), (1, 0)])


def rope_table():
    half = ROT // 2
    inverse = np.float32(10000.0) ** (-(np.arange(half, dtype=np.float32) * 2) / np.float32(ROT))
    angles = np.arange(LEN, dtype=np.float32)[:, None] * inverse.astype(np.float32)[None, :]
    table = np.zeros((2, LEN, 2, HEAD), np.float32)
    table[0] = 1.0
    table[0, :, :, :half] = np.cos(angles)[:, None]
    table[0, :, :, half:ROT] = np.cos(angles)[:, None]
    table[1, :, :, :half] = -np.sin(angles)[:, None]
    table[1, :, :, half:ROT] = np.sin(angles)[:, None]
    return jnp.asarray(table.reshape(2, LEN, 128))


def pick(array, axis, core):
    return lax.dynamic_index_in_dim(array, core, axis, keepdims=False)


def shards(
    inputs, cotangent, doc_lengths, present,
    w_qkv, m_qkv, v_qkv, w_out, m_out, v_out, w_up, m_up, v_up, w_down, m_down, v_down,
    vector, m_vector, v_vector,
):
    core = lax.axis_index("c")
    zl = lax.axis_index("zl")
    x_own, g_own = inputs.reshape(512, D), cotangent.reshape(512, D)

    rules = jnp.concatenate([present[:, 0], doc_lengths[:, 0]], axis=1)
    rules = jnp.where(zl == 0, rules, swap(rules))
    live, docs = rules[:, None, :LEN], rules[:, LEN:]

    norms = vector[: 4 * D].reshape(4, D)
    bias_qkv = pick(vector[4 * D : 7 * D].reshape(24, 2, HEAD), 1, core).reshape(1, 1536)
    bias_out = vector[7 * D : 8 * D]
    bias_up = pick(vector[8 * D : 8 * D + FF].reshape(4, 2, 2, 2, 128), 2, core)
    bias_up = bias_up.transpose(2, 0, 1, 3).reshape(2, 4, 1, 256)
    bias_down = vector[8 * D + FF :]
    table = rope_table()

    r, h1, y, dh2, dbu, pud, wt, wo, x_oth, g_oth = forward(
        x_own, g_own, (w_qkv, w_out, w_up, w_down), norms, bias_qkv, bias_up, table
    )
    t, oud = attention(r, docs, live, table, pud)
    u = to_tokens(t).reshape(4, 2, 4, MB, ROWS, 128)
    y, dxh, other, slots, vecs = backward(
        x_own, g_own, x_oth, g_oth, h1, u, wt, wo, y, dh2, norms, dbu.reshape(8, 256), oud
    )

    other = other.astype(F32)
    xf = x_own.astype(F32)
    outputs = xf + y + other[0] + (bias_out + bias_down)
    dxh = dxh + other[1]
    xhat, rstd = norm_parts(xf)
    grad_inputs = g_own.astype(F32) + rstd * (
        dxh
        - jnp.mean(dxh, axis=-1, keepdims=True)
        - xhat * jnp.mean(dxh * xhat, axis=-1, keepdims=True)
    )

    grad_qkv = pick(slots[:, 0, :192].reshape(2, 3, HEAD, 2, 64), 3, core)
    grad_qkv = grad_qkv.transpose(3, 1, 0, 2).reshape(64, 384)
    grad_out = pick(slots[:, 0, 192:], 0, core)
    grad_up = pick(slots[:, 1:, :128].reshape(2, 2, 2, 64, 128), 2, core)
    grad_up = grad_up.transpose(2, 0, 1, 3).reshape(64, 512)
    grad_down = pick(slots[:, 1:, 128:], 0, core)
    grad_down = grad_down.transpose(0, 2, 1).reshape(256, 128)

    whole = vecs[0, :5] + vecs[1, :5]
    vec = jnp.concatenate(
        [
            whole[:4].reshape(-1),
            vecs[:, 5:7].reshape(2, 2048)[:, :1536].reshape(2, 24, HEAD).transpose(1, 0, 2).reshape(-1),
            whole[4],
            vecs[:, 8:, :256].reshape(2, 2, 4, 2, 128).transpose(2, 3, 0, 1, 4).reshape(-1),
            whole[4],
        ]
    )

    out_rate = max(1, D * 16 // LEN) ** -0.5
    new_qkv = adam(w_qkv, m_qkv, v_qkv, grad_qkv, D**-0.5)
    new_out = adam(w_out, m_out, v_out, grad_out, out_rate)
    new_up = adam(w_up, m_up, v_up, grad_up, D**-0.5)
    new_down = adam(w_down, m_down, v_down, grad_down, FF**-0.5)
    new_vec = adam(vector, m_vector, v_vector, vec, VECTOR_RATE)
    shape = (MB, 1, ROWS, D)
    return (
        outputs.reshape(shape),
        grad_inputs.reshape(shape),
        *new_qkv,
        *new_out,
        *new_up,
        *new_down,
        *new_vec,
    )


def solution(mesh):
    finer = Mesh(mesh.devices.reshape(4, 2, 4, 2, 2), SEQ + FSDP)
    tokens = P(None, FSDP, SEQ, None)
    weight = P(FSDP, SEQ)
    in_specs = (tokens, tokens, P(None, FSDP, None), P(None, FSDP, None)) + (weight,) * 12 + (P(),) * 3
    out_specs = (tokens, tokens) + (weight,) * 12 + (P(),) * 3
    return jax.shard_map(
        shards, mesh=finer, in_specs=in_specs, out_specs=out_specs, check_vma=False
    )
```

```python
import math

import jax
import jax.numpy as jnp
import numpy as np
from jax import lax
from jax.experimental import pallas as pl
from jax.experimental.pallas import tpu as pltpu
from jax.sharding import Mesh
from jax.sharding import PartitionSpec as P

D = 1024
HEADS = 16
HEAD = 64
FF = 4096
ROT = 16
WINDOW = 1024
NDOC = 4
STEP = 10
VEC = 13312
MB = 2
ROWS = 256
LEN = 2048
BETA_ONE = 0.9
BETA_TWO = 0.95
ADAM_EPS = 1e-08
DECAY = 0.01
NORM_EPS = 1e-05
VECTOR_RATE = 0.5
BIG_NEG = -1e30
MESH = pl.DeviceIdType.MESH
MIB = 2**20
F32 = jnp.float32
BF16 = jnp.bfloat16

SEQ = ("x", "zl")
FSDP = ("y", "zh", "c")
LEAD = (4, 2, 4, 2)
QO = (
    (("x", "y", "z"), ((0, 48), (48, 32))),
    (("y", "z", "x"), ((80, 48), (128, 32))),
    (("z", "x", "y"), ((160, 48), (208, 48))),
)
UD = (
    (("x", "y", "z"), ((0, 32), (32, 16))),
    (("y", "z", "x"), ((48, 16), (64, 16))),
    (("z", "x", "y"), ((80, 96), (176, 80))),
)
GATHER = (QO, QO, QO)
SCATTER = (QO, QO, QO)
SLOT = (256, 128)


def dot_nn(a, b):
    return lax.dot_general(a, b, (((1,), (0,)), ((), ())), preferred_element_type=F32)


def dot_nt(a, b):
    return lax.dot_general(a, b, (((1,), (1,)), ((), ())), preferred_element_type=F32)


def dot_tn(a, b):
    return lax.dot_general(a, b, (((0,), (0,)), ((), ())), preferred_element_type=F32)


def place():
    zl, zh = lax.axis_index("zl"), lax.axis_index("zh")
    return {
        "x": lax.axis_index("x"),
        "y": lax.axis_index("y"),
        "z": zh * 2 + zl,
        "c": lax.axis_index("c"),
    }


def device(at):
    return (at["x"], lax.rem(at["z"], 2), at["y"], at["z"] // 2, at["c"])


def stepped(me, axis, by):
    at = dict(me)
    at[axis] = lax.rem(me[axis] + by + 4, 4)
    return at


def slot(sel):
    z = sel["z"]
    if isinstance(z, slice):
        return (sel["x"], slice(None), sel["y"], slice(None))
    return (sel["x"], lax.rem(z, 2), sel["y"], z // 2)


def greet(targets):
    bar = pltpu.get_barrier_semaphore()
    for t in targets:
        pl.semaphore_signal(bar, inc=1, device_id=t, device_id_type=MESH)
    pl.semaphore_wait(bar, len(targets))


def ring_neighbours(me):
    return [device(stepped(me, a, s)) for a in "xyz" for s in (1, -1)]


class Steps:
    def __init__(self, gens):
        self.live = list(gens)

    def step(self):
        still = []
        for g in self.live:
            if next(g, "end") != "end":
                still.append(g)
        self.live = still

    def finish(self):
        while self.live:
            self.step()


class Sems:
    def __init__(self, send, recv, at=0):
        self.send, self.recv, self.at, self.copies = send, recv, at, []

    def push(self, src, dst, to):
        k = self.at
        self.at += 1
        cp = pltpu.make_async_remote_copy(
            src_ref=src,
            dst_ref=dst,
            send_sem=self.send.at[k],
            recv_sem=self.recv.at[k],
            device_id=to,
            device_id_type=MESH,
        )
        cp.start()
        self.copies.append(cp)
        return k

    def arrived(self, k, dst, to):
        pltpu.make_async_remote_copy(
            src_ref=dst,
            dst_ref=dst,
            send_sem=self.send.at[k],
            recv_sem=self.recv.at[k],
            device_id=to,
            device_id_type=MESH,
        ).wait_recv()

    def drain(self):
        for cp in self.copies:
            cp.wait_send()
        self.copies = []


def other_core(me):
    at = dict(me)
    at["c"] = 1 - me["c"]
    return device(at)


def ring_gather(ref, order, halves, sems, me):
    h1, h2 = halves
    known = set()
    for a in order:
        i = me[a]
        up, down = device(stepped(me, a, 1)), device(stepped(me, a, -1))

        def block(v, half):
            sel = {b: (slice(None) if b in known else me[b]) for b in "xyz"}
            sel[a] = v
            return ref.at[slot(sel) + (pl.ds(*half), slice(None))]

        left, right, far = lax.rem(i + 3, 4), lax.rem(i + 1, 4), lax.rem(i + 2, 4)
        r1 = sems.push(block(i, h1), block(i, h1), up)
        l2 = sems.push(block(i, h2), block(i, h2), down)
        r2 = sems.push(block(i, h2), block(i, h2), up)
        l1 = sems.push(block(i, h1), block(i, h1), down)
        yield 0
        sems.arrived(r1, block(left, h1), up)
        rf = sems.push(block(left, h1), block(left, h1), up)
        sems.arrived(l2, block(right, h2), down)
        lf = sems.push(block(right, h2), block(right, h2), down)
        yield 0
        sems.arrived(r2, block(left, h2), up)
        sems.arrived(l1, block(right, h1), down)
        sems.arrived(rf, block(far, h1), up)
        sems.arrived(lf, block(far, h2), down)
        known.add(a)


def free_dims(sel):
    dims = []
    for n, v in zip(LEAD, slot(sel)):
        if isinstance(v, slice):
            dims.append(n)
    return dims


def each_cell(sel, body):
    lead = slot(sel)
    dims = free_dims(sel)
    count = math.prod(dims)

    def at(n):
        free = []
        for d in reversed(dims):
            free.append(lax.rem(n, d))
            n = n // d
        free = free[::-1]
        full, k = [], 0
        for v in lead:
            if isinstance(v, slice):
                full.append(free[k])
                k += 1
            else:
                full.append(v)
        return tuple(full), tuple(free)

    if count == 1:
        body(*at(0))
    else:

        @pl.loop(0, count)
        def _(n):
            body(*at(n))


def ring_scatter(ref, order, halves, bufs, sems, me, out):
    h1, h2 = halves
    done = set()
    for n, a in enumerate(order):
        i = me[a]
        up, down = device(stepped(me, a, 1)), device(stepped(me, a, -1))

        def sel(v):
            s = {b: (me[b] if b in done else slice(None)) for b in "xyz"}
            s[a] = v
            return s

        def block(v, half):
            return ref.at[slot(sel(v)) + (pl.ds(*half), slice(None))]

        def add(v, half, terms, final):
            def body(full, free):
                rows = (pl.ds(*half), slice(None))
                total = ref[full + rows].astype(F32)
                for t in terms:
                    total += t[free].astype(F32)
                if final:
                    out[rows] = total
                else:
                    ref[full + rows] = total.astype(BF16)

            each_cell(sel(v), body)

        left, right, far = lax.rem(i + 3, 4), lax.rem(i + 1, 4), lax.rem(i + 2, 4)
        ra, rb, rc, la, lb, lc = bufs[n]
        c0 = sems.push(block(far, h1), ra, up)
        c1 = sems.push(block(far, h2), la, down)
        c2 = sems.push(block(right, h2), rb, up)
        c3 = sems.push(block(left, h1), lb, down)
        yield 0
        sems.arrived(c0, ra, up)
        add(right, h1, [ra], False)
        c4 = sems.push(block(right, h1), rc, up)
        sems.arrived(c1, la, down)
        add(left, h2, [la], False)
        c5 = sems.push(block(left, h2), lc, down)
        yield 0
        last = n == 2
        sems.arrived(c3, lb, down)
        sems.arrived(c4, rc, up)
        add(i, h1, [lb, rc], last)
        sems.arrived(c2, rb, up)
        sems.arrived(c5, lc, down)
        add(i, h2, [rb, lc], last)
        done.add(a)


def scatter_shapes(order, halves, lanes):
    dims = {"x": (4,), "y": (4,), "z": (2, 2)}
    left = ["x", "y", "z"]
    shapes = []
    for a in order:
        left.remove(a)
        lead = []
        if "x" in left:
            lead.append(4)
        if "z" in left:
            lead.append(2)
        if "y" in left:
            lead.append(4)
        if "z" in left:
            lead.append(2)
        n1, n2 = halves[0][1], halves[1][1]
        shapes += [tuple(lead) + (r, lanes) for r in (n1, n2, n1, n2, n1, n2)]
    return shapes


def scatter_buffers(phases):
    shapes = []
    for ph in phases:
        for o, h in SCATTER[ph]:
            shapes += scatter_shapes(o[::-1], h, 128)
    return shapes


def start_scatter(refs, phases, bufs, sems, me, outs):
    gens, at = [], 0
    for ref, ph, out in zip(refs, phases, outs):
        for o, h in SCATTER[ph]:
            mine = [bufs[at + 6 * n : at + 6 * n + 6] for n in range(3)]
            gens.append(ring_scatter(ref, o[::-1], h, mine, sems, me, out))
            at += 18
    return Steps(gens)


def peers(me):
    out = []
    zl = lax.rem(me["z"], 2)
    for k in range(1, 8):
        at = dict(me)
        at["x"] = lax.rem(me["x"] + k // 2, 4)
        at["z"] = me["z"] - zl + lax.rem(zl + k % 2, 2)
        out.append(at)
    return out


def group_index(at):
    return at["x"] * 2 + lax.rem(at["z"], 2)


def own_rows(j):
    return pl.ds(pl.multiple_of(j * ROWS, ROWS), ROWS)


def norm_parts(x):
    mean = jnp.mean(x, axis=-1, keepdims=True)
    cen = x - mean
    var = jnp.mean(cen * cen, axis=-1, keepdims=True)
    rstd = lax.rsqrt(var + NORM_EPS)
    return cen * rstd, rstd


def rope(v, table, sign):
    lane = lax.rem(lax.broadcasted_iota(jnp.int32, v.shape, 1), HEAD)
    turned = jnp.where(lane < ROT // 2, pltpu.roll(v, 128 - ROT // 2, 1), pltpu.roll(v, ROT // 2, 1))
    return v * table[0] + (sign * turned) * table[1]


def forward_kernel(
    x_own, g_own, wq_in, wo_in, wu_in, wd_in, vec, live, docs, table,
    r_out, h1_out, y_out, dh_out, db_out, p_out, wt_out, wo_out, x_oth, g_oth, norms, live_oth, docs_oth,
    bqkv, xs, gs, gt, h1, h2, h2t, cells, wt, wo, sent, tab, wqs, awq, awu, cwq, cwu,
    send, recv, heads_send, heads_recv, local,
):
    me = place()
    core, zl, zh = me["c"], lax.rem(me["z"], 2), me["z"] // 2
    seq = group_index(me)
    partner = other_core(me)

    def load(src, dst, k):
        cp = pltpu.make_async_copy(src, dst, local.at[k])
        cp.start()
        return cp

    got_x = load(x_own, xs.at[0], 0)
    got_g = load(g_own, gs.at[0:512], 1)
    got_t = load(table.at[:, own_rows(seq)], tab, 2)

    wqs[...] = wq_in[...].T.astype(BF16).reshape(3, 2, HEAD, 64)
    gone = wqs[:, 1 - core].reshape(192, 64)
    awq[...] = jnp.concatenate([gone[:96], gone[96:]], axis=1)
    wu = wu_in[...].astype(BF16)
    awu[...] = jnp.where(core == 0, wu[:, 256:], wu[:, :256])
    others = [p for p in peers(me)]
    greet(
        [device(stepped(me, a, s)) for a in "xyz" for s in (1, -1)]
        + [partner]
        + [device(p) for k, p in enumerate(others) if k + 1 not in (1, 2, 6)]
    )
    sems = Sems(send, recv)
    kq = sems.push(awq, cwq, partner)
    ku = sems.push(awu, cwu, partner)
    kx = sems.push(x_own, x_oth, partner)
    kg = sems.push(g_own, g_oth, partner)
    kl = sems.push(live, live_oth, partner)
    kd = sems.push(docs, docs_oth, partner)
    own = slot(me)
    kept = wqs[:, core].reshape(192, 64)
    kept_u = jnp.where(core == 0, wu[:, :256], wu[:, 256:])
    wd = wd_in[...].T.astype(BF16)
    sems.arrived(kq, cwq, partner)
    came = jnp.concatenate([cwq[:, :64], cwq[:, 64:]], axis=0)
    cells[(0,) + own + (slice(0, 192),)] = jnp.where(
        core == 0,
        jnp.concatenate([kept, came], axis=1),
        jnp.concatenate([came, kept], axis=1),
    )
    cells[(0,) + own + (slice(192, 256),)] = wo_in[...].astype(BF16)
    sems.arrived(ku, cwu, partner)
    came_u = cwu[...]
    both = jnp.where(
        core == 0,
        jnp.concatenate([kept_u, came_u], axis=0),
        jnp.concatenate([came_u, kept_u], axis=0),
    )
    for f in range(2):
        cells[(1 + f,) + own + (slice(0, 128),)] = both[:, f * 128 : (f + 1) * 128]
        cells[(1 + f,) + own + (slice(128, 256),)] = wd[:, f * 128 : (f + 1) * 128]
    ring_sems = [Sems(send, recv, 6 + 54 * ph) for ph in range(3)]
    ring = [
        Steps(
            [
                ring_gather(cells.at[ph], o, h, ring_sems[ph], me)
                for o, h in GATHER[ph]
            ]
        )
        for ph in range(3)
    ]

    for i in range(4):
        for j in range(8):
            norms[i : i + 1, j * 128 : (j + 1) * 128] = vec[i * 8 + j : i * 8 + j + 1]
    for i in range(12):
        one, two = vec[32 + 2 * i : 33 + 2 * i], vec[33 + 2 * i : 34 + 2 * i]
        bqkv[:, i * 128 : (i + 1) * 128] = jnp.where(
            core == 0,
            jnp.concatenate([one[:, :64], two[:, :64]], axis=1),
            jnp.concatenate([one[:, 64:], two[:, 64:]], axis=1),
        )

    def bup(f, m):
        at = 64 + m * 8 + core * 2 + f
        return jnp.concatenate([vec[pl.ds(at, 1)], vec[pl.ds(at + 4, 1)]], axis=1)

    def normalise(s):
        @pl.loop(0, 4)
        def _(k):
            rows = pl.ds(pl.multiple_of(k * 128, 128), 128)
            at = pl.ds(pl.multiple_of(s * 512 + k * 128, 128), 128)
            xhat, _ = norm_parts(xs[s, rows].astype(F32))
            h1[at] = (xhat * norms[0:1] + norms[1:2]).astype(BF16)
            h2[at] = (xhat * norms[2:3] + norms[3:4]).astype(BF16)

    def turn(src, dst):
        @pl.loop(0, 4)
        def _(k):
            at = pl.ds(pl.multiple_of(k * 256, 256), 256)
            dst[:, at] = src[at].T

    for ph in range(3):
        ring[ph].step()
    got_x.wait()
    normalise(0)
    for ph in range(3):
        ring[ph].step()
    for ph in range(3):
        ring[ph].step()
    sems.arrived(kx, x_oth, partner)
    got_x = load(x_oth, xs.at[1], 0)
    for ph in range(3):
        ring[ph].step()
    ring[0].step()
    sems.arrived(kg, g_oth, partner)
    got_g.wait()
    got_g = load(g_oth, gs.at[512:1024], 1)
    got_x.wait()
    normalise(1)
    kept_h = load(h1, h1_out, 3)
    ring[0].step()
    ring[1].step()
    turn(h2, h2t)
    ring[0].finish()

    for k in range(8):
        for r in range(8):
            cell = cells[0, k // 2, k % 2, r // 2, r % 2]
            wt[k * 192 : (k + 1) * 192, r * 128 : (r + 1) * 128] = cell[:192]
            wo[r * 64 : (r + 1) * 64, k * 128 : (k + 1) * 128] = cell[192:]
    kept_w = [load(wt, wt_out, 4), load(wo, wo_out, 5)]
    got_g.wait()
    got_t.wait()

    def project(s):
        rows = slice(s * 512, (s + 1) * 512)
        do = dot_nt(gs[rows], wo[...]).astype(BF16)
        turns = [jnp.concatenate([tab[i]] * MB, axis=0) for i in range(2)]
        for a in range(4):
            if a < 3:
                part = dot_nt(h1[rows], wt[a * 512 : (a + 1) * 512])
                part = (part + bqkv[:, a * 512 : (a + 1) * 512]).astype(BF16)
            else:
                part = do
            for p in range(4):
                piece = part[:, p * 128 : (p + 1) * 128]
                if a < 2:
                    piece = rope(piece.astype(F32), turns, 1.0).astype(BF16)
                sent[p, s, a] = piece.reshape(MB, ROWS, 128)

    def heads_copy(s, dx):
        to = dict(me)
        to["x"] = lax.rem(me["x"] + dx, 4)
        to["z"] = zh * 2 + s
        return pltpu.make_async_remote_copy(
            src_ref=sent.at[to["x"], s],
            dst_ref=r_out.at[:, :, own_rows(seq)],
            send_sem=heads_send.at[s * 4 + dx],
            recv_sem=heads_recv.at[zl * 4 + dx],
            device_id=device(to),
            device_id_type=MESH,
        )

    own_heads = pltpu.make_async_copy(
        sent.at[me["x"], zl], r_out.at[:, :, own_rows(seq)], local.at[6]
    )

    def ship(s):
        for dx in (2, 1, 3):
            heads_copy(s, dx).start()

        @pl.when(zl == s)
        def _():
            own_heads.start()

        @pl.when(zl != s)
        def _():
            heads_copy(s, 0).start()

    project(0)
    ring[1].step()
    ring[2].step()
    ship(0)
    project(1)
    ring[1].finish()
    ring[2].step()
    ship(1)
    turn(gs, gt)

    y_out[...] = jnp.zeros_like(y_out)
    dh_out[...] = jnp.zeros_like(dh_out)

    def feed(f, m):
        u_at = [(1 + f, m, k, slice(None), slice(None), slice(0, 128)) for k in range(2)]
        d_at = [(1 + f, slice(None), slice(None), m, k, slice(128, 256)) for k in range(2)]
        wu = jnp.concatenate([cells[i].reshape(D, 128) for i in u_at], axis=1)
        wd = jnp.concatenate([cells[i].reshape(D, 128) for i in d_at], axis=1)
        u = dot_nn(h2[...], wu) + bup(f, m)
        ga = dot_nn(gs[...], wd)
        cdf = 0.5 + 0.5 * lax.erf(u * (0.5**0.5))
        pdf = jnp.exp(-0.5 * u * u) * ((2.0 * math.pi) ** -0.5)
        act = (u * cdf).astype(BF16)
        du = (ga * (cdf + u * pdf)).astype(BF16)
        db_out[f, m] = jnp.sum(du.astype(F32), axis=0, keepdims=True)
        for k in range(4):
            rows = slice(k * 256, (k + 1) * 256)
            y_out[rows] += dot_nt(act[rows], wd)
            dh_out[rows] += dot_nt(du[rows], wu)
        dwu = dot_nn(h2t[...], du).astype(BF16)
        dwd = dot_nn(gt[...], act).astype(BF16)
        for k in range(2):
            lanes = slice(k * 128, (k + 1) * 128)
            cells[u_at[k]] = dwu[:, lanes].reshape(4, 2, 128, 128)
            cells[d_at[k]] = dwd[:, lanes].reshape(4, 2, 128, 128)

    for f in range(2):
        ring[1 + f].finish()
        ring_sems[1 + f].drain()

        @pl.loop(0, 4)
        def _(m):
            feed(f, m)

        kept_w.append(load(cells.at[1 + f], p_out.at[f], 7 + f))

    for s in range(2):
        for dx in (2, 1, 3):
            heads_copy(s, dx).wait_send()

        @pl.when(zl != s)
        def _():
            heads_copy(s, 0).wait_send()

    for src_zl in range(2):
        for dx in range(4):
            frm = lax.rem(me["x"] + 4 - dx, 4) * 2 + src_zl

            def wait(src_zl=src_zl, dx=dx, frm=frm):
                there = dict(me)
                there["x"] = lax.rem(me["x"] + 4 - dx, 4)
                there["z"] = zh * 2 + src_zl
                pltpu.make_async_remote_copy(
                    src_ref=r_out.at[:, :, own_rows(frm)],
                    dst_ref=r_out.at[:, :, own_rows(frm)],
                    send_sem=heads_send.at[0],
                    recv_sem=heads_recv.at[src_zl * 4 + dx],
                    device_id=device(there),
                    device_id_type=MESH,
                ).wait_recv()

            if dx:
                wait()
            else:
                pl.when(zl != src_zl)(wait)

    own_heads.wait()
    sems.arrived(kl, live_oth, partner)
    sems.arrived(kd, docs_oth, partner)
    ring_sems[0].drain()
    sems.drain()
    kept_h.wait()
    for cp in kept_w:
        cp.wait()


def forward(x, g, weights, vec, live, docs, table):
    any_spec = pl.BlockSpec(memory_space=pl.ANY)
    vmem = pl.BlockSpec(memory_space=pltpu.VMEM)
    n = 3 * 3 * 18 + 6
    return pl.pallas_call(
        forward_kernel,
        name="forward",
        out_shape=(
            jax.ShapeDtypeStruct((4, MB, LEN, 128), BF16),
            jax.ShapeDtypeStruct((1024, D), BF16),
            jax.ShapeDtypeStruct((1024, D), F32),
            jax.ShapeDtypeStruct((1024, D), F32),
            jax.ShapeDtypeStruct((2, 4, 1, 256), F32),
            jax.ShapeDtypeStruct((2,) + LEAD + SLOT, BF16),
            jax.ShapeDtypeStruct((1536, D), BF16),
            jax.ShapeDtypeStruct((512, D), BF16),
            jax.ShapeDtypeStruct((512, D), BF16),
            jax.ShapeDtypeStruct((512, D), BF16),
            jax.ShapeDtypeStruct((4, D), F32),
            jax.ShapeDtypeStruct(live.shape, jnp.int32),
            jax.ShapeDtypeStruct(docs.shape, jnp.int32),
        ),
        in_specs=[any_spec] * 2 + [vmem] * 5 + [any_spec] * 3,
        out_specs=[any_spec] * 2 + [vmem] * 3 + [any_spec] * 5 + [vmem] + [any_spec] * 2,
        scratch_shapes=[
            pltpu.VMEM((1, 1536), F32),
            pltpu.VMEM((2, 512, D), BF16),
            pltpu.VMEM((1024, D), BF16),
            pltpu.VMEM((D, 1024), BF16),
            pltpu.VMEM((1024, D), BF16),
            pltpu.VMEM((1024, D), BF16),
            pltpu.VMEM((D, 1024), BF16),
            pltpu.VMEM((3,) + LEAD + SLOT, BF16),
            pltpu.VMEM((1536, D), BF16),
            pltpu.VMEM((512, D), BF16),
            pltpu.VMEM((4, 2, 4, MB, ROWS, 128), BF16),
            pltpu.VMEM((2, ROWS, 128), F32),
            pltpu.VMEM((3, 2, HEAD, 64), BF16),
            pltpu.VMEM((96, 128), BF16),
            pltpu.VMEM((64, 256), BF16),
            pltpu.VMEM((96, 128), BF16),
            pltpu.VMEM((64, 256), BF16),
            pltpu.SemaphoreType.DMA((n,)),
            pltpu.SemaphoreType.DMA((n,)),
            pltpu.SemaphoreType.DMA((8,)),
            pltpu.SemaphoreType.DMA((8,)),
            pltpu.SemaphoreType.DMA((9,)),
        ],
        compiler_params=pltpu.CompilerParams(
            collective_id=0, has_side_effects=True, vmem_limit_bytes=62 * MIB
        ),
    )(x, g, *weights, vec, live, docs, table)


def attention_kernel(
    r_ref, docs_own, docs_oth, live_own, live_oth, table_ref, p_hbm,
    u_out, out_ref, t_ref, dk, dv, cells, *rest,
):
    bufs, (send, recv, local) = rest[:-3], rest[-3:]
    me = place()
    zl = lax.rem(me["z"], 2)
    mine = group_index(me)
    got = pltpu.make_async_copy(p_hbm, cells, local.at[0])
    got.start()
    others = peers(me)
    greet(ring_neighbours(me) + [device(p) for k, p in enumerate(others) if k + 1 not in (1, 2, 6)])
    got.wait()
    sems = Sems(send, recv)
    ring = start_scatter(
        [cells.at[0], cells.at[1]], (1, 2), bufs, sems, me, [out_ref.at[0], out_ref.at[1]]
    )
    ring.step()
    scale = HEAD**-0.5
    lane = lax.broadcasted_iota(jnp.int32, (ROWS, 128), 1)
    first = lane < HEAD

    def pair(v):
        zero = jnp.zeros_like(v)
        return jnp.concatenate([jnp.where(first, v, zero), jnp.where(first, zero, v)], axis=0)

    def merge(v):
        return jnp.where(first, v[:ROWS], v[ROWS:])

    def one(b, q0, k0, width):
        qs, ks = pl.ds(q0, ROWS), pl.ds(k0, width)
        q = pair(r_ref[0, b, qs])
        do = pair(r_ref[3, b, qs])
        k, v = r_ref[1, b, ks], r_ref[2, b, ks]
        row = q0 + lax.broadcasted_iota(jnp.int32, (ROWS, 1), 0)
        lo, end = row - (WINDOW - 1), 0
        for d in range(NDOC - 1):
            end = end + jnp.where(zl == 0, docs_own[b, d], docs_oth[b, d])
            lo = jnp.where(row >= end, jnp.maximum(lo, end), lo)
        col = k0 + lax.broadcasted_iota(jnp.int32, (1, width), 1)
        live = jnp.where(zl == 0, live_own[b, :, ks], live_oth[b, :, ks])
        jeff = jnp.where(live > 0, col, LEN)
        i = q0 + lax.broadcasted_iota(jnp.int32, (ROWS, width), 0)
        j = k0 + lax.broadcasted_iota(jnp.int32, (ROWS, width), 1)
        ok = ((jeff <= i) & (jeff >= lo)) | (i == j)
        ok = jnp.concatenate([ok, ok], axis=0)
        s = jnp.where(ok, dot_nt(q, k) * scale, BIG_NEG)
        top = jnp.max(s, axis=-1, keepdims=True)
        e = jnp.exp(s - top)
        prob = e * (1.0 / jnp.sum(e, axis=-1, keepdims=True))
        low = prob.astype(BF16)
        o = dot_nn(low, v)
        delta = jnp.sum(o * do.astype(F32), axis=-1, keepdims=True)
        ds = (prob * (dot_nt(do, v) - delta)).astype(BF16)
        t_ref[0, b, qs] = merge(o).astype(BF16)
        dq = merge(dot_nn(ds, k)) * scale
        table = [table_ref[n, qs] for n in range(2)]
        t_ref[1, b, qs] = rope(dq, table, -1.0).astype(BF16)
        dk[ks] += dot_tn(ds, q)
        dv[ks] += dot_tn(low, do)

    def ship(b):
        own = pltpu.make_async_copy(
            t_ref.at[:, b, own_rows(mine)], u_out.at[mine, :, b], local.at[1 + b]
        )
        own.start()
        sent = []
        for p in others:
            src = t_ref.at[:, b, own_rows(group_index(p))]
            sent.append(sems.push(src, u_out.at[mine, :, b], device(p)))
        return own, sent

    def landed(b, own, sent):
        own.wait()
        for k, at in enumerate(sent):
            frm = dict(me)
            frm["x"] = lax.rem(me["x"] + 4 - (k + 1) // 2, 4)
            frm["z"] = me["z"] - zl + lax.rem(zl + (k + 1) % 2, 2)
            sems.arrived(at, u_out.at[group_index(frm), :, b], device(frm))

    shipped = []
    for b in range(MB):
        dk[...] = jnp.zeros_like(dk)
        dv[...] = jnp.zeros_like(dv)
        for n in range(4):
            one(b, n * ROWS, 0, (n + 1) * ROWS)
            if b == 1 and n == 1:
                ring.step()
                shipped.append(ship(0))
        for begin, end in ((4, 5), (5, 8)) if b == 0 else ((4, 8),):

            @pl.loop(begin, end)
            def _(n):
                one(
                    b,
                    pl.multiple_of(n * ROWS, ROWS),
                    pl.multiple_of((n - 4) * ROWS, ROWS),
                    5 * ROWS,
                )

            ring.step()
        table = [table_ref[n] for n in range(2)]
        t_ref[2, b] = rope(dk[...] * scale, table, -1.0).astype(BF16)
        t_ref[3, b] = dv[...].astype(BF16)
    shipped.append(ship(1))
    ring.finish()
    for b in range(MB):
        landed(b, *shipped[b])
    sems.drain()


def attention(r, docs, docs_oth, live, live_oth, table, p):
    vmem = pl.BlockSpec(memory_space=pltpu.VMEM)
    smem = pl.BlockSpec(memory_space=pltpu.SMEM)
    any_spec = pl.BlockSpec(memory_space=pl.ANY)
    n = 2 * 3 * 18 + 14
    return pl.pallas_call(
        attention_kernel,
        name="attention",
        out_shape=(
            jax.ShapeDtypeStruct((8, 4, MB, ROWS, 128), BF16),
            jax.ShapeDtypeStruct((2,) + SLOT, F32),
        ),
        in_specs=[vmem, smem, smem, vmem, vmem, vmem, any_spec],
        out_specs=[any_spec, vmem],
        scratch_shapes=[
            pltpu.VMEM((4, MB, LEN, 128), BF16),
            pltpu.VMEM((LEN, 128), F32),
            pltpu.VMEM((LEN, 128), F32),
            pltpu.VMEM((2,) + LEAD + SLOT, BF16),
        ]
        + [pltpu.VMEM(s, BF16) for s in scatter_buffers((1, 2))]
        + [
            pltpu.SemaphoreType.DMA((n,)),
            pltpu.SemaphoreType.DMA((n,)),
            pltpu.SemaphoreType.DMA((3,)),
        ],
        compiler_params=pltpu.CompilerParams(
            collective_id=1, has_side_effects=True, vmem_limit_bytes=62 * MIB
        ),
    )(r, docs, docs_oth, live, live_oth, table, p)


def vector_sum(vecs, sems, me):
    for n, a in enumerate("xyz"):
        i = me[a]
        ks = []
        for by in (1, 2, 3):
            ks.append(sems.push(vecs.at[n, i], vecs.at[n, i], device(stepped(me, a, by))))
        yield 0
        for k, by in zip(ks, (1, 2, 3)):
            frm = stepped(me, a, -by)
            sems.arrived(k, vecs.at[n, frm[a]], device(frm))
        total = vecs[n, 0] + vecs[n, 1] + vecs[n, 2] + vecs[n, 3]
        if n < 2:
            vecs[n + 1, me["xyz"[n + 1]]] = total
        else:
            vecs[3, me["c"]] = total


def backward_kernel(
    x_own, g_own, x_oth, g_oth, h_in, u_in, wt_in, wo_in, y_in, dh_in, norms, db_in, ud_in,
    y_out, dx_out, e_out, w_out, v_out,
    xs, gs, hs, us, wt, wo, ys, dhs, dqkv, os, cells, e_send, slots, vecs, *rest,
):
    bufs, (send, recv, local) = rest[:-3], rest[-3:]
    me = place()
    core = me["c"]
    partner = other_core(me)

    def load(src, dst, k):
        cp = pltpu.make_async_copy(src, dst, local.at[k])
        cp.start()
        return cp

    first = [
        load(u_in, us, 0),
        load(h_in, hs, 1),
        load(g_own, gs.at[0:512], 2),
        load(g_oth, gs.at[512:1024], 3),
    ]
    second = [
        load(wt_in, wt, 4),
        load(wo_in, wo, 5),
        load(x_own, xs.at[0], 6),
        load(x_oth, xs.at[1], 7),
        load(dh_in, dhs, 8),
        load(y_in, ys, 9),
    ]
    greet(
        ring_neighbours(me)
        + [partner]
        + [device(stepped(me, a, 2)) for a in "xyz"]
    )
    sems = Sems(send, recv)
    for cp in first:
        cp.wait()
    for s in range(2):
        rows = slice(s * 512, (s + 1) * 512)
        for p in range(4):
            for a in range(4):
                piece = us[p, s, a].reshape(512, 128)
                if a == 0:
                    os[rows, p * 128 : (p + 1) * 128] = piece
                else:
                    at = (a - 1) * 512 + p * 128
                    dqkv[rows, at : at + 128] = piece
    for m in range(4):
        part = dot_tn(dqkv[:, m * 384 : (m + 1) * 384], hs[...]).astype(BF16)
        for k in range(2):
            for r in range(8):
                cells[m, k, r // 2, r % 2, 0:192] = part[
                    k * 192 : (k + 1) * 192, r * 128 : (r + 1) * 128
                ]
    part = dot_tn(os[...], gs[...]).astype(BF16)
    for k in range(8):
        for r in range(8):
            cells[k // 2, k % 2, r // 2, r % 2, 192:256] = part[
                r * 64 : (r + 1) * 64, k * 128 : (k + 1) * 128
            ]
    slots[core, 1:3] = ud_in[...]
    ring = start_scatter([cells], (0,), bufs, sems, me, [slots.at[core, 0]])
    ring.step()
    for cp in second:
        cp.wait()
    sums = jnp.zeros((5, D), F32)
    for s in (1, 0):
        rows = slice(s * 512, (s + 1) * 512)
        y = ys[rows] + dot_nn(os[rows], wo[...])
        dh1 = dot_nn(dqkv[rows], wt[...])
        dh2 = dhs[rows]
        xhat, _ = norm_parts(xs[s].astype(F32))
        dx = dh1 * norms[0:1] + dh2 * norms[2:3]
        sums += jnp.concatenate(
            [
                jnp.sum(dh1 * xhat, axis=0, keepdims=True),
                jnp.sum(dh1, axis=0, keepdims=True),
                jnp.sum(dh2 * xhat, axis=0, keepdims=True),
                jnp.sum(dh2, axis=0, keepdims=True),
                jnp.sum(gs[rows].astype(F32), axis=0, keepdims=True) * (1.0 - s),
            ],
            axis=0,
        )
        if s == 1:
            e_send[0] = y.astype(BF16)
            e_send[1] = dx.astype(BF16)
            ke = sems.push(e_send, e_out, partner)
        else:
            y_out[...] = y
            dx_out[...] = dx
        ring.step()
    bias = jnp.sum(dqkv[...].astype(F32), axis=0, keepdims=True)
    vecs[0, me["x"]] = jnp.zeros((16, D), F32)
    vecs[0, me["x"], 0:5] = sums
    vecs[0, me["x"], 5:6] = bias[:, :1024]
    vecs[0, me["x"], 6:7, 0:512] = bias[:, 1024:]
    for f in range(2):
        for m in range(4):
            vecs[0, me["x"], 8 + f * 4 + m : 9 + f * 4 + m, 0:256] = db_in[f, m]
    line = Steps([vector_sum(vecs, sems, me)])
    line.step()
    while ring.live or line.live:
        ring.step()
        line.step()
    kw = sems.push(slots.at[core], slots.at[core], partner)
    kv = sems.push(vecs.at[3, core], vecs.at[3, core], partner)
    sems.arrived(ke, e_out, partner)
    sems.arrived(kw, slots.at[1 - core], partner)
    sems.arrived(kv, vecs.at[3, 1 - core], partner)
    w_out[...] = slots[...]
    v_out[...] = vecs[3, 0:2]
    sems.drain()


def backward(x, g, x_oth, g_oth, h1, u, wt, wo, y, dh, norms, db, ud):
    any_spec = pl.BlockSpec(memory_space=pl.ANY)
    vmem = pl.BlockSpec(memory_space=pltpu.VMEM)
    n = 3 * 18 + 9 + 3
    return pl.pallas_call(
        backward_kernel,
        name="backward",
        out_shape=(
            jax.ShapeDtypeStruct((512, D), F32),
            jax.ShapeDtypeStruct((512, D), F32),
            jax.ShapeDtypeStruct((2, 512, D), BF16),
            jax.ShapeDtypeStruct((2, 3) + SLOT, F32),
            jax.ShapeDtypeStruct((2, 16, D), F32),
        ),
        in_specs=[any_spec] * 10 + [vmem] * 3,
        out_specs=[vmem] * 2 + [any_spec] + [vmem] * 2,
        scratch_shapes=[
            pltpu.VMEM((2, 512, D), BF16),
            pltpu.VMEM((1024, D), BF16),
            pltpu.VMEM((1024, D), BF16),
            pltpu.VMEM((4, 2, 4, MB, ROWS, 128), BF16),
            pltpu.VMEM((1536, D), BF16),
            pltpu.VMEM((512, D), BF16),
            pltpu.VMEM((1024, D), F32),
            pltpu.VMEM((1024, D), F32),
            pltpu.VMEM((1024, 1536), BF16),
            pltpu.VMEM((1024, 512), BF16),
            pltpu.VMEM(LEAD + SLOT, BF16),
            pltpu.VMEM((2, 512, D), BF16),
            pltpu.VMEM((2, 3) + SLOT, F32),
            pltpu.VMEM((4, 4, 16, D), F32),
        ]
        + [pltpu.VMEM(s, BF16) for s in scatter_buffers((0,))]
        + [
            pltpu.SemaphoreType.DMA((n,)),
            pltpu.SemaphoreType.DMA((n,)),
            pltpu.SemaphoreType.DMA((10,)),
        ],
        compiler_params=pltpu.CompilerParams(
            collective_id=2, has_side_effects=True, vmem_limit_bytes=62 * MIB
        ),
    )(x, g, x_oth, g_oth, h1, u, wt, wo, y, dh, norms, db, ud)


def adam(weight, first, second, grad, rate):
    first_new = BETA_ONE * first + (1.0 - BETA_ONE) * grad
    second_new = BETA_TWO * second + (1.0 - BETA_TWO) * grad * grad
    first_hat = first_new / (1.0 - BETA_ONE**STEP)
    second_hat = second_new / (1.0 - BETA_TWO**STEP)
    weight_new = weight - rate * (first_hat / (jnp.sqrt(second_hat) + ADAM_EPS) + DECAY * weight)
    return (first_new, second_new, weight_new)


RATES = (D**-0.5, max(1, D * 16 // LEN) ** -0.5, D**-0.5, FF**-0.5, VECTOR_RATE)


def final_kernel(x_ref, g_ref, y_ref, dx_ref, e_ref, slots, vecs, *rest):
    masters, outs, (grad, line) = rest[:15], rest[15:-2], rest[-2:]
    core = lax.axis_index("c")
    vector = masters[12]

    def bias(at):
        return jnp.concatenate([vector[at + j : at + j + 1] for j in range(8)], axis=1)

    x = x_ref[...].astype(F32)
    other = e_ref[...].astype(F32)
    outs[0][...] = x + y_ref[...] + other[0] + (bias(56) + bias(96))
    dxh = dx_ref[...] + other[1]
    xhat, rstd = norm_parts(x)
    outs[1][...] = g_ref[...].astype(F32) + rstd * (
        dxh
        - jnp.mean(dxh, axis=-1, keepdims=True)
        - xhat * jnp.mean(dxh * xhat, axis=-1, keepdims=True)
    )

    def update(k, total):
        new = adam(*[r[...] for r in masters[3 * k : 3 * k + 3]], total, RATES[k])
        for ref, value in zip(outs[2 + 3 * k : 5 + 3 * k], new):
            ref[...] = value

    step = pl.program_id(0)

    @pl.when(step == 0)
    def _():
        cols = []
        for t in range(3):
            rows = slice(t * 64, (t + 1) * 64)
            both = jnp.concatenate([slots[0, 0, rows], slots[1, 0, rows]], axis=0).T
            cols.append(jnp.where(core == 0, both[:64], both[64:]))
        update(0, jnp.concatenate(cols, axis=1))
        update(1, slots[core, 0, 192:256])

    @pl.when(step == 1)
    def _():
        rows = pl.ds(pl.multiple_of(core * 64, 64), 64)
        update(2, jnp.concatenate([slots[c, 1 + f, rows] for c in range(2) for f in range(2)], axis=1))

    @pl.when(step == 2)
    def _():
        for f in range(2):
            grad[f * 128 : (f + 1) * 128] = slots[core, 1 + f, 128:256].T
        update(3, grad[...])

    @pl.when(step == 3)
    def _():
        whole = vecs[0, 0:5] + vecs[1, 0:5]
        for i, at in ((0, 0), (1, 8), (2, 16), (3, 24), (4, 56), (4, 96)):
            for j in range(8):
                line[at + j : at + j + 1] = whole[i : i + 1, j * 128 : (j + 1) * 128]
        for i in range(12):
            lanes = slice(i % 8 * 128, (i % 8 + 1) * 128)
            zero, one = vecs[0, 5 + i // 8, lanes], vecs[1, 5 + i // 8, lanes]
            line[32 + 2 * i] = jnp.concatenate([zero[:64], one[:64]])
            line[33 + 2 * i] = jnp.concatenate([zero[64:], one[64:]])
        for n in range(8):
            for c in range(2):
                for f in range(2):
                    line[64 + n * 4 + c * 2 + f] = vecs[
                        c, 8 + f * 4 + n // 2, n % 2 * 128 : (n % 2 + 1) * 128
                    ]
        update(4, line[...])


def final(x, g, y, dx, e, slots, vecs, masters):
    def tok(*lead):
        return pl.BlockSpec(lead + (128, D), lambda s: (0,) * len(lead) + (s, 0))

    def whole(a):
        return pl.BlockSpec(a.shape, lambda s: (0,) * len(a.shape))

    return pl.pallas_call(
        final_kernel,
        name="final",
        grid=(4,),
        out_shape=[jax.ShapeDtypeStruct((512, D), F32)] * 2
        + [jax.ShapeDtypeStruct(m.shape, F32) for m in masters],
        in_specs=[tok(), tok(), tok(), tok(), tok(2)]
        + [whole(a) for a in (slots, vecs, *masters)],
        out_specs=[tok(), tok()] + [whole(m) for m in masters],
        scratch_shapes=[pltpu.VMEM((256, 128), F32), pltpu.VMEM((104, 128), F32)],
        compiler_params=pltpu.CompilerParams(vmem_limit_bytes=63 * MIB),
    )(x, g, y, dx, e, slots, vecs, *masters)


def rope_table():
    half = ROT // 2
    inverse = np.float32(10000.0) ** (-(np.arange(half, dtype=np.float32) * 2) / np.float32(ROT))
    angles = np.arange(LEN, dtype=np.float32)[:, None] * inverse.astype(np.float32)[None, :]
    table = np.zeros((2, LEN, 2, HEAD), np.float32)
    table[0] = 1.0
    table[0, :, :, :half] = np.cos(angles)[:, None]
    table[0, :, :, half:ROT] = np.cos(angles)[:, None]
    table[1, :, :, :half] = -np.sin(angles)[:, None]
    table[1, :, :, half:ROT] = np.sin(angles)[:, None]
    return jnp.asarray(table.reshape(2, LEN, 128))


def shards(
    inputs, cotangent, doc_lengths, present,
    w_qkv, m_qkv, v_qkv, w_out, m_out, v_out, w_up, m_up, v_up, w_down, m_down, v_down,
    vector, m_vector, v_vector,
):
    x_own, g_own = inputs.reshape(512, D), cotangent.reshape(512, D)
    docs = doc_lengths[:, 0]
    table = rope_table()
    vec, m_vec, v_vec = (a.reshape(104, 128) for a in (vector, m_vector, v_vector))

    r, h1, y, dh2, dbu, pud, wt, wo, x_oth, g_oth, norms, live_oth, docs_oth = forward(
        x_own, g_own, (w_qkv, w_out, w_up, w_down), vec, present, docs, table
    )
    u, oud = attention(r, docs, docs_oth, present, live_oth, table, pud)
    u = u.reshape(4, 2, 4, MB, ROWS, 128)
    y, dxh, other, slots, vecs = backward(
        x_own, g_own, x_oth, g_oth, h1, u, wt, wo, y, dh2, norms, dbu, oud
    )
    masters = (
        w_qkv, m_qkv, v_qkv, w_out, m_out, v_out, w_up, m_up, v_up, w_down, m_down, v_down,
        vec, m_vec, v_vec,
    )
    new = final(x_own, g_own, y, dxh, other, slots, vecs, masters)
    shape = (MB, 1, ROWS, D)
    return (
        new[0].reshape(shape),
        new[1].reshape(shape),
        *new[2:14],
        *(a.reshape(VEC) for a in new[14:]),
    )


def solution(mesh):
    finer = Mesh(mesh.devices.reshape(4, 2, 4, 2, 2), SEQ + FSDP)
    tokens = P(None, FSDP, SEQ, None)
    weight = P(FSDP, SEQ)
    in_specs = (tokens, tokens, P(None, FSDP, None), P(None, FSDP, None)) + (weight,) * 12 + (P(),) * 3
    out_specs = (tokens, tokens) + (weight,) * 12 + (P(),) * 3
    return jax.shard_map(
        shards, mesh=finer, in_specs=in_specs, out_specs=out_specs, check_vma=False
    )
```

```python
import math

import jax
import jax.numpy as jnp
import numpy as np
from jax import lax
from jax.experimental import pallas as pl
from jax.experimental.pallas import tpu as pltpu
from jax.sharding import Mesh
from jax.sharding import PartitionSpec as P

D = 1024
HEADS = 16
HEAD = 64
FF = 4096
ROT = 16
WINDOW = 1024
NDOC = 4
STEP = 10
VEC = 13312
MB = 2
ROWS = 256
LEN = 2048
BETA_ONE = 0.9
BETA_TWO = 0.95
ADAM_EPS = 1e-08
DECAY = 0.01
NORM_EPS = 1e-05
VECTOR_RATE = 0.5
BIG_NEG = -1e30
MESH = pl.DeviceIdType.MESH
MIB = 2**20
F32 = jnp.float32
BF16 = jnp.bfloat16

SEQ = ("x", "zl")
FSDP = ("y", "zh", "c")
LEAD = (4, 2, 4, 2)
EVEN = (
    (("x", "y", "z"), ((0, 48), (48, 32))),
    (("y", "z", "x"), ((80, 48), (128, 32))),
    (("z", "x", "y"), ((160, 48), (208, 48))),
)
ALONG_Y = (
    (("z", "x", "y"), ((0, 64), (64, 64))),
    (("x", "z", "y"), ((128, 64), (192, 64))),
)
GATHER = (EVEN, EVEN, ALONG_Y)
SCATTER = (EVEN, EVEN, EVEN)
SLOT = (256, 128)


def dot_nn(a, b):
    return lax.dot_general(a, b, (((1,), (0,)), ((), ())), preferred_element_type=F32)


def dot_nt(a, b):
    return lax.dot_general(a, b, (((1,), (1,)), ((), ())), preferred_element_type=F32)


def dot_tn(a, b):
    return lax.dot_general(a, b, (((0,), (0,)), ((), ())), preferred_element_type=F32)


def place():
    zl, zh = lax.axis_index("zl"), lax.axis_index("zh")
    return {
        "x": lax.axis_index("x"),
        "y": lax.axis_index("y"),
        "z": zh * 2 + zl,
        "c": lax.axis_index("c"),
    }


def device(at):
    return (at["x"], lax.rem(at["z"], 2), at["y"], at["z"] // 2, at["c"])


def stepped(me, axis, by):
    at = dict(me)
    at[axis] = lax.rem(me[axis] + by + 4, 4)
    return at


def slot(sel):
    z = sel["z"]
    if isinstance(z, slice):
        return (sel["x"], slice(None), sel["y"], slice(None))
    return (sel["x"], lax.rem(z, 2), sel["y"], z // 2)


def announce(targets):
    bar = pltpu.get_barrier_semaphore()
    for t in targets:
        pl.semaphore_signal(bar, inc=1, device_id=t, device_id_type=MESH)
    return lambda: pl.semaphore_wait(bar, len(targets))


def ring_neighbours(me):
    return [device(stepped(me, a, s)) for a in "xyz" for s in (1, 2, -1)]


def all_neighbours(me):
    return ring_neighbours(me) + [device(p) for k, p in enumerate(peers(me)) if k + 1 in (3, 5, 7)]


class Steps:
    def __init__(self, gens):
        self.live = list(gens)

    def step(self):
        still = []
        for g in self.live:
            if next(g, "end") != "end":
                still.append(g)
        self.live = still

    def finish(self):
        while self.live:
            self.step()


class Sems:
    def __init__(self, send, recv, at=0):
        self.send, self.recv, self.at, self.copies = send, recv, at, []

    def push(self, src, dst, to):
        k = self.at
        self.at += 1
        cp = pltpu.make_async_remote_copy(
            src_ref=src,
            dst_ref=dst,
            send_sem=self.send.at[k],
            recv_sem=self.recv.at[k],
            device_id=to,
            device_id_type=MESH,
        )
        cp.start()
        self.copies.append(cp)
        return k

    def arrived(self, k, dst, to):
        pltpu.make_async_remote_copy(
            src_ref=dst,
            dst_ref=dst,
            send_sem=self.send.at[k],
            recv_sem=self.recv.at[k],
            device_id=to,
            device_id_type=MESH,
        ).wait_recv()

    def drain(self):
        for cp in self.copies:
            cp.wait_send()
        self.copies = []


def other_core(me):
    at = dict(me)
    at["c"] = 1 - me["c"]
    return device(at)


def ring_gather(ref, order, halves, sems, me, known=()):
    h1, h2 = halves
    rows = (h1[0], h1[1] + h2[1])
    known = set(known)
    for a in order:
        i = me[a]
        up, down = device(stepped(me, a, 1)), device(stepped(me, a, -1))

        def block(v, half):
            sel = {b: (slice(None) if b in known else me[b]) for b in "xyz"}
            sel[a] = v
            return ref.at[slot(sel) + (pl.ds(*half), slice(None))]

        left, right, far = lax.rem(i + 3, 4), lax.rem(i + 1, 4), lax.rem(i + 2, 4)
        if not known:
            ks = [
                sems.push(block(i, rows), block(i, rows), device(stepped(me, a, by)))
                for by in (1, 3, 2)
            ]
            yield 0
            for k, frm in zip(ks, (left, right, far)):
                sems.arrived(k, block(frm, rows), up)
            known.add(a)
            continue
        r1 = sems.push(block(i, h1), block(i, h1), up)
        l2 = sems.push(block(i, h2), block(i, h2), down)
        r2 = sems.push(block(i, h2), block(i, h2), up)
        l1 = sems.push(block(i, h1), block(i, h1), down)
        yield 0
        sems.arrived(r1, block(left, h1), up)
        rf = sems.push(block(left, h1), block(left, h1), up)
        sems.arrived(l2, block(right, h2), down)
        lf = sems.push(block(right, h2), block(right, h2), down)
        yield 0
        sems.arrived(r2, block(left, h2), up)
        sems.arrived(l1, block(right, h1), down)
        sems.arrived(rf, block(far, h1), up)
        sems.arrived(lf, block(far, h2), down)
        known.add(a)


def free_dims(sel):
    dims = []
    for n, v in zip(LEAD, slot(sel)):
        if isinstance(v, slice):
            dims.append(n)
    return dims


def each_cell(sel, body):
    lead = slot(sel)
    dims = free_dims(sel)
    count = math.prod(dims)

    def at(n):
        free = []
        for d in reversed(dims):
            free.append(lax.rem(n, d))
            n = n // d
        free = free[::-1]
        full, k = [], 0
        for v in lead:
            if isinstance(v, slice):
                full.append(free[k])
                k += 1
            else:
                full.append(v)
        return tuple(full), tuple(free)

    if count == 1:
        body(*at(0))
    else:

        @pl.loop(0, count)
        def _(n):
            body(*at(n))


def ring_scatter(ref, order, halves, bufs, sems, me, out):
    h1, h2 = halves
    rows = (h1[0], h1[1] + h2[1])
    done = set()
    for n, a in enumerate(order):
        i = me[a]
        up, down = device(stepped(me, a, 1)), device(stepped(me, a, -1))

        def sel(v):
            s = {b: (me[b] if b in done else slice(None)) for b in "xyz"}
            s[a] = v
            return s

        def block(v, half):
            return ref.at[slot(sel(v)) + (pl.ds(*half), slice(None))]

        def add(v, half, terms, final):
            def body(full, free):
                rows = (pl.ds(*half), slice(None))
                total = ref[full + rows].astype(F32)
                for t in terms:
                    total += t[free].astype(F32)
                if final:
                    out[rows] = total
                else:
                    ref[full + rows] = total.astype(BF16)

            each_cell(sel(v), body)

        left, right, far = lax.rem(i + 3, 4), lax.rem(i + 1, 4), lax.rem(i + 2, 4)
        if n > 0:
            ks = [
                sems.push(block(lax.rem(i + by, 4), rows), buf, device(stepped(me, a, by)))
                for by, buf in zip((2, 1, 3), bufs[n])
            ]
            yield 0
            for k, buf in zip(ks, bufs[n]):
                sems.arrived(k, buf, up)
            add(i, rows, bufs[n], n == 2)
            done.add(a)
            continue
        ra, rb, rc, la, lb, lc = bufs[n]
        c0 = sems.push(block(far, h1), ra, up)
        c1 = sems.push(block(far, h2), la, down)
        c2 = sems.push(block(right, h2), rb, up)
        c3 = sems.push(block(left, h1), lb, down)
        yield 0
        sems.arrived(c0, ra, up)
        add(right, h1, [ra], False)
        c4 = sems.push(block(right, h1), rc, up)
        sems.arrived(c1, la, down)
        add(left, h2, [la], False)
        c5 = sems.push(block(left, h2), lc, down)
        yield 0
        sems.arrived(c3, lb, down)
        sems.arrived(c4, rc, up)
        add(i, h1, [lb, rc], False)
        sems.arrived(c2, rb, up)
        sems.arrived(c5, lc, down)
        add(i, h2, [rb, lc], False)
        done.add(a)


def scatter_shapes(order, halves, lanes):
    dims = {"x": (4,), "y": (4,), "z": (2, 2)}
    left = ["x", "y", "z"]
    shapes = []
    for a in order:
        left.remove(a)
        lead = []
        if "x" in left:
            lead.append(4)
        if "z" in left:
            lead.append(2)
        if "y" in left:
            lead.append(4)
        if "z" in left:
            lead.append(2)
        n1, n2 = halves[0][1], halves[1][1]
        counts = (n1, n2, n1, n2, n1, n2) if a == order[0] else (n1 + n2,) * 3
        shapes += [tuple(lead) + (r, lanes) for r in counts]
    return shapes


def scatter_buffers(phases):
    shapes = []
    for ph in phases:
        for o, h in SCATTER[ph]:
            shapes += scatter_shapes(o[::-1], h, 128)
    return shapes


def start_scatter(refs, phases, bufs, sems, me, outs):
    gens, at = [], 0
    for ref, ph, out in zip(refs, phases, outs):
        for o, h in SCATTER[ph]:
            mine = [bufs[at : at + 6], bufs[at + 6 : at + 9], bufs[at + 9 : at + 12]]
            gens.append(ring_scatter(ref, o[::-1], h, mine, sems, me, out))
            at += 12
    return Steps(gens)


def peers(me):
    out = []
    zl = lax.rem(me["z"], 2)
    for k in range(1, 8):
        at = dict(me)
        at["x"] = lax.rem(me["x"] + k // 2, 4)
        at["z"] = me["z"] - zl + lax.rem(zl + k % 2, 2)
        out.append(at)
    return out


def group_index(at):
    return at["x"] * 2 + lax.rem(at["z"], 2)


def own_rows(j):
    return pl.ds(pl.multiple_of(j * ROWS, ROWS), ROWS)


class HeadsExchange:
    def __init__(self, me, src, dst, send, recv, local):
        self.me, self.src, self.dst = me, src, dst
        self.send, self.recv = send, recv
        self.zl, self.zh = lax.rem(me["z"], 2), me["z"] // 2
        self.own = pltpu.make_async_copy(
            src.at[me["x"], self.zl], dst.at[:, own_rows(group_index(me))], local
        )

    def copy(self, s, dx):
        to = dict(self.me)
        to["x"] = lax.rem(self.me["x"] + dx, 4)
        to["z"] = self.zh * 2 + s
        return pltpu.make_async_remote_copy(
            src_ref=self.src.at[to["x"], s],
            dst_ref=self.dst.at[:, own_rows(group_index(self.me))],
            send_sem=self.send.at[s * 4 + dx],
            recv_sem=self.recv.at[self.zl * 4 + dx],
            device_id=device(to),
            device_id_type=MESH,
        )

    def start(self, s):
        for dx in (2, 1, 3):
            self.copy(s, dx).start()

        @pl.when(self.zl == s)
        def _():
            self.own.start()

        @pl.when(self.zl != s)
        def _():
            self.copy(s, 0).start()

    def wait_sent(self):
        for s in range(2):
            for dx in (2, 1, 3):
                self.copy(s, dx).wait_send()

            @pl.when(self.zl != s)
            def _(s=s):
                self.copy(s, 0).wait_send()

    def wait_came(self):
        for zl in range(2):
            for dx in range(4):
                there = dict(self.me)
                there["x"] = lax.rem(self.me["x"] + 4 - dx, 4)
                there["z"] = self.zh * 2 + zl
                came = self.dst.at[:, own_rows(group_index(there))]

                def wait(zl=zl, dx=dx, there=there, came=came):
                    pltpu.make_async_remote_copy(
                        src_ref=came,
                        dst_ref=came,
                        send_sem=self.send.at[0],
                        recv_sem=self.recv.at[zl * 4 + dx],
                        device_id=device(there),
                        device_id_type=MESH,
                    ).wait_recv()

                if dx:
                    wait()
                else:
                    pl.when(self.zl != zl)(wait)
        self.own.wait()


def norm_parts(x):
    mean = jnp.mean(x, axis=-1, keepdims=True)
    cen = x - mean
    var = jnp.mean(cen * cen, axis=-1, keepdims=True)
    rstd = lax.rsqrt(var + NORM_EPS)
    return cen * rstd, rstd


def rope(v, table, sign):
    lane = lax.rem(lax.broadcasted_iota(jnp.int32, v.shape, 1), HEAD)
    turned = jnp.where(lane < ROT // 2, pltpu.roll(v, 128 - ROT // 2, 1), pltpu.roll(v, ROT // 2, 1))
    return v * table[0] + (sign * turned) * table[1]


def feed(cells, m, bias, h2, h2t, gs, gt, y_ref, dh_ref, db_ref):
    u_at = [(m, k, slice(None), slice(None), slice(0, 128)) for k in range(2)]
    d_at = [(slice(None), slice(None), m, k, slice(128, 256)) for k in range(2)]
    wu = jnp.concatenate([cells[i].reshape(D, 128) for i in u_at], axis=1)
    wd = jnp.concatenate([cells[i].reshape(D, 128) for i in d_at], axis=1)
    u = dot_nn(h2[...], wu) + bias
    ga = dot_nn(gs[...], wd)
    cdf = 0.5 + 0.5 * lax.erf(u * (0.5**0.5))
    pdf = jnp.exp(-0.5 * u * u) * ((2.0 * math.pi) ** -0.5)
    act = (u * cdf).astype(BF16)
    du = (ga * (cdf + u * pdf)).astype(BF16)
    db_ref[m] = jnp.sum(du.astype(F32), axis=0, keepdims=True)
    for k in range(4):
        rows = slice(k * 256, (k + 1) * 256)
        y_ref[rows] += dot_nt(act[rows], wd)
        dh_ref[rows] += dot_nt(du[rows], wu)
    dwu = dot_nn(h2t[...], du).astype(BF16)
    dwd = dot_nn(gt[...], act).astype(BF16)
    for k in range(2):
        lanes = slice(k * 128, (k + 1) * 128)
        cells[u_at[k]] = dwu[:, lanes].reshape(4, 2, 128, 128)
        cells[d_at[k]] = dwd[:, lanes].reshape(4, 2, 128, 128)


def up_bias(vec, core, f, m):
    at = 64 + m * 8 + core * 2 + f
    return jnp.concatenate([vec[pl.ds(at, 1)], vec[pl.ds(at + 4, 1)]], axis=1)


def forward_kernel(
    x_own, g_own, wq_in, wo_in, wu_in, wd_in, vec, live, docs, table,
    r_out, s_out, h1_out, h2_out, h2t_out, gt_out, y_out, dh_out, p_out, part_out, wt_out, wo_out,
    x_oth, g_oth, live_oth, docs_oth, db_out, norms,
    bqkv, y, dh, xs, gs, gt, h1, h2, h2t, cells, wt, wo, sent, tab, wqs, awq, awu, cwq, cwu,
    send, recv, heads_send, heads_recv, local,
):
    me = place()
    core = me["c"]
    seq = group_index(me)
    partner = other_core(me)
    ready = announce(all_neighbours(me) + [partner])

    def load(src, dst, k):
        cp = pltpu.make_async_copy(src, dst, local.at[k])
        cp.start()
        return cp

    got_x = load(x_own, xs.at[0], 0)
    got_g = load(g_own, gs.at[0:512], 1)
    got_t = load(table.at[:, own_rows(seq)], tab, 2)

    wqs[...] = wq_in[...].T.astype(BF16).reshape(3, 2, HEAD, 64)
    gone = wqs[:, 1 - core].reshape(192, 64)
    awq[...] = jnp.concatenate([gone[:96], gone[96:]], axis=1)
    wu = wu_in[...].astype(BF16)
    awu[...] = jnp.where(core == 0, wu[:, 256:], wu[:, :256])
    ready()
    sems = Sems(send, recv)
    kq = sems.push(awq, cwq, partner)
    ku = sems.push(awu, cwu, partner)
    kx = sems.push(x_own, x_oth, partner)
    kg = sems.push(g_own, g_oth, partner)
    kl = sems.push(live, live_oth, partner)
    kd = sems.push(docs, docs_oth, partner)
    own = slot(me)
    kept = wqs[:, core].reshape(192, 64)
    kept_u = jnp.where(core == 0, wu[:, :256], wu[:, 256:])
    wd = wd_in[...].T.astype(BF16)
    sems.arrived(kq, cwq, partner)
    came = jnp.concatenate([cwq[:, :64], cwq[:, 64:]], axis=0)
    cells[(0,) + own + (slice(0, 192),)] = jnp.where(
        core == 0,
        jnp.concatenate([kept, came], axis=1),
        jnp.concatenate([came, kept], axis=1),
    )
    cells[(0,) + own + (slice(192, 256),)] = wo_in[...].astype(BF16)
    sems.arrived(ku, cwu, partner)
    came_u = cwu[...]
    both = jnp.where(
        core == 0,
        jnp.concatenate([kept_u, came_u], axis=0),
        jnp.concatenate([came_u, kept_u], axis=0),
    )
    for f in range(2):
        cells[(1 + f,) + own + (slice(0, 128),)] = both[:, f * 128 : (f + 1) * 128]
        cells[(1 + f,) + own + (slice(128, 256),)] = wd[:, f * 128 : (f + 1) * 128]
    ring_sems = [Sems(send, recv, 6 + 54 * ph) for ph in range(3)]
    ring = [
        Steps(
            [
                ring_gather(cells.at[ph], o[: 3 if ph < 2 else 2], h, ring_sems[ph], me)
                for o, h in GATHER[ph]
            ]
        )
        for ph in range(3)
    ]

    for i in range(4):
        for j in range(8):
            norms[i : i + 1, j * 128 : (j + 1) * 128] = vec[i * 8 + j : i * 8 + j + 1]
    for i in range(12):
        one, two = vec[32 + 2 * i : 33 + 2 * i], vec[33 + 2 * i : 34 + 2 * i]
        bqkv[:, i * 128 : (i + 1) * 128] = jnp.where(
            core == 0,
            jnp.concatenate([one[:, :64], two[:, :64]], axis=1),
            jnp.concatenate([one[:, 64:], two[:, 64:]], axis=1),
        )

    def normalise(s):
        @pl.loop(0, 4)
        def _(k):
            rows = pl.ds(pl.multiple_of(k * 128, 128), 128)
            at = pl.ds(pl.multiple_of(s * 512 + k * 128, 128), 128)
            xhat, _ = norm_parts(xs[s, rows].astype(F32))
            h1[at] = (xhat * norms[0:1] + norms[1:2]).astype(BF16)
            h2[at] = (xhat * norms[2:3] + norms[3:4]).astype(BF16)

    def turn(src, dst):
        @pl.loop(0, 4)
        def _(k):
            at = pl.ds(pl.multiple_of(k * 256, 256), 256)
            dst[:, at] = src[at].T

    for ph in range(3):
        ring[ph].step()
    got_x.wait()
    normalise(0)
    for ph in range(3):
        ring[ph].step()
    sems.arrived(kx, x_oth, partner)
    got_x = load(x_oth, xs.at[1], 0)
    for ph in range(3):
        ring[ph].step()
    ring[0].step()
    sems.arrived(kg, g_oth, partner)
    got_g.wait()
    got_g = load(g_oth, gs.at[512:1024], 1)
    got_x.wait()
    normalise(1)
    kept_h = [load(h1, h1_out, 3), load(h2, h2_out, 10)]
    ring[0].step()
    ring[1].step()
    ring[2].finish()
    ring_sems[2].drain()
    kept_h.append(load(cells.at[2, :, :, me["y"]], part_out, 8))
    turn(h2, h2t)
    kept_h.append(load(h2t, h2t_out, 11))
    ring[0].finish()

    for k in range(8):
        for r in range(8):
            cell = cells[0, k // 2, k % 2, r // 2, r % 2]
            wt[k * 192 : (k + 1) * 192, r * 128 : (r + 1) * 128] = cell[:192]
            wo[r * 64 : (r + 1) * 64, k * 128 : (k + 1) * 128] = cell[192:]
    kept_w = [load(wt, wt_out, 4), load(wo, wo_out, 5)]
    got_g.wait()
    got_t.wait()

    def project(s):
        rows = slice(s * 512, (s + 1) * 512)
        do = dot_nt(gs[rows], wo[...]).astype(BF16)
        turns = [jnp.concatenate([tab[i]] * MB, axis=0) for i in range(2)]
        for a in range(4):
            if a < 3:
                part = dot_nt(h1[rows], wt[a * 512 : (a + 1) * 512])
                part = (part + bqkv[:, a * 512 : (a + 1) * 512]).astype(BF16)
            else:
                part = do
            for p in range(4):
                piece = part[:, p * 128 : (p + 1) * 128]
                if a < 2:
                    piece = rope(piece.astype(F32), turns, 1.0).astype(BF16)
                for b in range(MB):
                    sent[b, p, s, a] = piece[b * ROWS : (b + 1) * ROWS]

    heads = HeadsExchange(me, sent.at[0], r_out, heads_send, heads_recv, local.at[6])
    project(0)
    ring[1].step()
    heads.start(0)
    project(1)
    heads.start(1)
    kept_w.append(load(sent.at[1], s_out, 9))
    turn(gs, gt)
    kept_h.append(load(gt, gt_out, 12))
    ring[1].finish()
    ring_sems[1].drain()
    y[...] = jnp.zeros_like(y)
    dh[...] = jnp.zeros_like(dh)

    @pl.loop(0, 4)
    def _(m):
        feed(cells.at[1], m, up_bias(vec, core, 0, m), h2, h2t, gs, gt, y, dh, db_out)

    kept_w.append(load(cells.at[1], p_out, 7))
    kept_w.append(load(y, y_out, 13))
    kept_w.append(load(dh, dh_out, 14))
    heads.wait_sent()
    heads.wait_came()
    sems.arrived(kl, live_oth, partner)
    sems.arrived(kd, docs_oth, partner)
    ring_sems[0].drain()
    sems.drain()
    for cp in kept_h + kept_w:
        cp.wait()


def forward(x, g, weights, vec, live, docs, table):
    any_spec = pl.BlockSpec(memory_space=pl.ANY)
    vmem = pl.BlockSpec(memory_space=pltpu.VMEM)
    n = 3 * 3 * 18 + 6
    return pl.pallas_call(
        forward_kernel,
        name="forward",
        out_shape=(
            jax.ShapeDtypeStruct((4, LEN, 128), BF16),
            jax.ShapeDtypeStruct((4, 2, 4, ROWS, 128), BF16),
            jax.ShapeDtypeStruct((1024, D), BF16),
            jax.ShapeDtypeStruct((1024, D), BF16),
            jax.ShapeDtypeStruct((D, 1024), BF16),
            jax.ShapeDtypeStruct((D, 1024), BF16),
            jax.ShapeDtypeStruct((1024, D), F32),
            jax.ShapeDtypeStruct((1024, D), F32),
            jax.ShapeDtypeStruct(LEAD + SLOT, BF16),
            jax.ShapeDtypeStruct((4, 2, 2) + SLOT, BF16),
            jax.ShapeDtypeStruct((1536, D), BF16),
            jax.ShapeDtypeStruct((512, D), BF16),
            jax.ShapeDtypeStruct((512, D), BF16),
            jax.ShapeDtypeStruct((512, D), BF16),
            jax.ShapeDtypeStruct(live.shape, jnp.int32),
            jax.ShapeDtypeStruct(docs.shape, jnp.int32),
            jax.ShapeDtypeStruct((4, 1, 256), F32),
            jax.ShapeDtypeStruct((4, D), F32),
        ),
        in_specs=[any_spec] * 2 + [vmem] * 5 + [any_spec] * 3,
        out_specs=[any_spec] * 16 + [vmem] * 2,
        scratch_shapes=[
            pltpu.VMEM((1, 1536), F32),
            pltpu.VMEM((1024, D), F32),
            pltpu.VMEM((1024, D), F32),
            pltpu.VMEM((2, 512, D), BF16),
            pltpu.VMEM((1024, D), BF16),
            pltpu.VMEM((D, 1024), BF16),
            pltpu.VMEM((1024, D), BF16),
            pltpu.VMEM((1024, D), BF16),
            pltpu.VMEM((D, 1024), BF16),
            pltpu.VMEM((3,) + LEAD + SLOT, BF16),
            pltpu.VMEM((1536, D), BF16),
            pltpu.VMEM((512, D), BF16),
            pltpu.VMEM((MB, 4, 2, 4, ROWS, 128), BF16),
            pltpu.VMEM((2, ROWS, 128), F32),
            pltpu.VMEM((3, 2, HEAD, 64), BF16),
            pltpu.VMEM((96, 128), BF16),
            pltpu.VMEM((64, 256), BF16),
            pltpu.VMEM((96, 128), BF16),
            pltpu.VMEM((64, 256), BF16),
            pltpu.SemaphoreType.DMA((n,)),
            pltpu.SemaphoreType.DMA((n,)),
            pltpu.SemaphoreType.DMA((8,)),
            pltpu.SemaphoreType.DMA((8,)),
            pltpu.SemaphoreType.DMA((15,)),
        ],
        compiler_params=pltpu.CompilerParams(
            collective_id=0, has_side_effects=True, vmem_limit_bytes=62 * MIB
        ),
    )(x, g, *weights, vec, live, docs, table)


def attention_kernel(
    r_ref, docs_own, docs_oth, live_own, live_oth, table_ref, vec,
    s_hbm, part_in, h2_in, h2t_in, g_own, g_oth, gt_in, y_in, dh_in,
    u_out, p_out, y_out, dh_out, db_out,
    r_next, t_ref, dk, dv, cells, y, dh, h2, h2t, gs, gt,
    send, recv, heads_send, heads_recv, local,
):
    me = place()
    ready = announce(all_neighbours(me))
    zl = lax.rem(me["z"], 2)
    mine = group_index(me)

    def load(src, dst, k):
        cp = pltpu.make_async_copy(src, dst, local.at[k])
        cp.start()
        return cp

    got = load(part_in, cells.at[:, :, me["y"]], 0)
    others = peers(me)
    ready()
    heads = HeadsExchange(me, s_hbm, r_next, heads_send, heads_recv, local.at[3])
    heads.start(0)
    heads.start(1)
    got.wait()
    sems, ring_sems = Sems(send, recv), Sems(send, recv, 14)
    ring = Steps(
        [ring_gather(cells, o[2:], h, ring_sems, me, o[:2]) for o, h in GATHER[2]]
    )
    ring.step()
    loads = [
        load(src, dst, 4 + k)
        for k, (src, dst) in enumerate(
            (
                (h2_in, h2),
                (h2t_in, h2t),
                (g_own, gs.at[0:512]),
                (g_oth, gs.at[512:1024]),
                (gt_in, gt),
                (y_in, y),
                (dh_in, dh),
            )
        )
    ]
    scale = HEAD**-0.5
    lane = lax.broadcasted_iota(jnp.int32, (ROWS, 128), 1)
    first = lane < HEAD

    def pair(v):
        zero = jnp.zeros_like(v)
        return jnp.concatenate([jnp.where(first, v, zero), jnp.where(first, zero, v)], axis=0)

    def merge(v):
        return jnp.where(first, v[:ROWS], v[ROWS:])

    def one(b, q0, k0, width):
        qs, ks = pl.ds(q0, ROWS), pl.ds(k0, width)
        r = r_next if b else r_ref
        q, do = pair(r[0, qs]), pair(r[3, qs])
        k, v = r[1, ks], r[2, ks]
        row = q0 + lax.broadcasted_iota(jnp.int32, (ROWS, 1), 0)
        lo, end = row - (WINDOW - 1), 0
        for d in range(NDOC - 1):
            end = end + jnp.where(zl == 0, docs_own[b, d], docs_oth[b, d])
            lo = jnp.where(row >= end, jnp.maximum(lo, end), lo)
        col = k0 + lax.broadcasted_iota(jnp.int32, (1, width), 1)
        live = jnp.where(zl == 0, live_own[b, :, ks], live_oth[b, :, ks])
        jeff = jnp.where(live > 0, col, LEN)
        i = q0 + lax.broadcasted_iota(jnp.int32, (ROWS, width), 0)
        j = k0 + lax.broadcasted_iota(jnp.int32, (ROWS, width), 1)
        ok = ((jeff <= i) & (jeff >= lo)) | (i == j)
        ok = jnp.concatenate([ok, ok], axis=0)
        s = jnp.where(ok, dot_nt(q, k) * scale, BIG_NEG)
        top = jnp.max(s, axis=-1, keepdims=True)
        e = jnp.exp(s - top)
        prob = e * (1.0 / jnp.sum(e, axis=-1, keepdims=True))
        low = prob.astype(BF16)
        o = dot_nn(low, v)
        delta = jnp.sum(o * do.astype(F32), axis=-1, keepdims=True)
        ds = (prob * (dot_nt(do, v) - delta)).astype(BF16)
        t_ref[0, b, qs] = merge(o).astype(BF16)
        dq = merge(dot_nn(ds, k)) * scale
        table = [table_ref[n, qs] for n in range(2)]
        t_ref[1, b, qs] = rope(dq, table, -1.0).astype(BF16)
        dk[ks] += dot_tn(ds, q)
        dv[ks] += dot_tn(low, do)

    def ship(b):
        own = pltpu.make_async_copy(
            t_ref.at[:, b, own_rows(mine)], u_out.at[mine, :, b], local.at[1 + b]
        )
        own.start()
        sent = []
        for p in others:
            src = t_ref.at[:, b, own_rows(group_index(p))]
            sent.append(sems.push(src, u_out.at[mine, :, b], device(p)))
        return own, sent

    def landed(b, own, sent):
        own.wait()
        for k, at in enumerate(sent):
            frm = dict(me)
            frm["x"] = lax.rem(me["x"] + 4 - (k + 1) // 2, 4)
            frm["z"] = me["z"] - zl + lax.rem(zl + (k + 1) % 2, 2)
            sems.arrived(at, u_out.at[group_index(frm), :, b], device(frm))

    shipped = []
    for b in range(MB):
        if b == 1:
            heads.wait_came()
        dk[...] = jnp.zeros_like(dk)
        dv[...] = jnp.zeros_like(dv)
        for n in range(4):
            one(b, n * ROWS, 0, (n + 1) * ROWS)
        if b == 0:
            ring.step()

        @pl.loop(4, 8)
        def _(n):
            one(
                b,
                pl.multiple_of(n * ROWS, ROWS),
                pl.multiple_of((n - 4) * ROWS, ROWS),
                5 * ROWS,
            )

        table = [table_ref[n] for n in range(2)]
        t_ref[2, b] = rope(dk[...] * scale, table, -1.0).astype(BF16)
        t_ref[3, b] = dv[...].astype(BF16)
        shipped.append(ship(b))
    heads.wait_sent()
    ring.finish()
    ring_sems.drain()
    for cp in loads:
        cp.wait()

    @pl.loop(0, 4)
    def _(m):
        feed(cells, m, up_bias(vec, me["c"], 1, m), h2, h2t, gs, gt, y, dh, db_out)

    kept = [load(cells, p_out, 4), load(y, y_out, 5), load(dh, dh_out, 6)]
    for b in range(MB):
        landed(b, *shipped[b])
    for cp in kept:
        cp.wait()
    sems.drain()


def attention(r, docs, docs_oth, live, live_oth, table, vec, *streamed):
    vmem = pl.BlockSpec(memory_space=pltpu.VMEM)
    smem = pl.BlockSpec(memory_space=pltpu.SMEM)
    any_spec = pl.BlockSpec(memory_space=pl.ANY)
    n = 14 + 12
    return pl.pallas_call(
        attention_kernel,
        name="attention",
        out_shape=(
            jax.ShapeDtypeStruct((8, 4, MB, ROWS, 128), BF16),
            jax.ShapeDtypeStruct(LEAD + SLOT, BF16),
            jax.ShapeDtypeStruct((1024, D), F32),
            jax.ShapeDtypeStruct((1024, D), F32),
            jax.ShapeDtypeStruct((4, 1, 256), F32),
        ),
        in_specs=[vmem, smem, smem, vmem, vmem, vmem, vmem] + [any_spec] * 9,
        out_specs=[any_spec] * 4 + [vmem],
        scratch_shapes=[
            pltpu.VMEM((4, LEN, 128), BF16),
            pltpu.VMEM((4, MB, LEN, 128), BF16),
            pltpu.VMEM((LEN, 128), F32),
            pltpu.VMEM((LEN, 128), F32),
            pltpu.VMEM(LEAD + SLOT, BF16),
            pltpu.VMEM((1024, D), F32),
            pltpu.VMEM((1024, D), F32),
            pltpu.VMEM((1024, D), BF16),
            pltpu.VMEM((D, 1024), BF16),
            pltpu.VMEM((1024, D), BF16),
            pltpu.VMEM((D, 1024), BF16),
            pltpu.SemaphoreType.DMA((n,)),
            pltpu.SemaphoreType.DMA((n,)),
            pltpu.SemaphoreType.DMA((8,)),
            pltpu.SemaphoreType.DMA((8,)),
            pltpu.SemaphoreType.DMA((11,)),
        ],
        compiler_params=pltpu.CompilerParams(
            collective_id=1, has_side_effects=True, vmem_limit_bytes=63 * MIB
        ),
    )(r, docs, docs_oth, live, live_oth, table, vec, *streamed)


def vector_sum(vecs, sems, me):
    for n, a in enumerate("xyz"):
        i = me[a]
        ks = []
        for by in (1, 2, 3):
            ks.append(sems.push(vecs.at[n, i], vecs.at[n, i], device(stepped(me, a, by))))
        yield 0
        for k, by in zip(ks, (1, 2, 3)):
            frm = stepped(me, a, -by)
            sems.arrived(k, vecs.at[n, frm[a]], device(frm))
        total = vecs[n, 0] + vecs[n, 1] + vecs[n, 2] + vecs[n, 3]
        if n < 2:
            vecs[n + 1, me["xyz"[n + 1]]] = total
        else:
            vecs[3, me["c"]] = total


def backward_kernel(
    x_own, g_own, x_oth, g_oth, h_in, u_in, wt_in, wo_in, y_in, dh_in, p0_in, p1_in, norms, db0, db1,
    y_out, dx_out, e_out, w_out, v_out,
    xs, gs, hs, us, wt, wo, ys, dhs, dqkv, os, cells, e_send, slots, vecs, *rest,
):
    bufs, (send, recv, local) = rest[:-3], rest[-3:]
    me = place()
    core = me["c"]
    partner = other_core(me)
    ready = announce(ring_neighbours(me) + [partner])

    def load(src, dst, k):
        cp = pltpu.make_async_copy(src, dst, local.at[k])
        cp.start()
        return cp

    zeroth = [load(p0_in, cells.at[1], 0), load(p1_in, cells.at[2], 1)]
    first = [
        load(u_in, us, 2),
        load(h_in, hs, 3),
        load(g_own, gs.at[0:512], 4),
        load(g_oth, gs.at[512:1024], 5),
    ]
    ready()
    sems = Sems(send, recv)
    for cp in zeroth:
        cp.wait()
    ring_ud = start_scatter(
        [cells.at[1], cells.at[2]], (1, 2), bufs[36:], sems, me, [slots.at[core, 1], slots.at[core, 2]]
    )
    ring_ud.step()
    for cp in first:
        cp.wait()
    second = [
        load(wt_in, wt, 6),
        load(wo_in, wo, 7),
        load(x_own, xs.at[0], 8),
        load(x_oth, xs.at[1], 9),
        load(dh_in.at[512:1024], dhs, 10),
        load(y_in.at[512:1024], ys, 11),
    ]
    for s in range(2):
        rows = slice(s * 512, (s + 1) * 512)
        for p in range(4):
            for a in range(4):
                piece = us[p, s, a].reshape(512, 128)
                if a == 0:
                    os[rows, p * 128 : (p + 1) * 128] = piece
                else:
                    at = (a - 1) * 512 + p * 128
                    dqkv[rows, at : at + 128] = piece
    for m in range(4):
        part = dot_tn(dqkv[:, m * 384 : (m + 1) * 384], hs[...]).astype(BF16)
        for k in range(2):
            for r in range(8):
                cells[0, m, k, r // 2, r % 2, 0:192] = part[
                    k * 192 : (k + 1) * 192, r * 128 : (r + 1) * 128
                ]
    part = dot_tn(os[...], gs[...]).astype(BF16)
    for k in range(8):
        for r in range(8):
            cells[0, k // 2, k % 2, r // 2, r % 2, 192:256] = part[
                r * 64 : (r + 1) * 64, k * 128 : (k + 1) * 128
            ]
    ring_ud.step()
    ring = start_scatter([cells.at[0]], (0,), bufs[:36], sems, me, [slots.at[core, 0]])
    ring.step()
    for cp in second:
        cp.wait()
    sums = jnp.zeros((5, D), F32)
    for s in (1, 0):
        rows = slice(s * 512, (s + 1) * 512)
        if s == 0:
            second = [load(dh_in.at[0:512], dhs, 10), load(y_in.at[0:512], ys, 11)]
        attn = dot_nn(os[rows], wo[...])
        dh1 = dot_nn(dqkv[rows], wt[...])
        if s == 0:
            for cp in second:
                cp.wait()
        y = ys[...] + attn
        dh2 = dhs[...]
        xhat, _ = norm_parts(xs[s].astype(F32))
        dx = dh1 * norms[0:1] + dh2 * norms[2:3]
        sums += jnp.concatenate(
            [
                jnp.sum(dh1 * xhat, axis=0, keepdims=True),
                jnp.sum(dh1, axis=0, keepdims=True),
                jnp.sum(dh2 * xhat, axis=0, keepdims=True),
                jnp.sum(dh2, axis=0, keepdims=True),
                jnp.sum(gs[rows].astype(F32), axis=0, keepdims=True) * (1.0 - s),
            ],
            axis=0,
        )
        if s == 1:
            e_send[0] = y.astype(BF16)
            e_send[1] = dx.astype(BF16)
            ke = sems.push(e_send, e_out, partner)
        else:
            y_out[...] = y
            dx_out[...] = dx
            ring_ud.step()
    bias = jnp.sum(dqkv[...].astype(F32), axis=0, keepdims=True)
    vecs[0, me["x"]] = jnp.zeros((16, D), F32)
    vecs[0, me["x"], 0:5] = sums
    vecs[0, me["x"], 5:6] = bias[:, :1024]
    vecs[0, me["x"], 6:7, 0:512] = bias[:, 1024:]
    for f, db in enumerate((db0, db1)):
        for m in range(4):
            vecs[0, me["x"], 8 + f * 4 + m : 9 + f * 4 + m, 0:256] = db[m]
    line = Steps([vector_sum(vecs, sems, me)])
    line.step()
    ring.step()
    while ring.live or line.live or ring_ud.live:
        ring_ud.step()
        line.step()
        ring.step()
    kw = sems.push(slots.at[core], slots.at[core], partner)
    kv = sems.push(vecs.at[3, core], vecs.at[3, core], partner)
    sems.arrived(ke, e_out, partner)
    sems.arrived(kw, slots.at[1 - core], partner)
    sems.arrived(kv, vecs.at[3, 1 - core], partner)
    w_out[...] = slots[...]
    v_out[...] = vecs[3, 0:2]
    sems.drain()


def backward(streamed, norms, db0, db1):
    any_spec = pl.BlockSpec(memory_space=pl.ANY)
    vmem = pl.BlockSpec(memory_space=pltpu.VMEM)
    n = 3 * 3 * 12 + 9 + 3
    return pl.pallas_call(
        backward_kernel,
        name="backward",
        out_shape=(
            jax.ShapeDtypeStruct((512, D), F32),
            jax.ShapeDtypeStruct((512, D), F32),
            jax.ShapeDtypeStruct((2, 512, D), BF16),
            jax.ShapeDtypeStruct((2, 3) + SLOT, F32),
            jax.ShapeDtypeStruct((2, 16, D), F32),
        ),
        in_specs=[any_spec] * 12 + [vmem] * 3,
        out_specs=[vmem] * 2 + [any_spec] + [vmem] * 2,
        scratch_shapes=[
            pltpu.VMEM((2, 512, D), BF16),
            pltpu.VMEM((1024, D), BF16),
            pltpu.VMEM((1024, D), BF16),
            pltpu.VMEM((4, 2, 4, MB, ROWS, 128), BF16),
            pltpu.VMEM((1536, D), BF16),
            pltpu.VMEM((512, D), BF16),
            pltpu.VMEM((512, D), F32),
            pltpu.VMEM((512, D), F32),
            pltpu.VMEM((1024, 1536), BF16),
            pltpu.VMEM((1024, 512), BF16),
            pltpu.VMEM((3,) + LEAD + SLOT, BF16),
            pltpu.VMEM((2, 512, D), BF16),
            pltpu.VMEM((2, 3) + SLOT, F32),
            pltpu.VMEM((4, 4, 16, D), F32),
        ]
        + [pltpu.VMEM(s, BF16) for s in scatter_buffers((0, 1, 2))]
        + [
            pltpu.SemaphoreType.DMA((n,)),
            pltpu.SemaphoreType.DMA((n,)),
            pltpu.SemaphoreType.DMA((12,)),
        ],
        compiler_params=pltpu.CompilerParams(
            collective_id=2, has_side_effects=True, vmem_limit_bytes=63 * MIB
        ),
    )(*streamed, norms, db0, db1)


def adam(weight, first, second, grad, rate):
    first_new = BETA_ONE * first + (1.0 - BETA_ONE) * grad
    second_new = BETA_TWO * second + (1.0 - BETA_TWO) * grad * grad
    first_hat = first_new / (1.0 - BETA_ONE**STEP)
    second_hat = second_new / (1.0 - BETA_TWO**STEP)
    weight_new = weight - rate * (first_hat / (jnp.sqrt(second_hat) + ADAM_EPS) + DECAY * weight)
    return (first_new, second_new, weight_new)


RATES = (D**-0.5, max(1, D * 16 // LEN) ** -0.5, D**-0.5, FF**-0.5, VECTOR_RATE)


def final_kernel(x_ref, g_ref, y_ref, dx_ref, e_ref, slots, vecs, *rest):
    masters, outs, (grad, line) = rest[:15], rest[15:-2], rest[-2:]
    core = lax.axis_index("c")
    vector = masters[12]

    def bias(at):
        return jnp.concatenate([vector[at + j : at + j + 1] for j in range(8)], axis=1)

    x = x_ref[...].astype(F32)
    other = e_ref[...].astype(F32)
    outs[0][...] = x + y_ref[...] + other[0] + (bias(56) + bias(96))
    dxh = dx_ref[...] + other[1]
    xhat, rstd = norm_parts(x)
    outs[1][...] = g_ref[...].astype(F32) + rstd * (
        dxh
        - jnp.mean(dxh, axis=-1, keepdims=True)
        - xhat * jnp.mean(dxh * xhat, axis=-1, keepdims=True)
    )

    def update(k, total):
        new = adam(*[r[...] for r in masters[3 * k : 3 * k + 3]], total, RATES[k])
        for ref, value in zip(outs[2 + 3 * k : 5 + 3 * k], new):
            ref[...] = value

    step = pl.program_id(0)

    @pl.when(step == 0)
    def _():
        cols = []
        for t in range(3):
            rows = slice(t * 64, (t + 1) * 64)
            both = jnp.concatenate([slots[0, 0, rows], slots[1, 0, rows]], axis=0).T
            cols.append(jnp.where(core == 0, both[:64], both[64:]))
        update(0, jnp.concatenate(cols, axis=1))
        update(1, slots[core, 0, 192:256])

    @pl.when(step == 1)
    def _():
        rows = pl.ds(pl.multiple_of(core * 64, 64), 64)
        update(2, jnp.concatenate([slots[c, 1 + f, rows] for c in range(2) for f in range(2)], axis=1))

    @pl.when(step == 2)
    def _():
        for f in range(2):
            grad[f * 128 : (f + 1) * 128] = slots[core, 1 + f, 128:256].T
        update(3, grad[...])

    @pl.when(step == 3)
    def _():
        whole = vecs[0, 0:5] + vecs[1, 0:5]
        for i, at in ((0, 0), (1, 8), (2, 16), (3, 24), (4, 56), (4, 96)):
            for j in range(8):
                line[at + j : at + j + 1] = whole[i : i + 1, j * 128 : (j + 1) * 128]
        for i in range(12):
            lanes = slice(i % 8 * 128, (i % 8 + 1) * 128)
            zero, one = vecs[0, 5 + i // 8, lanes], vecs[1, 5 + i // 8, lanes]
            line[32 + 2 * i] = jnp.concatenate([zero[:64], one[:64]])
            line[33 + 2 * i] = jnp.concatenate([zero[64:], one[64:]])
        for n in range(8):
            for c in range(2):
                for f in range(2):
                    line[64 + n * 4 + c * 2 + f] = vecs[
                        c, 8 + f * 4 + n // 2, n % 2 * 128 : (n % 2 + 1) * 128
                    ]
        update(4, line[...])


def final(x, g, y, dx, e, slots, vecs, masters):
    def tok(*lead):
        return pl.BlockSpec(lead + (128, D), lambda s: (0,) * len(lead) + (s, 0))

    def whole(a):
        return pl.BlockSpec(a.shape, lambda s: (0,) * len(a.shape))

    return pl.pallas_call(
        final_kernel,
        name="final",
        grid=(4,),
        out_shape=[jax.ShapeDtypeStruct((512, D), F32)] * 2
        + [jax.ShapeDtypeStruct(m.shape, F32) for m in masters],
        in_specs=[tok(), tok(), tok(), tok(), tok(2)]
        + [whole(a) for a in (slots, vecs, *masters)],
        out_specs=[tok(), tok()] + [whole(m) for m in masters],
        scratch_shapes=[pltpu.VMEM((256, 128), F32), pltpu.VMEM((104, 128), F32)],
        compiler_params=pltpu.CompilerParams(vmem_limit_bytes=63 * MIB),
    )(x, g, y, dx, e, slots, vecs, *masters)


def rope_table():
    half = ROT // 2
    inverse = np.float32(10000.0) ** (-(np.arange(half, dtype=np.float32) * 2) / np.float32(ROT))
    angles = np.arange(LEN, dtype=np.float32)[:, None] * inverse.astype(np.float32)[None, :]
    table = np.zeros((2, LEN, 2, HEAD), np.float32)
    table[0] = 1.0
    table[0, :, :, :half] = np.cos(angles)[:, None]
    table[0, :, :, half:ROT] = np.cos(angles)[:, None]
    table[1, :, :, :half] = -np.sin(angles)[:, None]
    table[1, :, :, half:ROT] = np.sin(angles)[:, None]
    return jnp.asarray(table.reshape(2, LEN, 128))


def shards(
    inputs, cotangent, doc_lengths, present,
    w_qkv, m_qkv, v_qkv, w_out, m_out, v_out, w_up, m_up, v_up, w_down, m_down, v_down,
    vector, m_vector, v_vector,
):
    x_own, g_own = inputs.reshape(512, D), cotangent.reshape(512, D)
    docs = doc_lengths[:, 0]
    table = rope_table()
    vec, m_vec, v_vec = (a.reshape(104, 128) for a in (vector, m_vector, v_vector))

    (
        r, sent, h1, h2, h2t, gt, y, dh2, p0, part, wt, wo, x_oth, g_oth, live_oth, docs_oth, db0, norms,
    ) = forward(x_own, g_own, (w_qkv, w_out, w_up, w_down), vec, present, docs, table)
    u, p1, y, dh2, db1 = attention(
        r, docs, docs_oth, present, live_oth, table, vec, sent, part, h2, h2t, g_own, g_oth, gt, y, dh2
    )
    u = u.reshape(4, 2, 4, MB, ROWS, 128)
    y, dxh, other, slots, vecs = backward(
        (x_own, g_own, x_oth, g_oth, h1, u, wt, wo, y, dh2, p0, p1), norms, db0, db1
    )
    masters = (
        w_qkv, m_qkv, v_qkv, w_out, m_out, v_out, w_up, m_up, v_up, w_down, m_down, v_down,
        vec, m_vec, v_vec,
    )
    new = final(x_own, g_own, y, dxh, other, slots, vecs, masters)
    shape = (MB, 1, ROWS, D)
    return (
        new[0].reshape(shape),
        new[1].reshape(shape),
        *new[2:14],
        *(a.reshape(VEC) for a in new[14:]),
    )


def solution(mesh):
    finer = Mesh(mesh.devices.reshape(4, 2, 4, 2, 2), SEQ + FSDP)
    tokens = P(None, FSDP, SEQ, None)
    weight = P(FSDP, SEQ)
    in_specs = (tokens, tokens, P(None, FSDP, None), P(None, FSDP, None)) + (weight,) * 12 + (P(),) * 3
    out_specs = (tokens, tokens) + (weight,) * 12 + (P(),) * 3
    return jax.shard_map(
        shards, mesh=finer, in_specs=in_specs, out_specs=out_specs, check_vma=False
    )
```

```python
import math

import jax
import jax.numpy as jnp
import numpy as np
from jax import lax
from jax.experimental import pallas as pl
from jax.experimental.pallas import tpu as pltpu
from jax.sharding import Mesh
from jax.sharding import PartitionSpec as P

D = 1024
HEADS = 16
HEAD = 64
FF = 4096
ROT = 16
WINDOW = 1024
NDOC = 4
STEP = 10
VEC = 13312
MB = 2
ROWS = 256
LEN = 2048
BETA_ONE = 0.9
BETA_TWO = 0.95
ADAM_EPS = 1e-08
DECAY = 0.01
NORM_EPS = 1e-05
VECTOR_RATE = 0.5
BIG_NEG = -1e30
MESH = pl.DeviceIdType.MESH
MIB = 2**20
F32 = jnp.float32
BF16 = jnp.bfloat16

SEQ = ("x", "zl")
FSDP = ("y", "zh", "c")
LEAD = (4, 2, 4, 2)
EVEN = (
    (("x", "y", "z"), ((0, 48), (48, 32))),
    (("y", "z", "x"), ((80, 48), (128, 32))),
    (("z", "x", "y"), ((160, 48), (208, 48))),
)
ALONG_Y = (
    (("z", "x", "y"), ((0, 64), (64, 64))),
    (("x", "z", "y"), ((128, 64), (192, 64))),
)
GATHER = (EVEN, EVEN, ALONG_Y)
SCATTER = tuple((o[::-1], h, ()) for o, h in EVEN)
SCATTER_Y = tuple((("y",), h, ()) for o, h in ALONG_Y)
SCATTER_XZ = tuple((o[1::-1], h, ("y",)) for o, h in ALONG_Y)
SLOT = (256, 128)


def dot_nn(a, b):
    return lax.dot_general(a, b, (((1,), (0,)), ((), ())), preferred_element_type=F32)


def dot_nt(a, b):
    return lax.dot_general(a, b, (((1,), (1,)), ((), ())), preferred_element_type=F32)


def dot_tn(a, b):
    return lax.dot_general(a, b, (((0,), (0,)), ((), ())), preferred_element_type=F32)


def place():
    zl, zh = lax.axis_index("zl"), lax.axis_index("zh")
    return {
        "x": lax.axis_index("x"),
        "y": lax.axis_index("y"),
        "z": zh * 2 + zl,
        "c": lax.axis_index("c"),
    }


def device(at):
    return (at["x"], lax.rem(at["z"], 2), at["y"], at["z"] // 2, at["c"])


def stepped(me, axis, by):
    at = dict(me)
    at[axis] = lax.rem(me[axis] + by + 4, 4)
    return at


def slot(sel):
    z = sel["z"]
    if isinstance(z, slice):
        return (sel["x"], slice(None), sel["y"], slice(None))
    return (sel["x"], lax.rem(z, 2), sel["y"], z // 2)


def announce(targets):
    bar = pltpu.get_barrier_semaphore()
    for t in targets:
        pl.semaphore_signal(bar, inc=1, device_id=t, device_id_type=MESH)
    return lambda: pl.semaphore_wait(bar, len(targets))


def ring_neighbours(me):
    return [device(stepped(me, a, s)) for a in "xyz" for s in (1, 2, -1)]


def all_neighbours(me):
    return ring_neighbours(me) + [device(p) for k, p in enumerate(peers(me)) if k + 1 in (3, 5, 7)]


class Steps:
    def __init__(self, gens):
        self.live = list(gens)

    def step(self):
        still = []
        for g in self.live:
            if next(g, "end") != "end":
                still.append(g)
        self.live = still

    def finish(self):
        while self.live:
            self.step()


class Sems:
    def __init__(self, send, recv, at=0):
        self.send, self.recv, self.at, self.copies = send, recv, at, []

    def push(self, src, dst, to):
        k = self.at
        self.at += 1
        cp = pltpu.make_async_remote_copy(
            src_ref=src,
            dst_ref=dst,
            send_sem=self.send.at[k],
            recv_sem=self.recv.at[k],
            device_id=to,
            device_id_type=MESH,
        )
        cp.start()
        self.copies.append(cp)
        return k

    def arrived(self, k, dst, to):
        pltpu.make_async_remote_copy(
            src_ref=dst,
            dst_ref=dst,
            send_sem=self.send.at[k],
            recv_sem=self.recv.at[k],
            device_id=to,
            device_id_type=MESH,
        ).wait_recv()

    def drain(self):
        for cp in self.copies:
            cp.wait_send()
        self.copies = []


def other_core(me):
    at = dict(me)
    at["c"] = 1 - me["c"]
    return device(at)


def ring_gather(ref, order, halves, sems, me, known=()):
    h1, h2 = halves
    rows = (h1[0], h1[1] + h2[1])
    known = set(known)
    for a in order:
        i = me[a]
        up, down = device(stepped(me, a, 1)), device(stepped(me, a, -1))

        def block(v, half):
            sel = {b: (slice(None) if b in known else me[b]) for b in "xyz"}
            sel[a] = v
            return ref.at[slot(sel) + (pl.ds(*half), slice(None))]

        left, right, far = lax.rem(i + 3, 4), lax.rem(i + 1, 4), lax.rem(i + 2, 4)
        if not known:
            ks = [
                sems.push(block(i, rows), block(i, rows), device(stepped(me, a, by)))
                for by in (1, 3, 2)
            ]
            yield 0
            for k, frm in zip(ks, (left, right, far)):
                sems.arrived(k, block(frm, rows), up)
            known.add(a)
            continue
        r1 = sems.push(block(i, h1), block(i, h1), up)
        l2 = sems.push(block(i, h2), block(i, h2), down)
        r2 = sems.push(block(i, h2), block(i, h2), up)
        l1 = sems.push(block(i, h1), block(i, h1), down)
        yield 0
        sems.arrived(r1, block(left, h1), up)
        rf = sems.push(block(left, h1), block(left, h1), up)
        sems.arrived(l2, block(right, h2), down)
        lf = sems.push(block(right, h2), block(right, h2), down)
        yield 0
        sems.arrived(r2, block(left, h2), up)
        sems.arrived(l1, block(right, h1), down)
        sems.arrived(rf, block(far, h1), up)
        sems.arrived(lf, block(far, h2), down)
        known.add(a)


def free_dims(sel):
    dims = []
    for n, v in zip(LEAD, slot(sel)):
        if isinstance(v, slice):
            dims.append(n)
    return dims


def each_cell(sel, body):
    lead = slot(sel)
    dims = free_dims(sel)
    count = math.prod(dims)

    def at(n):
        free = []
        for d in reversed(dims):
            free.append(lax.rem(n, d))
            n = n // d
        free = free[::-1]
        full, k = [], 0
        for v in lead:
            if isinstance(v, slice):
                full.append(free[k])
                k += 1
            else:
                full.append(v)
        return tuple(full), tuple(free)

    if count == 1:
        body(*at(0))
    else:

        @pl.loop(0, count)
        def _(n):
            body(*at(n))


def ring_scatter(ref, order, halves, bufs, sems, me, out, done=()):
    h1, h2 = halves
    rows = (h1[0], h1[1] + h2[1])
    done = set(done)
    for n, a in enumerate(order):
        i = me[a]
        up, down = device(stepped(me, a, 1)), device(stepped(me, a, -1))

        def sel(v):
            s = {b: (me[b] if b in done else slice(None)) for b in "xyz"}
            s[a] = v
            return s

        def block(v, half):
            return ref.at[slot(sel(v)) + (pl.ds(*half), slice(None))]

        def add(v, half, terms, final):
            def body(full, free):
                rows = (pl.ds(*half), slice(None))
                total = ref[full + rows].astype(F32)
                for t in terms:
                    total += t[free].astype(F32)
                if final:
                    out[rows] = total
                else:
                    ref[full + rows] = total.astype(BF16)

            each_cell(sel(v), body)

        left, right, far = lax.rem(i + 3, 4), lax.rem(i + 1, 4), lax.rem(i + 2, 4)
        if done:
            ks = [
                sems.push(block(lax.rem(i + by, 4), rows), buf, device(stepped(me, a, by)))
                for by, buf in zip((2, 1, 3), bufs[n])
            ]
            yield 0
            for k, buf in zip(ks, bufs[n]):
                sems.arrived(k, buf, up)
            add(i, rows, bufs[n], len(done) == 2)
            done.add(a)
            continue
        ra, rb, rc, la, lb, lc = bufs[n]
        c0 = sems.push(block(far, h1), ra, up)
        c1 = sems.push(block(far, h2), la, down)
        c2 = sems.push(block(right, h2), rb, up)
        c3 = sems.push(block(left, h1), lb, down)
        yield 0
        sems.arrived(c0, ra, up)
        add(right, h1, [ra], False)
        c4 = sems.push(block(right, h1), rc, up)
        sems.arrived(c1, la, down)
        add(left, h2, [la], False)
        c5 = sems.push(block(left, h2), lc, down)
        yield 0
        sems.arrived(c3, lb, down)
        sems.arrived(c4, rc, up)
        add(i, h1, [lb, rc], False)
        sems.arrived(c2, rb, up)
        sems.arrived(c5, lc, down)
        add(i, h2, [rb, lc], False)
        done.add(a)


def scatter_shapes(order, halves, done=()):
    left = [a for a in "xyz" if a not in done]
    shapes = []
    for n, a in enumerate(order):
        left.remove(a)
        lead = [(4 if "x" in left else 0), (2 if "z" in left else 0), (4 if "y" in left else 0), (2 if "z" in left else 0)]
        n1, n2 = halves[0][1], halves[1][1]
        counts = (n1 + n2,) * 3 if n or done else (n1, n2, n1, n2, n1, n2)
        shapes.append([tuple(d for d in lead if d) + (r, 128) for r in counts])
    return shapes


def scatter_buffers(plan):
    return [
        pltpu.VMEM(s, BF16) for part in plan for stage in scatter_shapes(*part) for s in stage
    ]


def start_scatter(ref, plan, bufs, sems, me, out):
    gens, at = [], 0
    for order, halves, done in plan:
        mine = []
        for stage in scatter_shapes(order, halves, done):
            mine.append(bufs[at : at + len(stage)])
            at += len(stage)
        gens.append(ring_scatter(ref, order, halves, mine, sems, me, out, done))
    return Steps(gens)


def peers(me):
    out = []
    zl = lax.rem(me["z"], 2)
    for k in range(1, 8):
        at = dict(me)
        at["x"] = lax.rem(me["x"] + k // 2, 4)
        at["z"] = me["z"] - zl + lax.rem(zl + k % 2, 2)
        out.append(at)
    return out


def group_index(at):
    return at["x"] * 2 + lax.rem(at["z"], 2)


def own_rows(j):
    return pl.ds(pl.multiple_of(j * ROWS, ROWS), ROWS)


EXCHANGE_ORDER = ((1, 2, 6, 4, 3, 7, 5), (5, 4, 3, 7, 1, 2, 6))


class Exchange:
    def __init__(self, me, src_of, dst_of, send, recv, local):
        self.me, self.dst_of, self.send, self.recv = me, dst_of, send, recv
        self.own = pltpu.make_async_copy(src_of(me), dst_of(me), local)
        self.copies = [self.copy(k + 1, src_of(p), dst_of(me), p) for k, p in enumerate(peers(me))]

    def copy(self, k, src, dst, to):
        return pltpu.make_async_remote_copy(
            src_ref=src,
            dst_ref=dst,
            send_sem=self.send.at[k],
            recv_sem=self.recv.at[k],
            device_id=device(to),
            device_id_type=MESH,
        )

    def start(self):
        self.own.start()
        for core, order in enumerate(EXCHANGE_ORDER):

            @pl.when(self.me["c"] == core)
            def _(order=order):
                for k in order:
                    self.copies[k - 1].start()

    def wait_sent(self):
        for cp in self.copies:
            cp.wait_send()

    def wait_came(self):
        self.own.wait()
        zl = lax.rem(self.me["z"], 2)
        for k in range(1, 8):
            frm = dict(self.me)
            frm["x"] = lax.rem(self.me["x"] + 4 - k // 2, 4)
            frm["z"] = self.me["z"] - zl + lax.rem(zl + k % 2, 2)
            came = self.dst_of(frm)
            self.copy(k, came, came, frm).wait_recv()


def heads_exchange(me, src, dst, send, recv, local):
    return Exchange(
        me,
        lambda at: src.at[at["x"], lax.rem(at["z"], 2)],
        lambda at: dst.at[:, own_rows(group_index(at))],
        send,
        recv,
        local,
    )


def norm_parts(x):
    mean = jnp.mean(x, axis=-1, keepdims=True)
    cen = x - mean
    var = jnp.mean(cen * cen, axis=-1, keepdims=True)
    rstd = lax.rsqrt(var + NORM_EPS)
    return cen * rstd, rstd


def rope(v, table, sign):
    lane = lax.rem(lax.broadcasted_iota(jnp.int32, v.shape, 1), HEAD)
    turned = jnp.where(lane < ROT // 2, pltpu.roll(v, 128 - ROT // 2, 1), pltpu.roll(v, ROT // 2, 1))
    return v * table[0] + (sign * turned) * table[1]


def feed(cells, m, bias, h2, h2t, gs, gt, y_ref, dh_ref, db_ref):
    u_at = [(m, k, slice(None), slice(None), slice(0, 128)) for k in range(2)]
    d_at = [(slice(None), slice(None), m, k, slice(128, 256)) for k in range(2)]
    wu = jnp.concatenate([cells[i].reshape(D, 128) for i in u_at], axis=1)
    wd = jnp.concatenate([cells[i].reshape(D, 128) for i in d_at], axis=1)
    u = dot_nn(h2[...], wu) + bias
    ga = dot_nn(gs[...], wd)
    cdf = 0.5 + 0.5 * lax.erf(u * (0.5**0.5))
    pdf = jnp.exp(-0.5 * u * u) * ((2.0 * math.pi) ** -0.5)
    act = (u * cdf).astype(BF16)
    du = (ga * (cdf + u * pdf)).astype(BF16)
    db_ref[m] = jnp.sum(du.astype(F32), axis=0, keepdims=True)
    for k in range(4):
        rows = slice(k * 256, (k + 1) * 256)
        y_ref[rows] += dot_nt(act[rows], wd)
        dh_ref[rows] += dot_nt(du[rows], wu)
    dwu = dot_nn(h2t[...], du).astype(BF16)
    dwd = dot_nn(gt[...], act).astype(BF16)
    for k in range(2):
        lanes = slice(k * 128, (k + 1) * 128)
        cells[u_at[k]] = dwu[:, lanes].reshape(4, 2, 128, 128)
        cells[d_at[k]] = dwd[:, lanes].reshape(4, 2, 128, 128)


def up_bias(vec, core, f, m):
    at = 64 + m * 8 + core * 2 + f
    return jnp.concatenate([vec[pl.ds(at, 1)], vec[pl.ds(at + 4, 1)]], axis=1)


def forward_kernel(
    x_own, g_own, wq_in, wo_in, wu_in, wd_in, vec, live, docs, table,
    r_out, s_out, h1_out, h2_out, h2t_out, gt_out, y_out, dh_out, p_out, part_out, wt_out, wo_out,
    x_oth, g_oth, live_oth, docs_oth, db_out, norms,
    bqkv, y, dh, xs, gs, gt, h1, h2, h2t, cells, wt, wo, sent, tab, wqs, awq, awu, cwq, cwu,
    send, recv, heads_send, heads_recv, local,
):
    me = place()
    core = me["c"]
    seq = group_index(me)
    partner = other_core(me)
    ready = announce(all_neighbours(me) + [partner])

    def load(src, dst, k):
        cp = pltpu.make_async_copy(src, dst, local.at[k])
        cp.start()
        return cp

    got_x = load(x_own, xs.at[0], 0)
    got_g = load(g_own, gs.at[0:512], 1)
    got_t = load(table.at[:, own_rows(seq)], tab, 2)

    wqs[...] = wq_in[...].T.astype(BF16).reshape(3, 2, HEAD, 64)
    gone = wqs[:, 1 - core].reshape(192, 64)
    awq[...] = jnp.concatenate([gone[:96], gone[96:]], axis=1)
    wu = wu_in[...].astype(BF16)
    awu[...] = jnp.where(core == 0, wu[:, 256:], wu[:, :256])
    ready()
    sems = Sems(send, recv)
    kq = sems.push(awq, cwq, partner)
    ku = sems.push(awu, cwu, partner)
    kx = sems.push(x_own, x_oth, partner)
    kg = sems.push(g_own, g_oth, partner)
    kl = sems.push(live, live_oth, partner)
    kd = sems.push(docs, docs_oth, partner)
    own = slot(me)
    kept = wqs[:, core].reshape(192, 64)
    kept_u = jnp.where(core == 0, wu[:, :256], wu[:, 256:])
    wd = wd_in[...].T.astype(BF16)
    sems.arrived(kq, cwq, partner)
    came = jnp.concatenate([cwq[:, :64], cwq[:, 64:]], axis=0)
    cells[(0,) + own + (slice(0, 192),)] = jnp.where(
        core == 0,
        jnp.concatenate([kept, came], axis=1),
        jnp.concatenate([came, kept], axis=1),
    )
    cells[(0,) + own + (slice(192, 256),)] = wo_in[...].astype(BF16)
    sems.arrived(ku, cwu, partner)
    came_u = cwu[...]
    both = jnp.where(
        core == 0,
        jnp.concatenate([kept_u, came_u], axis=0),
        jnp.concatenate([came_u, kept_u], axis=0),
    )
    for f in range(2):
        cells[(1 + f,) + own + (slice(0, 128),)] = both[:, f * 128 : (f + 1) * 128]
        cells[(1 + f,) + own + (slice(128, 256),)] = wd[:, f * 128 : (f + 1) * 128]
    ring_sems = [Sems(send, recv, 6 + 54 * ph) for ph in range(3)]
    ring = [
        Steps(
            [
                ring_gather(cells.at[ph], o[: 3 if ph < 2 else 2], h, ring_sems[ph], me)
                for o, h in GATHER[ph]
            ]
        )
        for ph in range(3)
    ]

    for i in range(4):
        for j in range(8):
            norms[i : i + 1, j * 128 : (j + 1) * 128] = vec[i * 8 + j : i * 8 + j + 1]
    for i in range(12):
        one, two = vec[32 + 2 * i : 33 + 2 * i], vec[33 + 2 * i : 34 + 2 * i]
        bqkv[:, i * 128 : (i + 1) * 128] = jnp.where(
            core == 0,
            jnp.concatenate([one[:, :64], two[:, :64]], axis=1),
            jnp.concatenate([one[:, 64:], two[:, 64:]], axis=1),
        )

    def normalise(s):
        @pl.loop(0, 4)
        def _(k):
            rows = pl.ds(pl.multiple_of(k * 128, 128), 128)
            at = pl.ds(pl.multiple_of(s * 512 + k * 128, 128), 128)
            xhat, _ = norm_parts(xs[s, rows].astype(F32))
            h1[at] = (xhat * norms[0:1] + norms[1:2]).astype(BF16)
            h2[at] = (xhat * norms[2:3] + norms[3:4]).astype(BF16)

    def turn(src, dst):
        @pl.loop(0, 4)
        def _(k):
            at = pl.ds(pl.multiple_of(k * 256, 256), 256)
            dst[:, at] = src[at].T

    for ph in range(3):
        ring[ph].step()
    got_x.wait()
    normalise(0)
    for ph in range(3):
        ring[ph].step()
    sems.arrived(kx, x_oth, partner)
    got_x = load(x_oth, xs.at[1], 0)
    for ph in range(3):
        ring[ph].step()
    ring[0].step()
    sems.arrived(kg, g_oth, partner)
    got_g.wait()
    got_g = load(g_oth, gs.at[512:1024], 1)
    got_x.wait()
    normalise(1)
    kept_h = [load(h1, h1_out, 3), load(h2, h2_out, 10)]
    ring[0].step()
    ring[1].step()
    ring[2].finish()
    ring_sems[2].drain()
    kept_h.append(load(cells.at[2, :, :, me["y"]], part_out, 8))
    turn(h2, h2t)
    kept_h.append(load(h2t, h2t_out, 11))
    ring[0].finish()

    for k in range(8):
        for r in range(8):
            cell = cells[0, k // 2, k % 2, r // 2, r % 2]
            wt[k * 192 : (k + 1) * 192, r * 128 : (r + 1) * 128] = cell[:192]
            wo[r * 64 : (r + 1) * 64, k * 128 : (k + 1) * 128] = cell[192:]
    kept_w = [load(wt, wt_out, 4), load(wo, wo_out, 5)]
    got_g.wait()
    got_t.wait()

    def project(s):
        rows = slice(s * 512, (s + 1) * 512)
        do = dot_nt(gs[rows], wo[...]).astype(BF16)
        turns = [jnp.concatenate([tab[i]] * MB, axis=0) for i in range(2)]
        for a in range(4):
            if a < 3:
                part = dot_nt(h1[rows], wt[a * 512 : (a + 1) * 512])
                part = (part + bqkv[:, a * 512 : (a + 1) * 512]).astype(BF16)
            else:
                part = do
            for p in range(4):
                piece = part[:, p * 128 : (p + 1) * 128]
                if a < 2:
                    piece = rope(piece.astype(F32), turns, 1.0).astype(BF16)
                for b in range(MB):
                    sent[b, p, s, a] = piece[b * ROWS : (b + 1) * ROWS]

    heads = heads_exchange(me, sent.at[0], r_out, heads_send, heads_recv, local.at[6])
    project(0)
    ring[1].step()
    project(1)
    heads.start()
    kept_w.append(load(sent.at[1], s_out, 9))
    turn(gs, gt)
    kept_h.append(load(gt, gt_out, 12))
    ring[1].finish()
    ring_sems[1].drain()
    y[...] = jnp.zeros_like(y)
    dh[...] = jnp.zeros_like(dh)

    @pl.loop(0, 4)
    def _(m):
        feed(cells.at[1], m, up_bias(vec, core, 0, m), h2, h2t, gs, gt, y, dh, db_out)

    kept_w.append(load(cells.at[1], p_out, 7))
    kept_w.append(load(y, y_out, 13))
    kept_w.append(load(dh, dh_out, 14))
    heads.wait_sent()
    heads.wait_came()
    sems.arrived(kl, live_oth, partner)
    sems.arrived(kd, docs_oth, partner)
    ring_sems[0].drain()
    sems.drain()
    for cp in kept_h + kept_w:
        cp.wait()


def forward(x, g, weights, vec, live, docs, table):
    any_spec = pl.BlockSpec(memory_space=pl.ANY)
    vmem = pl.BlockSpec(memory_space=pltpu.VMEM)
    n = 3 * 3 * 18 + 6
    return pl.pallas_call(
        forward_kernel,
        name="forward",
        out_shape=(
            jax.ShapeDtypeStruct((4, LEN, 128), BF16),
            jax.ShapeDtypeStruct((4, 2, 4, ROWS, 128), BF16),
            jax.ShapeDtypeStruct((1024, D), BF16),
            jax.ShapeDtypeStruct((1024, D), BF16),
            jax.ShapeDtypeStruct((D, 1024), BF16),
            jax.ShapeDtypeStruct((D, 1024), BF16),
            jax.ShapeDtypeStruct((1024, D), F32),
            jax.ShapeDtypeStruct((1024, D), F32),
            jax.ShapeDtypeStruct(LEAD + SLOT, BF16),
            jax.ShapeDtypeStruct((4, 2, 2) + SLOT, BF16),
            jax.ShapeDtypeStruct((1536, D), BF16),
            jax.ShapeDtypeStruct((512, D), BF16),
            jax.ShapeDtypeStruct((512, D), BF16),
            jax.ShapeDtypeStruct((512, D), BF16),
            jax.ShapeDtypeStruct(live.shape, jnp.int32),
            jax.ShapeDtypeStruct(docs.shape, jnp.int32),
            jax.ShapeDtypeStruct((4, 1, 256), F32),
            jax.ShapeDtypeStruct((4, D), F32),
        ),
        in_specs=[any_spec] * 2 + [vmem] * 5 + [any_spec] * 3,
        out_specs=[any_spec] * 16 + [vmem] * 2,
        scratch_shapes=[
            pltpu.VMEM((1, 1536), F32),
            pltpu.VMEM((1024, D), F32),
            pltpu.VMEM((1024, D), F32),
            pltpu.VMEM((2, 512, D), BF16),
            pltpu.VMEM((1024, D), BF16),
            pltpu.VMEM((D, 1024), BF16),
            pltpu.VMEM((1024, D), BF16),
            pltpu.VMEM((1024, D), BF16),
            pltpu.VMEM((D, 1024), BF16),
            pltpu.VMEM((3,) + LEAD + SLOT, BF16),
            pltpu.VMEM((1536, D), BF16),
            pltpu.VMEM((512, D), BF16),
            pltpu.VMEM((MB, 4, 2, 4, ROWS, 128), BF16),
            pltpu.VMEM((2, ROWS, 128), F32),
            pltpu.VMEM((3, 2, HEAD, 64), BF16),
            pltpu.VMEM((96, 128), BF16),
            pltpu.VMEM((64, 256), BF16),
            pltpu.VMEM((96, 128), BF16),
            pltpu.VMEM((64, 256), BF16),
            pltpu.SemaphoreType.DMA((n,)),
            pltpu.SemaphoreType.DMA((n,)),
            pltpu.SemaphoreType.DMA((8,)),
            pltpu.SemaphoreType.DMA((8,)),
            pltpu.SemaphoreType.DMA((15,)),
        ],
        compiler_params=pltpu.CompilerParams(
            collective_id=0, has_side_effects=True, vmem_limit_bytes=62 * MIB
        ),
    )(x, g, *weights, vec, live, docs, table)


def attention_kernel(
    r_ref, docs_own, docs_oth, live_own, live_oth, table_ref, vec,
    s_hbm, part_in, h2_in, h2t_in, g_own, g_oth, gt_in, y_in, dh_in, p0_in,
    u_out, p_out, y_out, dh_out, p0_out, db_out,
    r_next, t_ref, dk, dv, cells, cells0, y, dh, h2, h2t, gs, gt, *rest,
):
    bufs, (send, recv, heads_send, heads_recv, local) = rest[:-5], rest[-5:]
    me = place()
    ready = announce(all_neighbours(me))
    zl = lax.rem(me["z"], 2)

    def load(src, dst, k):
        cp = pltpu.make_async_copy(src, dst, local.at[k])
        cp.start()
        return cp

    got = load(part_in, cells.at[:, :, me["y"]], 0)
    got0 = load(p0_in, cells0, 11)
    ready()
    heads = heads_exchange(me, s_hbm, r_next, heads_send.at[0], heads_recv.at[0], local.at[3])
    heads.start()
    got.wait()
    ring_sems = Sems(send, recv)
    ring = Steps(
        [ring_gather(cells, o[2:], h, ring_sems, me, o[:2]) for o, h in GATHER[2]]
    )
    ring.step()
    scatter_sems = Sems(send, recv, 12)
    scatter = start_scatter(cells0, SCATTER_Y, bufs, scatter_sems, me, None)
    loads = [
        load(src, dst, 4 + k)
        for k, (src, dst) in enumerate(
            (
                (h2_in, h2),
                (h2t_in, h2t),
                (g_own, gs.at[0:512]),
                (g_oth, gs.at[512:1024]),
                (gt_in, gt),
                (y_in, y),
                (dh_in, dh),
            )
        )
    ]
    scale = HEAD**-0.5
    lane = lax.broadcasted_iota(jnp.int32, (ROWS, 128), 1)
    first = lane < HEAD

    def pair(v):
        zero = jnp.zeros_like(v)
        return jnp.concatenate([jnp.where(first, v, zero), jnp.where(first, zero, v)], axis=0)

    def merge(v):
        return jnp.where(first, v[:ROWS], v[ROWS:])

    def one(b, q0, k0, width):
        qs, ks = pl.ds(q0, ROWS), pl.ds(k0, width)
        r = r_next if b else r_ref
        q, do = pair(r[0, qs] * jnp.asarray(scale, BF16)), pair(r[3, qs])
        k, v = r[1, ks], r[2, ks]
        row = q0 + lax.broadcasted_iota(jnp.int32, (1, ROWS), 1)
        lo, end = row - (WINDOW - 1), 0
        for d in range(NDOC - 1):
            end = end + jnp.where(zl == 0, docs_own[b, d], docs_oth[b, d])
            lo = jnp.where(row >= end, jnp.maximum(lo, end), lo)
        live = jnp.where(zl == 0, live_own[b, :, ks], live_oth[b, :, ks])
        col = k0 + lax.broadcasted_iota(jnp.int32, (width, 1), 0)
        jeff = jnp.where(live.reshape(width, 1) > 0, col, LEN)
        i = q0 + lax.broadcasted_iota(jnp.int32, (width, ROWS), 1)
        j = k0 + lax.broadcasted_iota(jnp.int32, (width, ROWS), 0)
        ok = ((jeff <= i) & (jeff >= lo)) | (i == j)
        s = jnp.where(jnp.concatenate([ok, ok], axis=1), dot_nt(k, q), BIG_NEG)
        e = jnp.exp(s - jnp.max(s, axis=0, keepdims=True))
        prob = e * (1.0 / jnp.sum(e, axis=0, keepdims=True))
        low = prob.astype(BF16)
        dp = dot_nt(v, do)
        ds = (prob * (dp - jnp.sum(dp * prob, axis=0, keepdims=True))).astype(BF16)
        t_ref[0, b, qs] = merge(dot_tn(v, low).T).astype(BF16)
        dq = merge(dot_tn(k, ds).T) * scale
        table = [table_ref[n, qs] for n in range(2)]
        t_ref[1, b, qs] = rope(dq, table, -1.0).astype(BF16)
        dk[ks] += dot_nn(ds, q)
        dv[ks] += dot_nn(low, do)

    def ship(b):
        out = Exchange(
            me,
            lambda at: t_ref.at[:, b, own_rows(group_index(at))],
            lambda at: u_out.at[group_index(at), :, b],
            heads_send.at[1 + b],
            heads_recv.at[1 + b],
            local.at[1 + b],
        )
        out.start()
        return out

    shipped = []
    for b in range(MB):
        if b == 1:
            heads.wait_came()
        dk[...] = jnp.zeros_like(dk)
        dv[...] = jnp.zeros_like(dv)
        for n in range(4):
            one(b, n * ROWS, 0, (n + 1) * ROWS)
        if b == 0:
            ring.step()
            got0.wait()
            scatter.step()

        @pl.loop(4, 8)
        def _(n):
            one(
                b,
                pl.multiple_of(n * ROWS, ROWS),
                pl.multiple_of((n - 4) * ROWS, ROWS),
                5 * ROWS,
            )

        table = [table_ref[n] for n in range(2)]
        t_ref[2, b] = rope(dk[...], table, -1.0).astype(BF16)
        t_ref[3, b] = dv[...].astype(BF16)
        shipped.append(ship(b))
    heads.wait_sent()
    scatter.step()
    ring.finish()
    ring_sems.drain()
    for cp in loads:
        cp.wait()

    @pl.loop(0, 4)
    def _(m):
        feed(cells, m, up_bias(vec, me["c"], 1, m), h2, h2t, gs, gt, y, dh, db_out)

    kept = [load(cells, p_out, 4), load(y, y_out, 5), load(dh, dh_out, 6)]
    scatter.finish()
    scatter_sems.drain()
    kept.append(load(cells0.at[:, :, me["y"]], p0_out, 7))
    for out in shipped:
        out.wait_came()
        out.wait_sent()
    for cp in kept:
        cp.wait()


def attention(r, docs, docs_oth, live, live_oth, table, vec, *streamed):
    vmem = pl.BlockSpec(memory_space=pltpu.VMEM)
    smem = pl.BlockSpec(memory_space=pltpu.SMEM)
    any_spec = pl.BlockSpec(memory_space=pl.ANY)
    n = 12 + 12
    return pl.pallas_call(
        attention_kernel,
        name="attention",
        out_shape=(
            jax.ShapeDtypeStruct((8, 4, MB, ROWS, 128), BF16),
            jax.ShapeDtypeStruct(LEAD + SLOT, BF16),
            jax.ShapeDtypeStruct((1024, D), F32),
            jax.ShapeDtypeStruct((1024, D), F32),
            jax.ShapeDtypeStruct((4, 2, 2) + SLOT, BF16),
            jax.ShapeDtypeStruct((4, 1, 256), F32),
        ),
        in_specs=[vmem, smem, smem, vmem, vmem, vmem, vmem] + [any_spec] * 10,
        out_specs=[any_spec] * 5 + [vmem],
        scratch_shapes=[
            pltpu.VMEM((4, LEN, 128), BF16),
            pltpu.VMEM((4, MB, LEN, 128), BF16),
            pltpu.VMEM((LEN, 128), F32),
            pltpu.VMEM((LEN, 128), F32),
            pltpu.VMEM(LEAD + SLOT, BF16),
            pltpu.VMEM(LEAD + SLOT, BF16),
            pltpu.VMEM((1024, D), F32),
            pltpu.VMEM((1024, D), F32),
            pltpu.VMEM((1024, D), BF16),
            pltpu.VMEM((D, 1024), BF16),
            pltpu.VMEM((1024, D), BF16),
            pltpu.VMEM((D, 1024), BF16),
        ]
        + scatter_buffers(SCATTER_Y)
        + [
            pltpu.SemaphoreType.DMA((n,)),
            pltpu.SemaphoreType.DMA((n,)),
            pltpu.SemaphoreType.DMA((3, 8)),
            pltpu.SemaphoreType.DMA((3, 8)),
            pltpu.SemaphoreType.DMA((12,)),
        ],
        compiler_params=pltpu.CompilerParams(
            collective_id=1, has_side_effects=True, vmem_limit_bytes=63 * MIB
        ),
    )(r, docs, docs_oth, live, live_oth, table, vec, *streamed)


def vector_sum(vecs, sems, me):
    for n, a in enumerate("xyz"):
        i = me[a]
        ks = []
        for by in (1, 2, 3):
            ks.append(sems.push(vecs.at[n, i], vecs.at[n, i], device(stepped(me, a, by))))
        yield 0
        for k, by in zip(ks, (1, 2, 3)):
            frm = stepped(me, a, -by)
            sems.arrived(k, vecs.at[n, frm[a]], device(frm))
        total = vecs[n, 0] + vecs[n, 1] + vecs[n, 2] + vecs[n, 3]
        if n < 2:
            vecs[n + 1, me["xyz"[n + 1]]] = total
        else:
            vecs[3, me["c"]] = total


def backward_kernel(
    x_own, g_own, x_oth, g_oth, h_in, u_in, wt_in, wo_in, y_in, dh_in, p0_in, p1_in, norms, db0, db1,
    y_out, dx_out, e_out, w_out, v_out,
    xs, gs, hs, us, wt, wo, ys, dhs, dqkv, os, cells, e_send, slots, vecs, *rest,
):
    bufs, (send, recv, local) = rest[:-3], rest[-3:]
    me = place()
    core = me["c"]
    partner = other_core(me)
    ready = announce(ring_neighbours(me) + [partner])

    def load(src, dst, k):
        cp = pltpu.make_async_copy(src, dst, local.at[k])
        cp.start()
        return cp

    zeroth = [load(p1_in, cells.at[2], 1), load(p0_in, cells.at[1, :, :, me["y"]], 0)]
    first = [
        load(u_in, us, 2),
        load(h_in, hs, 3),
        load(g_own, gs.at[0:512], 4),
        load(g_oth, gs.at[512:1024], 5),
    ]
    ready()
    sems = Sems(send, recv)
    for cp in zeroth:
        cp.wait()
    cut = len(scatter_buffers(SCATTER))
    ring_ud = start_scatter(cells.at[2], SCATTER, bufs[cut : 2 * cut], sems, me, slots.at[core, 2])
    ring_ud.live += start_scatter(
        cells.at[1], SCATTER_XZ, bufs[2 * cut :], sems, me, slots.at[core, 1]
    ).live
    ring_ud.step()
    for cp in first:
        cp.wait()
    second = [
        load(wt_in, wt, 6),
        load(wo_in, wo, 7),
        load(x_own, xs.at[0], 8),
        load(x_oth, xs.at[1], 9),
        load(dh_in.at[512:1024], dhs, 10),
        load(y_in.at[512:1024], ys, 11),
    ]
    for s in range(2):
        rows = slice(s * 512, (s + 1) * 512)
        for p in range(4):
            for a in range(4):
                piece = us[p, s, a].reshape(512, 128)
                if a == 0:
                    os[rows, p * 128 : (p + 1) * 128] = piece
                else:
                    at = (a - 1) * 512 + p * 128
                    dqkv[rows, at : at + 128] = piece
    for m in range(4):
        part = dot_tn(dqkv[:, m * 384 : (m + 1) * 384], hs[...]).astype(BF16)
        for k in range(2):
            for r in range(8):
                cells[0, m, k, r // 2, r % 2, 0:192] = part[
                    k * 192 : (k + 1) * 192, r * 128 : (r + 1) * 128
                ]
    part = dot_tn(os[...], gs[...]).astype(BF16)
    for k in range(8):
        for r in range(8):
            cells[0, k // 2, k % 2, r // 2, r % 2, 192:256] = part[
                r * 64 : (r + 1) * 64, k * 128 : (k + 1) * 128
            ]
    ring_ud.step()
    ring = start_scatter(cells.at[0], SCATTER, bufs[:cut], sems, me, slots.at[core, 0])
    ring.step()
    for cp in second:
        cp.wait()
    sums = jnp.zeros((5, D), F32)
    for s in (1, 0):
        rows = slice(s * 512, (s + 1) * 512)
        if s == 0:
            second = [load(dh_in.at[0:512], dhs, 10), load(y_in.at[0:512], ys, 11)]
        attn = dot_nn(os[rows], wo[...])
        dh1 = dot_nn(dqkv[rows], wt[...])
        if s == 0:
            for cp in second:
                cp.wait()
        y = ys[...] + attn
        dh2 = dhs[...]
        xhat, _ = norm_parts(xs[s].astype(F32))
        dx = dh1 * norms[0:1] + dh2 * norms[2:3]
        sums += jnp.concatenate(
            [
                jnp.sum(dh1 * xhat, axis=0, keepdims=True),
                jnp.sum(dh1, axis=0, keepdims=True),
                jnp.sum(dh2 * xhat, axis=0, keepdims=True),
                jnp.sum(dh2, axis=0, keepdims=True),
                jnp.sum(gs[rows].astype(F32), axis=0, keepdims=True) * (1.0 - s),
            ],
            axis=0,
        )
        if s == 1:
            e_send[0] = y.astype(BF16)
            e_send[1] = dx.astype(BF16)
            ke = sems.push(e_send, e_out, partner)
            ring_ud.step()
            ring.step()
        else:
            y_out[...] = y
            dx_out[...] = dx
    bias = jnp.sum(dqkv[...].astype(F32), axis=0, keepdims=True)
    vecs[0, me["x"]] = jnp.zeros((16, D), F32)
    vecs[0, me["x"], 0:5] = sums
    vecs[0, me["x"], 5:6] = bias[:, :1024]
    vecs[0, me["x"], 6:7, 0:512] = bias[:, 1024:]
    for f, db in enumerate((db0, db1)):
        for m in range(4):
            vecs[0, me["x"], 8 + f * 4 + m : 9 + f * 4 + m, 0:256] = db[m]
    line = Steps([vector_sum(vecs, sems, me)])
    line.step()
    while ring.live or line.live or ring_ud.live:
        ring_ud.step()
        line.step()
        ring.step()
    kw = sems.push(slots.at[core], slots.at[core], partner)
    kv = sems.push(vecs.at[3, core], vecs.at[3, core], partner)
    sems.arrived(ke, e_out, partner)
    sems.arrived(kw, slots.at[1 - core], partner)
    sems.arrived(kv, vecs.at[3, 1 - core], partner)
    w_out[...] = slots[...]
    v_out[...] = vecs[3, 0:2]
    sems.drain()


def backward(streamed, norms, db0, db1):
    any_spec = pl.BlockSpec(memory_space=pl.ANY)
    vmem = pl.BlockSpec(memory_space=pltpu.VMEM)
    n = 2 * 3 * 12 + 2 * 6 + 9 + 3
    return pl.pallas_call(
        backward_kernel,
        name="backward",
        out_shape=(
            jax.ShapeDtypeStruct((512, D), F32),
            jax.ShapeDtypeStruct((512, D), F32),
            jax.ShapeDtypeStruct((2, 512, D), BF16),
            jax.ShapeDtypeStruct((2, 3) + SLOT, F32),
            jax.ShapeDtypeStruct((2, 16, D), F32),
        ),
        in_specs=[any_spec] * 12 + [vmem] * 3,
        out_specs=[vmem] * 2 + [any_spec] + [vmem] * 2,
        scratch_shapes=[
            pltpu.VMEM((2, 512, D), BF16),
            pltpu.VMEM((1024, D), BF16),
            pltpu.VMEM((1024, D), BF16),
            pltpu.VMEM((4, 2, 4, MB, ROWS, 128), BF16),
            pltpu.VMEM((1536, D), BF16),
            pltpu.VMEM((512, D), BF16),
            pltpu.VMEM((512, D), F32),
            pltpu.VMEM((512, D), F32),
            pltpu.VMEM((1024, 1536), BF16),
            pltpu.VMEM((1024, 512), BF16),
            pltpu.VMEM((3,) + LEAD + SLOT, BF16),
            pltpu.VMEM((2, 512, D), BF16),
            pltpu.VMEM((2, 3) + SLOT, F32),
            pltpu.VMEM((4, 4, 16, D), F32),
        ]
        + scatter_buffers(SCATTER + SCATTER + SCATTER_XZ)
        + [
            pltpu.SemaphoreType.DMA((n,)),
            pltpu.SemaphoreType.DMA((n,)),
            pltpu.SemaphoreType.DMA((12,)),
        ],
        compiler_params=pltpu.CompilerParams(
            collective_id=2, has_side_effects=True, vmem_limit_bytes=63 * MIB
        ),
    )(*streamed, norms, db0, db1)


def adam(weight, first, second, grad, rate):
    first_new = BETA_ONE * first + (1.0 - BETA_ONE) * grad
    second_new = BETA_TWO * second + (1.0 - BETA_TWO) * grad * grad
    first_hat = first_new / (1.0 - BETA_ONE**STEP)
    second_hat = second_new / (1.0 - BETA_TWO**STEP)
    weight_new = weight - rate * (first_hat / (jnp.sqrt(second_hat) + ADAM_EPS) + DECAY * weight)
    return (first_new, second_new, weight_new)


RATES = (D**-0.5, max(1, D * 16 // LEN) ** -0.5, D**-0.5, FF**-0.5, VECTOR_RATE)


def final_kernel(x_ref, g_ref, y_ref, dx_ref, e_ref, slots, vecs, *rest):
    masters, outs, (grad, line) = rest[:15], rest[15:-2], rest[-2:]
    core = lax.axis_index("c")
    vector = masters[12]

    def bias(at):
        return jnp.concatenate([vector[at + j : at + j + 1] for j in range(8)], axis=1)

    x = x_ref[...].astype(F32)
    other = e_ref[...].astype(F32)
    outs[0][...] = x + y_ref[...] + other[0] + (bias(56) + bias(96))
    dxh = dx_ref[...] + other[1]
    xhat, rstd = norm_parts(x)
    outs[1][...] = g_ref[...].astype(F32) + rstd * (
        dxh
        - jnp.mean(dxh, axis=-1, keepdims=True)
        - xhat * jnp.mean(dxh * xhat, axis=-1, keepdims=True)
    )

    def update(k, total):
        new = adam(*[r[...] for r in masters[3 * k : 3 * k + 3]], total, RATES[k])
        for ref, value in zip(outs[2 + 3 * k : 5 + 3 * k], new):
            ref[...] = value

    step = pl.program_id(0)

    @pl.when(step == 0)
    def _():
        cols = []
        for t in range(3):
            rows = slice(t * 64, (t + 1) * 64)
            both = jnp.concatenate([slots[0, 0, rows], slots[1, 0, rows]], axis=0).T
            cols.append(jnp.where(core == 0, both[:64], both[64:]))
        update(0, jnp.concatenate(cols, axis=1))
        update(1, slots[core, 0, 192:256])

    @pl.when(step == 1)
    def _():
        rows = pl.ds(pl.multiple_of(core * 64, 64), 64)
        update(2, jnp.concatenate([slots[c, 1 + f, rows] for c in range(2) for f in range(2)], axis=1))

    @pl.when(step == 2)
    def _():
        for f in range(2):
            grad[f * 128 : (f + 1) * 128] = slots[core, 1 + f, 128:256].T
        update(3, grad[...])

    @pl.when(step == 3)
    def _():
        whole = vecs[0, 0:5] + vecs[1, 0:5]
        for i, at in ((0, 0), (1, 8), (2, 16), (3, 24), (4, 56), (4, 96)):
            for j in range(8):
                line[at + j : at + j + 1] = whole[i : i + 1, j * 128 : (j + 1) * 128]
        for i in range(12):
            lanes = slice(i % 8 * 128, (i % 8 + 1) * 128)
            zero, one = vecs[0, 5 + i // 8, lanes], vecs[1, 5 + i // 8, lanes]
            line[32 + 2 * i] = jnp.concatenate([zero[:64], one[:64]])
            line[33 + 2 * i] = jnp.concatenate([zero[64:], one[64:]])
        for n in range(8):
            for c in range(2):
                for f in range(2):
                    line[64 + n * 4 + c * 2 + f] = vecs[
                        c, 8 + f * 4 + n // 2, n % 2 * 128 : (n % 2 + 1) * 128
                    ]
        update(4, line[...])


def final(x, g, y, dx, e, slots, vecs, masters):
    def tok(*lead):
        return pl.BlockSpec(lead + (128, D), lambda s: (0,) * len(lead) + (s, 0))

    def whole(a):
        return pl.BlockSpec(a.shape, lambda s: (0,) * len(a.shape))

    return pl.pallas_call(
        final_kernel,
        name="final",
        grid=(4,),
        out_shape=[jax.ShapeDtypeStruct((512, D), F32)] * 2
        + [jax.ShapeDtypeStruct(m.shape, F32) for m in masters],
        in_specs=[tok(), tok(), tok(), tok(), tok(2)]
        + [whole(a) for a in (slots, vecs, *masters)],
        out_specs=[tok(), tok()] + [whole(m) for m in masters],
        scratch_shapes=[pltpu.VMEM((256, 128), F32), pltpu.VMEM((104, 128), F32)],
        compiler_params=pltpu.CompilerParams(vmem_limit_bytes=63 * MIB),
    )(x, g, y, dx, e, slots, vecs, *masters)


def rope_table():
    half = ROT // 2
    inverse = np.float32(10000.0) ** (-(np.arange(half, dtype=np.float32) * 2) / np.float32(ROT))
    angles = np.arange(LEN, dtype=np.float32)[:, None] * inverse.astype(np.float32)[None, :]
    table = np.zeros((2, LEN, 2, HEAD), np.float32)
    table[0] = 1.0
    table[0, :, :, :half] = np.cos(angles)[:, None]
    table[0, :, :, half:ROT] = np.cos(angles)[:, None]
    table[1, :, :, :half] = -np.sin(angles)[:, None]
    table[1, :, :, half:ROT] = np.sin(angles)[:, None]
    return jnp.asarray(table.reshape(2, LEN, 128))


def shards(
    inputs, cotangent, doc_lengths, present,
    w_qkv, m_qkv, v_qkv, w_out, m_out, v_out, w_up, m_up, v_up, w_down, m_down, v_down,
    vector, m_vector, v_vector,
):
    x_own, g_own = inputs.reshape(512, D), cotangent.reshape(512, D)
    docs = doc_lengths[:, 0]
    table = rope_table()
    vec, m_vec, v_vec = (a.reshape(104, 128) for a in (vector, m_vector, v_vector))

    (
        r, sent, h1, h2, h2t, gt, y, dh2, p0, part, wt, wo, x_oth, g_oth, live_oth, docs_oth, db0, norms,
    ) = forward(x_own, g_own, (w_qkv, w_out, w_up, w_down), vec, present, docs, table)
    u, p1, y, dh2, p0, db1 = attention(
        r, docs, docs_oth, present, live_oth, table, vec, sent, part, h2, h2t, g_own, g_oth, gt, y, dh2, p0
    )
    u = u.reshape(4, 2, 4, MB, ROWS, 128)
    y, dxh, other, slots, vecs = backward(
        (x_own, g_own, x_oth, g_oth, h1, u, wt, wo, y, dh2, p0, p1), norms, db0, db1
    )
    masters = (
        w_qkv, m_qkv, v_qkv, w_out, m_out, v_out, w_up, m_up, v_up, w_down, m_down, v_down,
        vec, m_vec, v_vec,
    )
    new = final(x_own, g_own, y, dxh, other, slots, vecs, masters)
    shape = (MB, 1, ROWS, D)
    return (
        new[0].reshape(shape),
        new[1].reshape(shape),
        *new[2:14],
        *(a.reshape(VEC) for a in new[14:]),
    )


def solution(mesh):
    finer = Mesh(mesh.devices.reshape(4, 2, 4, 2, 2), SEQ + FSDP)
    tokens = P(None, FSDP, SEQ, None)
    weight = P(FSDP, SEQ)
    in_specs = (tokens, tokens, P(None, FSDP, None), P(None, FSDP, None)) + (weight,) * 12 + (P(),) * 3
    out_specs = (tokens, tokens) + (weight,) * 12 + (P(),) * 3
    return jax.shard_map(
        shards, mesh=finer, in_specs=in_specs, out_specs=out_specs, check_vma=False
    )
```

```python
import math

import jax
import jax.numpy as jnp
import numpy as np
from jax import lax
from jax.experimental import pallas as pl
from jax.experimental.pallas import tpu as pltpu
from jax.sharding import Mesh
from jax.sharding import PartitionSpec as P

D = 1024
HEADS = 16
HEAD = 64
FF = 4096
ROT = 16
WINDOW = 1024
NDOC = 4
STEP = 10
VEC = 13312
MB = 2
ROWS = 256
LEN = 2048
BETA_ONE = 0.9
BETA_TWO = 0.95
ADAM_EPS = 1e-08
DECAY = 0.01
NORM_EPS = 1e-05
VECTOR_RATE = 0.5
BIG_NEG = -1e30
MESH = pl.DeviceIdType.MESH
MIB = 2**20
F32 = jnp.float32
BF16 = jnp.bfloat16

SEQ = ("x", "zl")
FSDP = ("y", "zh", "c")
LEAD = (4, 2, 4, 2)
EVEN = (
    (("x", "y", "z"), ((0, 48), (48, 32))),
    (("y", "z", "x"), ((80, 48), (128, 32))),
    (("z", "x", "y"), ((160, 48), (208, 48))),
)
ALONG_Y = (
    (("z", "x", "y"), ((0, 64), (64, 64))),
    (("x", "z", "y"), ((128, 64), (192, 64))),
)
GATHER = (EVEN, EVEN, ALONG_Y)
SCATTER = tuple((o[::-1], h, ()) for o, h in EVEN)
SCATTER_Y = tuple((("y",), h, ()) for o, h in ALONG_Y)
SCATTER_XZ = tuple((o[1::-1], h, ("y",)) for o, h in ALONG_Y)
SLOT = (256, 128)


def dot_nn(a, b):
    return lax.dot_general(a, b, (((1,), (0,)), ((), ())), preferred_element_type=F32)


def dot_nt(a, b):
    return lax.dot_general(a, b, (((1,), (1,)), ((), ())), preferred_element_type=F32)


def dot_tn(a, b):
    return lax.dot_general(a, b, (((0,), (0,)), ((), ())), preferred_element_type=F32)


def place():
    zl, zh = lax.axis_index("zl"), lax.axis_index("zh")
    return {
        "x": lax.axis_index("x"),
        "y": lax.axis_index("y"),
        "z": zh * 2 + zl,
        "c": lax.axis_index("c"),
    }


def device(at):
    return (at["x"], lax.rem(at["z"], 2), at["y"], at["z"] // 2, at["c"])


def stepped(me, axis, by):
    at = dict(me)
    at[axis] = lax.rem(me[axis] + by + 4, 4)
    return at


def slot(sel):
    z = sel["z"]
    if isinstance(z, slice):
        return (sel["x"], slice(None), sel["y"], slice(None))
    return (sel["x"], lax.rem(z, 2), sel["y"], z // 2)


def announce(targets):
    bar = pltpu.get_barrier_semaphore()
    for t in targets:
        pl.semaphore_signal(bar, inc=1, device_id=t, device_id_type=MESH)
    return lambda: pl.semaphore_wait(bar, len(targets))


def ring_neighbours(me):
    return [device(stepped(me, a, s)) for a in "xyz" for s in (1, 2, -1)]


def all_neighbours(me):
    return ring_neighbours(me) + [device(p) for k, p in enumerate(peers(me)) if k + 1 in (3, 5, 7)]


class Steps:
    def __init__(self, gens):
        self.live = list(gens)

    def step(self):
        still = []
        for g in self.live:
            if next(g, "end") != "end":
                still.append(g)
        self.live = still

    def finish(self):
        while self.live:
            self.step()


class Sems:
    def __init__(self, send, recv, at=0):
        self.send, self.recv, self.at, self.copies = send, recv, at, []

    def push(self, src, dst, to):
        k = self.at
        self.at += 1
        cp = pltpu.make_async_remote_copy(
            src_ref=src,
            dst_ref=dst,
            send_sem=self.send.at[k],
            recv_sem=self.recv.at[k],
            device_id=to,
            device_id_type=MESH,
        )
        cp.start()
        self.copies.append(cp)
        return k

    def arrived(self, k, dst, to):
        pltpu.make_async_remote_copy(
            src_ref=dst,
            dst_ref=dst,
            send_sem=self.send.at[k],
            recv_sem=self.recv.at[k],
            device_id=to,
            device_id_type=MESH,
        ).wait_recv()

    def drain(self):
        for cp in self.copies:
            cp.wait_send()
        self.copies = []


def other_core(me):
    at = dict(me)
    at["c"] = 1 - me["c"]
    return device(at)


def ring_gather(ref, order, halves, sems, me, known=()):
    h1, h2 = halves
    rows = (h1[0], h1[1] + h2[1])
    known = set(known)
    for a in order:
        i = me[a]
        up, down = device(stepped(me, a, 1)), device(stepped(me, a, -1))

        def block(v, half):
            sel = {b: (slice(None) if b in known else me[b]) for b in "xyz"}
            sel[a] = v
            return ref.at[slot(sel) + (pl.ds(*half), slice(None))]

        left, right, far = lax.rem(i + 3, 4), lax.rem(i + 1, 4), lax.rem(i + 2, 4)
        if not known:
            ks = [
                sems.push(block(i, rows), block(i, rows), device(stepped(me, a, by)))
                for by in (1, 3, 2)
            ]
            yield 0
            for k, frm in zip(ks, (left, right, far)):
                sems.arrived(k, block(frm, rows), up)
            known.add(a)
            continue
        r1 = sems.push(block(i, h1), block(i, h1), up)
        l2 = sems.push(block(i, h2), block(i, h2), down)
        r2 = sems.push(block(i, h2), block(i, h2), up)
        l1 = sems.push(block(i, h1), block(i, h1), down)
        yield 0
        sems.arrived(r1, block(left, h1), up)
        rf = sems.push(block(left, h1), block(left, h1), up)
        sems.arrived(l2, block(right, h2), down)
        lf = sems.push(block(right, h2), block(right, h2), down)
        yield 0
        sems.arrived(r2, block(left, h2), up)
        sems.arrived(l1, block(right, h1), down)
        sems.arrived(rf, block(far, h1), up)
        sems.arrived(lf, block(far, h2), down)
        known.add(a)


def free_dims(sel):
    dims = []
    for n, v in zip(LEAD, slot(sel)):
        if isinstance(v, slice):
            dims.append(n)
    return dims


def each_cell(sel, body):
    lead = slot(sel)
    dims = free_dims(sel)
    count = math.prod(dims)

    def at(n):
        free = []
        for d in reversed(dims):
            free.append(lax.rem(n, d))
            n = n // d
        free = free[::-1]
        full, k = [], 0
        for v in lead:
            if isinstance(v, slice):
                full.append(free[k])
                k += 1
            else:
                full.append(v)
        return tuple(full), tuple(free)

    if count == 1:
        body(*at(0))
    else:

        @pl.loop(0, count)
        def _(n):
            body(*at(n))


def ring_scatter(ref, order, halves, bufs, sems, me, out, done=()):
    h1, h2 = halves
    rows = (h1[0], h1[1] + h2[1])
    done = set(done)
    for n, a in enumerate(order):
        i = me[a]
        up, down = device(stepped(me, a, 1)), device(stepped(me, a, -1))

        def sel(v):
            s = {b: (me[b] if b in done else slice(None)) for b in "xyz"}
            s[a] = v
            return s

        def block(v, half):
            return ref.at[slot(sel(v)) + (pl.ds(*half), slice(None))]

        def add(v, half, terms, final):
            def body(full, free):
                rows = (pl.ds(*half), slice(None))
                total = ref[full + rows].astype(F32)
                for t in terms:
                    total += t[free].astype(F32)
                if final:
                    out[rows] = total
                else:
                    ref[full + rows] = total.astype(BF16)

            each_cell(sel(v), body)

        left, right, far = lax.rem(i + 3, 4), lax.rem(i + 1, 4), lax.rem(i + 2, 4)
        if done:
            ks = [
                sems.push(block(lax.rem(i + by, 4), rows), buf, device(stepped(me, a, by)))
                for by, buf in zip((2, 1, 3), bufs[n])
            ]
            yield 0
            for k, buf in zip(ks, bufs[n]):
                sems.arrived(k, buf, up)
            add(i, rows, bufs[n], len(done) == 2)
            done.add(a)
            continue
        ra, rb, rc, la, lb, lc = bufs[n]
        c0 = sems.push(block(far, h1), ra, up)
        c1 = sems.push(block(far, h2), la, down)
        c2 = sems.push(block(right, h2), rb, up)
        c3 = sems.push(block(left, h1), lb, down)
        yield 0
        sems.arrived(c0, ra, up)
        add(right, h1, [ra], False)
        c4 = sems.push(block(right, h1), rc, up)
        sems.arrived(c1, la, down)
        add(left, h2, [la], False)
        c5 = sems.push(block(left, h2), lc, down)
        yield 0
        sems.arrived(c3, lb, down)
        sems.arrived(c4, rc, up)
        add(i, h1, [lb, rc], False)
        sems.arrived(c2, rb, up)
        sems.arrived(c5, lc, down)
        add(i, h2, [rb, lc], False)
        done.add(a)


def scatter_shapes(order, halves, done=()):
    left = [a for a in "xyz" if a not in done]
    shapes = []
    for n, a in enumerate(order):
        left.remove(a)
        lead = [(4 if "x" in left else 0), (2 if "z" in left else 0), (4 if "y" in left else 0), (2 if "z" in left else 0)]
        n1, n2 = halves[0][1], halves[1][1]
        counts = (n1 + n2,) * 3 if n or done else (n1, n2, n1, n2, n1, n2)
        shapes.append([tuple(d for d in lead if d) + (r, 128) for r in counts])
    return shapes


def scatter_buffers(plan):
    return [
        pltpu.VMEM(s, BF16) for part in plan for stage in scatter_shapes(*part) for s in stage
    ]


def start_scatter(ref, plan, bufs, sems, me, out):
    gens, at = [], 0
    for order, halves, done in plan:
        mine = []
        for stage in scatter_shapes(order, halves, done):
            mine.append(bufs[at : at + len(stage)])
            at += len(stage)
        gens.append(ring_scatter(ref, order, halves, mine, sems, me, out, done))
    return Steps(gens)


def peers(me):
    out = []
    zl = lax.rem(me["z"], 2)
    for k in range(1, 8):
        at = dict(me)
        at["x"] = lax.rem(me["x"] + k // 2, 4)
        at["z"] = me["z"] - zl + lax.rem(zl + k % 2, 2)
        out.append(at)
    return out


def group_index(at):
    return at["x"] * 2 + lax.rem(at["z"], 2)


def own_rows(j):
    return pl.ds(pl.multiple_of(j * ROWS, ROWS), ROWS)


EXCHANGE_ORDER = ((1, 2, 6, 4, 3, 7, 5), (5, 4, 3, 7, 1, 2, 6))


class Exchange:
    def __init__(self, me, src_of, dst_of, send, recv, local):
        self.me, self.dst_of, self.send, self.recv = me, dst_of, send, recv
        self.own = pltpu.make_async_copy(src_of(me), dst_of(me), local)
        self.copies = [self.copy(k + 1, src_of(p), dst_of(me), p) for k, p in enumerate(peers(me))]

    def copy(self, k, src, dst, to):
        return pltpu.make_async_remote_copy(
            src_ref=src,
            dst_ref=dst,
            send_sem=self.send.at[k],
            recv_sem=self.recv.at[k],
            device_id=device(to),
            device_id_type=MESH,
        )

    def start(self):
        self.own.start()
        for core, order in enumerate(EXCHANGE_ORDER):

            @pl.when(self.me["c"] == core)
            def _(order=order):
                for k in order:
                    self.copies[k - 1].start()

    def wait_sent(self):
        for cp in self.copies:
            cp.wait_send()

    def wait_came(self):
        self.own.wait()
        zl = lax.rem(self.me["z"], 2)
        for k in range(1, 8):
            frm = dict(self.me)
            frm["x"] = lax.rem(self.me["x"] + 4 - k // 2, 4)
            frm["z"] = self.me["z"] - zl + lax.rem(zl + k % 2, 2)
            came = self.dst_of(frm)
            self.copy(k, came, came, frm).wait_recv()


def heads_exchange(me, src, dst, send, recv, local):
    return Exchange(
        me,
        lambda at: src.at[at["x"], lax.rem(at["z"], 2)],
        lambda at: dst.at[:, own_rows(group_index(at))],
        send,
        recv,
        local,
    )


def norm_parts(x):
    mean = jnp.mean(x, axis=-1, keepdims=True)
    cen = x - mean
    var = jnp.mean(cen * cen, axis=-1, keepdims=True)
    rstd = lax.rsqrt(var + NORM_EPS)
    return cen * rstd, rstd


def rope(v, table, sign):
    lane = lax.rem(lax.broadcasted_iota(jnp.int32, v.shape, 1), HEAD)
    turned = jnp.where(lane < ROT // 2, pltpu.roll(v, 128 - ROT // 2, 1), pltpu.roll(v, ROT // 2, 1))
    return v * table[0] + (sign * turned) * table[1]


def feed(cells, m, bias, h2, h2t, gs, gt, y_ref, dh_ref, db_ref):
    u_at = [(m, k, slice(None), slice(None), slice(0, 128)) for k in range(2)]
    d_at = [(slice(None), slice(None), m, k, slice(128, 256)) for k in range(2)]
    wu = jnp.concatenate([cells[i].reshape(D, 128) for i in u_at], axis=1)
    wd = jnp.concatenate([cells[i].reshape(D, 128) for i in d_at], axis=1)
    u = dot_nn(h2[...], wu) + bias
    ga = dot_nn(gs[...], wd)
    cdf = 0.5 + 0.5 * lax.erf(u * (0.5**0.5))
    pdf = jnp.exp(-0.5 * u * u) * ((2.0 * math.pi) ** -0.5)
    act = (u * cdf).astype(BF16)
    du = (ga * (cdf + u * pdf)).astype(BF16)
    db_ref[m] = jnp.sum(du.astype(F32), axis=0, keepdims=True)
    for k in range(4):
        rows = slice(k * 256, (k + 1) * 256)
        y_ref[rows] += dot_nt(act[rows], wd)
        dh_ref[rows] += dot_nt(du[rows], wu)
    dwu = dot_nn(h2t[...], du).astype(BF16)
    dwd = dot_nn(gt[...], act).astype(BF16)
    for k in range(2):
        lanes = slice(k * 128, (k + 1) * 128)
        cells[u_at[k]] = dwu[:, lanes].reshape(4, 2, 128, 128)
        cells[d_at[k]] = dwd[:, lanes].reshape(4, 2, 128, 128)


def up_bias(vec, core, f, m):
    at = 64 + m * 8 + core * 2 + f
    return jnp.concatenate([vec[pl.ds(at, 1)], vec[pl.ds(at + 4, 1)]], axis=1)


def forward_kernel(
    x_own, g_own, wq_in, wo_in, wu_in, wd_in, vec, live, docs, table,
    r_out, s_out, h1_out, h2_out, h2t_out, gt_out, y_out, dh_out, p_out, part_out, wt_out, wo_out,
    x_oth, g_oth, live_oth, docs_oth, db_out, norms,
    bqkv, y, dh, xs, gs, gt, h1, h2, h2t, cells, wt, wo, sent, tab, wqs, awq, awu, cwq, cwu,
    send, recv, heads_send, heads_recv, local,
):
    me = place()
    core = me["c"]
    seq = group_index(me)
    partner = other_core(me)
    ready = announce(all_neighbours(me) + [partner])

    def load(src, dst, k):
        cp = pltpu.make_async_copy(src, dst, local.at[k])
        cp.start()
        return cp

    got_x = load(x_own, xs.at[0], 0)
    got_g = load(g_own, gs.at[0:512], 1)
    got_t = load(table.at[:, own_rows(seq)], tab, 2)

    wqs[...] = wq_in[...].T.astype(BF16).reshape(3, 2, HEAD, 64)
    gone = wqs[:, 1 - core].reshape(192, 64)
    awq[...] = jnp.concatenate([gone[:96], gone[96:]], axis=1)
    wu = wu_in[...].astype(BF16)
    awu[...] = jnp.where(core == 0, wu[:, 256:], wu[:, :256])
    ready()
    sems = Sems(send, recv)
    kq = sems.push(awq, cwq, partner)
    ku = sems.push(awu, cwu, partner)
    kx = sems.push(x_own, x_oth, partner)
    kg = sems.push(g_own, g_oth, partner)
    kl = sems.push(live, live_oth, partner)
    kd = sems.push(docs, docs_oth, partner)
    own = slot(me)
    kept = wqs[:, core].reshape(192, 64)
    kept_u = jnp.where(core == 0, wu[:, :256], wu[:, 256:])
    wd = wd_in[...].T.astype(BF16)
    sems.arrived(kq, cwq, partner)
    came = jnp.concatenate([cwq[:, :64], cwq[:, 64:]], axis=0)
    cells[(0,) + own + (slice(0, 192),)] = jnp.where(
        core == 0,
        jnp.concatenate([kept, came], axis=1),
        jnp.concatenate([came, kept], axis=1),
    )
    cells[(0,) + own + (slice(192, 256),)] = wo_in[...].astype(BF16)
    sems.arrived(ku, cwu, partner)
    came_u = cwu[...]
    both = jnp.where(
        core == 0,
        jnp.concatenate([kept_u, came_u], axis=0),
        jnp.concatenate([came_u, kept_u], axis=0),
    )
    for f in range(2):
        cells[(1 + f,) + own + (slice(0, 128),)] = both[:, f * 128 : (f + 1) * 128]
        cells[(1 + f,) + own + (slice(128, 256),)] = wd[:, f * 128 : (f + 1) * 128]
    ring_sems = [Sems(send, recv, 6 + 54 * ph) for ph in range(3)]
    ring = [
        Steps(
            [
                ring_gather(cells.at[ph], o[: 3 if ph < 2 else 2], h, ring_sems[ph], me)
                for o, h in GATHER[ph]
            ]
        )
        for ph in range(3)
    ]

    for i in range(4):
        for j in range(8):
            norms[i : i + 1, j * 128 : (j + 1) * 128] = vec[i * 8 + j : i * 8 + j + 1]
    for j in range(8):
        norms[4:5, j * 128 : (j + 1) * 128] = vec[56 + j : 57 + j] + vec[96 + j : 97 + j]
    for i in range(12):
        one, two = vec[32 + 2 * i : 33 + 2 * i], vec[33 + 2 * i : 34 + 2 * i]
        bqkv[:, i * 128 : (i + 1) * 128] = jnp.where(
            core == 0,
            jnp.concatenate([one[:, :64], two[:, :64]], axis=1),
            jnp.concatenate([one[:, 64:], two[:, 64:]], axis=1),
        )

    def normalise(s):
        @pl.loop(0, 4)
        def _(k):
            rows = pl.ds(pl.multiple_of(k * 128, 128), 128)
            at = pl.ds(pl.multiple_of(s * 512 + k * 128, 128), 128)
            xhat, _ = norm_parts(xs[s, rows].astype(F32))
            h1[at] = (xhat * norms[0:1] + norms[1:2]).astype(BF16)
            h2[at] = (xhat * norms[2:3] + norms[3:4]).astype(BF16)

    def turn(src, dst):
        @pl.loop(0, 4)
        def _(k):
            at = pl.ds(pl.multiple_of(k * 256, 256), 256)
            dst[:, at] = src[at].T

    for ph in range(3):
        ring[ph].step()
    got_x.wait()
    normalise(0)
    for ph in range(3):
        ring[ph].step()
    sems.arrived(kx, x_oth, partner)
    got_x = load(x_oth, xs.at[1], 0)
    for ph in range(3):
        ring[ph].step()
    ring[0].step()
    sems.arrived(kg, g_oth, partner)
    got_g.wait()
    got_g = load(g_oth, gs.at[512:1024], 1)
    got_x.wait()
    normalise(1)
    ring[0].step()
    ring[1].step()
    ring[2].finish()
    ring_sems[2].drain()
    turn(h2, h2t)
    ring[0].finish()

    for k in range(8):
        for r in range(8):
            cell = cells[0, k // 2, k % 2, r // 2, r % 2]
            wt[k * 192 : (k + 1) * 192, r * 128 : (r + 1) * 128] = cell[:192]
            wo[r * 64 : (r + 1) * 64, k * 128 : (k + 1) * 128] = cell[192:]
    got_g.wait()
    got_t.wait()

    def project(s):
        rows = slice(s * 512, (s + 1) * 512)
        do = dot_nt(gs[rows], wo[...]).astype(BF16)
        turns = [jnp.concatenate([tab[i]] * MB, axis=0) for i in range(2)]
        for a in range(4):
            if a < 3:
                part = dot_nt(h1[rows], wt[a * 512 : (a + 1) * 512])
                part = (part + bqkv[:, a * 512 : (a + 1) * 512]).astype(BF16)
            else:
                part = do
            for p in range(4):
                piece = part[:, p * 128 : (p + 1) * 128]
                if a < 2:
                    piece = rope(piece.astype(F32), turns, 1.0).astype(BF16)
                for b in range(MB):
                    sent[b, p, s, a] = piece[b * ROWS : (b + 1) * ROWS]

    heads = heads_exchange(me, sent.at[0], r_out, heads_send, heads_recv, local.at[6])
    project(0)
    ring[1].step()
    project(1)
    heads.start()
    turn(gs, gt)
    ring[1].finish()
    ring_sems[1].drain()
    kept_h = [load(h1, h1_out, 3), load(h2, h2_out, 10)]
    kept_h.append(load(h2t, h2t_out, 11))
    kept_w = [load(wt, wt_out, 4), load(wo, wo_out, 5)]
    kept_w.append(load(sent.at[1], s_out, 9))
    kept_h.append(load(gt, gt_out, 12))
    kept_h.append(load(cells.at[2, :, :, me["y"]], part_out, 8))
    y[...] = jnp.zeros_like(y)
    dh[...] = jnp.zeros_like(dh)

    @pl.loop(0, 4)
    def _(m):
        feed(cells.at[1], m, up_bias(vec, core, 0, m), h2, h2t, gs, gt, y, dh, db_out)

    kept_w.append(load(cells.at[1], p_out, 7))
    kept_w.append(load(y, y_out, 13))
    kept_w.append(load(dh, dh_out, 14))
    heads.wait_sent()
    heads.wait_came()
    sems.arrived(kl, live_oth, partner)
    sems.arrived(kd, docs_oth, partner)
    ring_sems[0].drain()
    sems.drain()
    for cp in kept_h + kept_w:
        cp.wait()


def forward(x, g, weights, vec, live, docs, table):
    any_spec = pl.BlockSpec(memory_space=pl.ANY)
    vmem = pl.BlockSpec(memory_space=pltpu.VMEM)
    n = 3 * 3 * 18 + 6
    return pl.pallas_call(
        forward_kernel,
        name="forward",
        out_shape=(
            jax.ShapeDtypeStruct((4, LEN, 128), BF16),
            jax.ShapeDtypeStruct((4, 2, 4, ROWS, 128), BF16),
            jax.ShapeDtypeStruct((1024, D), BF16),
            jax.ShapeDtypeStruct((1024, D), BF16),
            jax.ShapeDtypeStruct((D, 1024), BF16),
            jax.ShapeDtypeStruct((D, 1024), BF16),
            jax.ShapeDtypeStruct((1024, D), F32),
            jax.ShapeDtypeStruct((1024, D), F32),
            jax.ShapeDtypeStruct(LEAD + SLOT, BF16),
            jax.ShapeDtypeStruct((4, 2, 2) + SLOT, BF16),
            jax.ShapeDtypeStruct((1536, D), BF16),
            jax.ShapeDtypeStruct((512, D), BF16),
            jax.ShapeDtypeStruct((512, D), BF16),
            jax.ShapeDtypeStruct((512, D), BF16),
            jax.ShapeDtypeStruct(live.shape, jnp.int32),
            jax.ShapeDtypeStruct(docs.shape, jnp.int32),
            jax.ShapeDtypeStruct((4, 1, 256), F32),
            jax.ShapeDtypeStruct((5, D), F32),
        ),
        in_specs=[any_spec] * 2 + [vmem] * 5 + [any_spec] * 3,
        out_specs=[any_spec] * 16 + [vmem] * 2,
        scratch_shapes=[
            pltpu.VMEM((1, 1536), F32),
            pltpu.VMEM((1024, D), F32),
            pltpu.VMEM((1024, D), F32),
            pltpu.VMEM((2, 512, D), BF16),
            pltpu.VMEM((1024, D), BF16),
            pltpu.VMEM((D, 1024), BF16),
            pltpu.VMEM((1024, D), BF16),
            pltpu.VMEM((1024, D), BF16),
            pltpu.VMEM((D, 1024), BF16),
            pltpu.VMEM((3,) + LEAD + SLOT, BF16),
            pltpu.VMEM((1536, D), BF16),
            pltpu.VMEM((512, D), BF16),
            pltpu.VMEM((MB, 4, 2, 4, ROWS, 128), BF16),
            pltpu.VMEM((2, ROWS, 128), F32),
            pltpu.VMEM((3, 2, HEAD, 64), BF16),
            pltpu.VMEM((96, 128), BF16),
            pltpu.VMEM((64, 256), BF16),
            pltpu.VMEM((96, 128), BF16),
            pltpu.VMEM((64, 256), BF16),
            pltpu.SemaphoreType.DMA((n,)),
            pltpu.SemaphoreType.DMA((n,)),
            pltpu.SemaphoreType.DMA((8,)),
            pltpu.SemaphoreType.DMA((8,)),
            pltpu.SemaphoreType.DMA((15,)),
        ],
        compiler_params=pltpu.CompilerParams(
            collective_id=0, has_side_effects=True, vmem_limit_bytes=62 * MIB
        ),
    )(x, g, *weights, vec, live, docs, table)


def attention_kernel(
    r_ref, docs_own, docs_oth, live_own, live_oth, table_ref, vec,
    s_hbm, part_in, h2_in, h2t_in, g_own, g_oth, gt_in, y_in, dh_in, p0_in,
    u_out, p_out, y_out, dh_out, p0_out, db_out,
    r_next, t_ref, dk, dv, cells, cells0, y, dh, h2, h2t, gs, gt, *rest,
):
    bufs, (send, recv, heads_send, heads_recv, local) = rest[:-5], rest[-5:]
    me = place()
    ready = announce(all_neighbours(me))
    zl = lax.rem(me["z"], 2)

    def load(src, dst, k):
        cp = pltpu.make_async_copy(src, dst, local.at[k])
        cp.start()
        return cp

    got = load(part_in, cells.at[:, :, me["y"]], 0)
    got0 = load(p0_in, cells0, 11)
    ready()
    heads = heads_exchange(me, s_hbm, r_next, heads_send.at[0], heads_recv.at[0], local.at[3])
    heads.start()
    got.wait()
    ring_sems = Sems(send, recv)
    ring = Steps(
        [ring_gather(cells, o[2:], h, ring_sems, me, o[:2]) for o, h in GATHER[2]]
    )
    ring.step()
    scatter_sems = Sems(send, recv, 12)
    scatter = start_scatter(cells0, SCATTER_Y, bufs, scatter_sems, me, None)
    scale = HEAD**-0.5
    lane = lax.broadcasted_iota(jnp.int32, (ROWS, 128), 1)
    first = lane < HEAD

    def pair(v):
        zero = jnp.zeros_like(v)
        return jnp.concatenate([jnp.where(first, v, zero), jnp.where(first, zero, v)], axis=0)

    def merge(v):
        return jnp.where(first, v[:ROWS], v[ROWS:])

    def one(b, q0, k0, width):
        qs, ks = pl.ds(q0, ROWS), pl.ds(k0, width)
        r = r_next if b else r_ref
        q, do = pair(r[0, qs] * jnp.asarray(scale, BF16)), pair(r[3, qs])
        k, v = r[1, ks], r[2, ks]
        row = q0 + lax.broadcasted_iota(jnp.int32, (1, ROWS), 1)
        lo, end = row - (WINDOW - 1), 0
        for d in range(NDOC - 1):
            end = end + jnp.where(zl == 0, docs_own[b, d], docs_oth[b, d])
            lo = jnp.where(row >= end, jnp.maximum(lo, end), lo)
        live = jnp.where(zl == 0, live_own[b, :, ks], live_oth[b, :, ks])
        col = k0 + lax.broadcasted_iota(jnp.int32, (width, 1), 0)
        jeff = jnp.where(live.reshape(width, 1) > 0, col, LEN)
        i = q0 + lax.broadcasted_iota(jnp.int32, (width, ROWS), 1)
        j = k0 + lax.broadcasted_iota(jnp.int32, (width, ROWS), 0)
        ok = ((jeff <= i) & (jeff >= lo)) | (i == j)
        s = jnp.where(jnp.concatenate([ok, ok], axis=1), dot_nt(k, q), BIG_NEG)
        e = jnp.exp(s - jnp.max(s, axis=0, keepdims=True))
        prob = e * (1.0 / jnp.sum(e, axis=0, keepdims=True))
        low = prob.astype(BF16)
        dp = dot_nt(v, do)
        ds = (prob * (dp - jnp.sum(dp * prob, axis=0, keepdims=True))).astype(BF16)
        t_ref[0, b, qs] = merge(dot_tn(v, low).T).astype(BF16)
        dq = merge(dot_tn(k, ds).T) * scale
        table = [table_ref[n, qs] for n in range(2)]
        t_ref[1, b, qs] = rope(dq, table, -1.0).astype(BF16)
        dk[ks] += dot_nn(ds, q)
        dv[ks] += dot_nn(low, do)

    def ship(b):
        out = Exchange(
            me,
            lambda at: t_ref.at[:, b, own_rows(group_index(at))],
            lambda at: u_out.at[group_index(at), :, b],
            heads_send.at[1 + b],
            heads_recv.at[1 + b],
            local.at[1 + b],
        )
        out.start()
        return out

    shipped = []
    for b in range(MB):
        if b == 1:
            heads.wait_came()
        dk[...] = jnp.zeros_like(dk)
        dv[...] = jnp.zeros_like(dv)
        for n in range(4):
            one(b, n * ROWS, 0, (n + 1) * ROWS)
        if b == 0:
            ring.step()
            got0.wait()
            scatter.step()
            loads = [
                load(src, dst, 4 + k)
                for k, (src, dst) in enumerate(
                    (
                        (h2_in, h2),
                        (h2t_in, h2t),
                        (g_own, gs.at[0:512]),
                        (g_oth, gs.at[512:1024]),
                        (gt_in, gt),
                        (y_in, y),
                        (dh_in, dh),
                    )
                )
            ]

        @pl.loop(4, 8)
        def _(n):
            one(
                b,
                pl.multiple_of(n * ROWS, ROWS),
                pl.multiple_of((n - 4) * ROWS, ROWS),
                5 * ROWS,
            )

        table = [table_ref[n] for n in range(2)]
        t_ref[2, b] = rope(dk[...], table, -1.0).astype(BF16)
        t_ref[3, b] = dv[...].astype(BF16)
        shipped.append(ship(b))
    heads.wait_sent()
    scatter.step()
    ring.finish()
    ring_sems.drain()
    for cp in loads:
        cp.wait()

    @pl.loop(0, 4)
    def _(m):
        feed(cells, m, up_bias(vec, me["c"], 1, m), h2, h2t, gs, gt, y, dh, db_out)

    kept = [load(cells, p_out, 4), load(y, y_out, 5), load(dh, dh_out, 6)]
    scatter.finish()
    scatter_sems.drain()
    kept.append(load(cells0.at[:, :, me["y"]], p0_out, 7))
    for out in shipped:
        out.wait_came()
        out.wait_sent()
    for cp in kept:
        cp.wait()


def attention(r, docs, docs_oth, live, live_oth, table, vec, *streamed):
    vmem = pl.BlockSpec(memory_space=pltpu.VMEM)
    smem = pl.BlockSpec(memory_space=pltpu.SMEM)
    any_spec = pl.BlockSpec(memory_space=pl.ANY)
    n = 12 + 12
    return pl.pallas_call(
        attention_kernel,
        name="attention",
        out_shape=(
            jax.ShapeDtypeStruct((8, 4, MB, ROWS, 128), BF16),
            jax.ShapeDtypeStruct(LEAD + SLOT, BF16),
            jax.ShapeDtypeStruct((1024, D), F32),
            jax.ShapeDtypeStruct((1024, D), F32),
            jax.ShapeDtypeStruct((4, 2, 2) + SLOT, BF16),
            jax.ShapeDtypeStruct((4, 1, 256), F32),
        ),
        in_specs=[vmem, smem, smem, vmem, vmem, vmem, vmem] + [any_spec] * 10,
        out_specs=[any_spec] * 5 + [vmem],
        scratch_shapes=[
            pltpu.VMEM((4, LEN, 128), BF16),
            pltpu.VMEM((4, MB, LEN, 128), BF16),
            pltpu.VMEM((LEN, 128), F32),
            pltpu.VMEM((LEN, 128), F32),
            pltpu.VMEM(LEAD + SLOT, BF16),
            pltpu.VMEM(LEAD + SLOT, BF16),
            pltpu.VMEM((1024, D), F32),
            pltpu.VMEM((1024, D), F32),
            pltpu.VMEM((1024, D), BF16),
            pltpu.VMEM((D, 1024), BF16),
            pltpu.VMEM((1024, D), BF16),
            pltpu.VMEM((D, 1024), BF16),
        ]
        + scatter_buffers(SCATTER_Y)
        + [
            pltpu.SemaphoreType.DMA((n,)),
            pltpu.SemaphoreType.DMA((n,)),
            pltpu.SemaphoreType.DMA((3, 8)),
            pltpu.SemaphoreType.DMA((3, 8)),
            pltpu.SemaphoreType.DMA((12,)),
        ],
        compiler_params=pltpu.CompilerParams(
            collective_id=1, has_side_effects=True, vmem_limit_bytes=63 * MIB
        ),
    )(r, docs, docs_oth, live, live_oth, table, vec, *streamed)


def vector_sum(vecs, sems, me):
    for n, a in enumerate("xyz"):
        i = me[a]
        ks = []
        for by in (1, 2, 3):
            ks.append(sems.push(vecs.at[n, i], vecs.at[n, i], device(stepped(me, a, by))))
        yield 0
        for k, by in zip(ks, (1, 2, 3)):
            frm = stepped(me, a, -by)
            sems.arrived(k, vecs.at[n, frm[a]], device(frm))
        total = vecs[n, 0] + vecs[n, 1] + vecs[n, 2] + vecs[n, 3]
        if n < 2:
            vecs[n + 1, me["xyz"[n + 1]]] = total
        else:
            vecs[3, me["c"]] = total


def backward_kernel(
    x_own, g_own, x_oth, g_oth, h_in, u_in, wt_in, wo_in, y_in, dh_in, p0_in, p1_in, norms, db0, db1,
    y_out, dx_out, slots, v_out,
    xs, gs, hs, us, wt, wo, ys, dhs, dqkv, os, cells, e_send, e_came, vecs, *rest,
):
    bufs, (send, recv, local) = rest[:-3], rest[-3:]
    me = place()
    core = me["c"]
    partner = other_core(me)
    ready = announce(ring_neighbours(me) + [partner])

    def load(src, dst, k):
        cp = pltpu.make_async_copy(src, dst, local.at[k])
        cp.start()
        return cp

    zeroth = [load(p1_in, cells.at[2], 1), load(p0_in, cells.at[1, :, :, me["y"]], 0)]
    first = [
        load(u_in, us, 2),
        load(h_in, hs, 3),
        load(g_own, gs.at[0:512], 4),
        load(g_oth, gs.at[512:1024], 5),
    ]
    ready()
    sems = Sems(send, recv)
    for cp in zeroth:
        cp.wait()
    cut = len(scatter_buffers(SCATTER))
    ring_ud = start_scatter(cells.at[2], SCATTER, bufs[cut : 2 * cut], sems, me, slots.at[core, 2])
    ring_ud.live += start_scatter(
        cells.at[1], SCATTER_XZ, bufs[2 * cut :], sems, me, slots.at[core, 1]
    ).live
    ring_ud.step()
    for cp in first:
        cp.wait()
    second = [
        load(wt_in, wt, 6),
        load(wo_in, wo, 7),
        load(x_own, xs.at[0], 8),
        load(x_oth, xs.at[1], 9),
        load(dh_in.at[512:1024], dhs, 10),
        load(y_in.at[512:1024], ys, 11),
    ]
    for s in range(2):
        rows = slice(s * 512, (s + 1) * 512)
        for p in range(4):
            for a in range(4):
                piece = us[p, s, a].reshape(512, 128)
                if a == 0:
                    os[rows, p * 128 : (p + 1) * 128] = piece
                else:
                    at = (a - 1) * 512 + p * 128
                    dqkv[rows, at : at + 128] = piece
    for m in range(4):
        part = dot_tn(dqkv[:, m * 384 : (m + 1) * 384], hs[...]).astype(BF16)
        for k in range(2):
            for r in range(8):
                cells[0, m, k, r // 2, r % 2, 0:192] = part[
                    k * 192 : (k + 1) * 192, r * 128 : (r + 1) * 128
                ]
    part = dot_tn(os[...], gs[...]).astype(BF16)
    for k in range(8):
        for r in range(8):
            cells[0, k // 2, k % 2, r // 2, r % 2, 192:256] = part[
                r * 64 : (r + 1) * 64, k * 128 : (k + 1) * 128
            ]
    ring_ud.step()
    ring = start_scatter(cells.at[0], SCATTER, bufs[:cut], sems, me, slots.at[core, 0])
    ring.step()
    for cp in second:
        cp.wait()
    sums = jnp.zeros((5, D), F32)
    for s in (1, 0):
        rows = slice(s * 512, (s + 1) * 512)
        if s == 0:
            second = [load(dh_in.at[0:512], dhs, 10), load(y_in.at[0:512], ys, 11)]
        attn = dot_nn(os[rows], wo[...])
        dh1 = dot_nn(dqkv[rows], wt[...])
        if s == 0:
            for cp in second:
                cp.wait()
        y = ys[...] + attn
        dh2 = dhs[...]
        xhat, _ = norm_parts(xs[s].astype(F32))
        dx = dh1 * norms[0:1] + dh2 * norms[2:3]
        sums += jnp.concatenate(
            [
                jnp.sum(dh1 * xhat, axis=0, keepdims=True),
                jnp.sum(dh1, axis=0, keepdims=True),
                jnp.sum(dh2 * xhat, axis=0, keepdims=True),
                jnp.sum(dh2, axis=0, keepdims=True),
                jnp.sum(gs[rows].astype(F32), axis=0, keepdims=True) * (1.0 - s),
            ],
            axis=0,
        )
        if s == 1:
            e_send[0] = y.astype(BF16)
            e_send[1] = dx.astype(BF16)
            ke = sems.push(e_send, e_came, partner)
            ring_ud.step()
            ring.step()
        else:
            ys[...] = y
            dhs[...] = dx
    bias = jnp.sum(dqkv[...].astype(F32), axis=0, keepdims=True)
    vecs[0, me["x"]] = jnp.zeros((16, D), F32)
    vecs[0, me["x"], 0:5] = sums
    vecs[0, me["x"], 5:6] = bias[:, :1024]
    vecs[0, me["x"], 6:7, 0:512] = bias[:, 1024:]
    for f, db in enumerate((db0, db1)):
        for m in range(4):
            vecs[0, me["x"], 8 + f * 4 + m : 9 + f * 4 + m, 0:256] = db[m]
    line = Steps([vector_sum(vecs, sems, me)])
    line.step()
    ring_ud.step()
    ring.step()
    sems.arrived(ke, e_came, partner)

    @pl.loop(0, 4)
    def _(k):
        rows = pl.ds(pl.multiple_of(k * 128, 128), 128)
        x = xs[0, rows].astype(F32)
        ys[rows] = x + ys[rows] + e_came[0, rows].astype(F32) + norms[4:5]
        dxh = dhs[rows] + e_came[1, rows].astype(F32)
        xhat, rstd = norm_parts(x)
        dhs[rows] = gs[rows].astype(F32) + rstd * (
            dxh
            - jnp.mean(dxh, axis=-1, keepdims=True)
            - xhat * jnp.mean(dxh * xhat, axis=-1, keepdims=True)
        )

    kept = [load(ys, y_out, 0), load(dhs, dx_out, 1)]
    while ring.live or line.live or ring_ud.live:
        ring_ud.step()
        line.step()
        ring.step()
    kw = sems.push(slots.at[core], slots.at[core], partner)
    kv = sems.push(vecs.at[3, core], vecs.at[3, core], partner)
    sems.arrived(kw, slots.at[1 - core], partner)
    sems.arrived(kv, vecs.at[3, 1 - core], partner)
    for cp in kept:
        cp.wait()
    v_out[...] = vecs[3, 0:2]
    sems.drain()


def backward(streamed, norms, db0, db1):
    any_spec = pl.BlockSpec(memory_space=pl.ANY)
    vmem = pl.BlockSpec(memory_space=pltpu.VMEM)
    n = 2 * 3 * 12 + 2 * 6 + 9 + 3
    return pl.pallas_call(
        backward_kernel,
        name="backward",
        out_shape=(
            jax.ShapeDtypeStruct((512, D), F32),
            jax.ShapeDtypeStruct((512, D), F32),
            jax.ShapeDtypeStruct((2, 3) + SLOT, F32),
            jax.ShapeDtypeStruct((2, 16, D), F32),
        ),
        in_specs=[any_spec] * 12 + [vmem] * 3,
        out_specs=[any_spec] * 2 + [vmem] * 2,
        scratch_shapes=[
            pltpu.VMEM((2, 512, D), BF16),
            pltpu.VMEM((1024, D), BF16),
            pltpu.VMEM((1024, D), BF16),
            pltpu.VMEM((4, 2, 4, MB, ROWS, 128), BF16),
            pltpu.VMEM((1536, D), BF16),
            pltpu.VMEM((512, D), BF16),
            pltpu.VMEM((512, D), F32),
            pltpu.VMEM((512, D), F32),
            pltpu.VMEM((1024, 1536), BF16),
            pltpu.VMEM((1024, 512), BF16),
            pltpu.VMEM((3,) + LEAD + SLOT, BF16),
            pltpu.VMEM((2, 512, D), BF16),
            pltpu.VMEM((2, 512, D), BF16),
            pltpu.VMEM((4, 4, 16, D), F32),
        ]
        + scatter_buffers(SCATTER + SCATTER + SCATTER_XZ)
        + [
            pltpu.SemaphoreType.DMA((n,)),
            pltpu.SemaphoreType.DMA((n,)),
            pltpu.SemaphoreType.DMA((12,)),
        ],
        compiler_params=pltpu.CompilerParams(
            collective_id=2, has_side_effects=True, vmem_limit_bytes=63 * MIB
        ),
    )(*streamed, norms, db0, db1)


def adam(weight, first, second, grad, rate):
    first_new = BETA_ONE * first + (1.0 - BETA_ONE) * grad
    second_new = BETA_TWO * second + (1.0 - BETA_TWO) * grad * grad
    first_hat = first_new / (1.0 - BETA_ONE**STEP)
    second_hat = second_new / (1.0 - BETA_TWO**STEP)
    weight_new = weight - rate * (first_hat / (jnp.sqrt(second_hat) + ADAM_EPS) + DECAY * weight)
    return (first_new, second_new, weight_new)


RATES = (D**-0.5, max(1, D * 16 // LEN) ** -0.5, D**-0.5, FF**-0.5, VECTOR_RATE)


def final_kernel(y_ref, dx_ref, slots, vecs, *rest):
    masters, outs, (grad, line) = rest[:15], rest[15:-2], rest[-2:]
    core = lax.axis_index("c")
    outs[0][...] = y_ref[...]
    outs[1][...] = dx_ref[...]

    def update(k, total):
        new = adam(*[r[...] for r in masters[3 * k : 3 * k + 3]], total, RATES[k])
        for ref, value in zip(outs[2 + 3 * k : 5 + 3 * k], new):
            ref[...] = value

    step = pl.program_id(0)

    @pl.when(step == 0)
    def _():
        cols = []
        for t in range(3):
            rows = slice(t * 64, (t + 1) * 64)
            both = jnp.concatenate([slots[0, 0, rows], slots[1, 0, rows]], axis=0).T
            cols.append(jnp.where(core == 0, both[:64], both[64:]))
        update(0, jnp.concatenate(cols, axis=1))
        update(1, slots[core, 0, 192:256])

    @pl.when(step == 1)
    def _():
        rows = pl.ds(pl.multiple_of(core * 64, 64), 64)
        update(2, jnp.concatenate([slots[c, 1 + f, rows] for c in range(2) for f in range(2)], axis=1))

    @pl.when(step == 2)
    def _():
        for f in range(2):
            grad[f * 128 : (f + 1) * 128] = slots[core, 1 + f, 128:256].T
        update(3, grad[...])

    @pl.when(step == 3)
    def _():
        whole = vecs[0, 0:5] + vecs[1, 0:5]
        for i, at in ((0, 0), (1, 8), (2, 16), (3, 24), (4, 56), (4, 96)):
            for j in range(8):
                line[at + j : at + j + 1] = whole[i : i + 1, j * 128 : (j + 1) * 128]
        for i in range(12):
            lanes = slice(i % 8 * 128, (i % 8 + 1) * 128)
            zero, one = vecs[0, 5 + i // 8, lanes], vecs[1, 5 + i // 8, lanes]
            line[32 + 2 * i] = jnp.concatenate([zero[:64], one[:64]])
            line[33 + 2 * i] = jnp.concatenate([zero[64:], one[64:]])
        for n in range(8):
            for c in range(2):
                for f in range(2):
                    line[64 + n * 4 + c * 2 + f] = vecs[
                        c, 8 + f * 4 + n // 2, n % 2 * 128 : (n % 2 + 1) * 128
                    ]
        update(4, line[...])


def final(y, dx, slots, vecs, masters):
    def tok():
        return pl.BlockSpec((128, D), lambda s: (s, 0))

    def whole(a):
        return pl.BlockSpec(a.shape, lambda s: (0,) * len(a.shape))

    return pl.pallas_call(
        final_kernel,
        name="final",
        grid=(4,),
        out_shape=[jax.ShapeDtypeStruct((512, D), F32)] * 2
        + [jax.ShapeDtypeStruct(m.shape, F32) for m in masters],
        in_specs=[tok(), tok()]
        + [whole(a) for a in (slots, vecs, *masters)],
        out_specs=[tok(), tok()] + [whole(m) for m in masters],
        scratch_shapes=[pltpu.VMEM((256, 128), F32), pltpu.VMEM((104, 128), F32)],
        compiler_params=pltpu.CompilerParams(vmem_limit_bytes=63 * MIB),
    )(y, dx, slots, vecs, *masters)


def rope_table():
    half = ROT // 2
    inverse = np.float32(10000.0) ** (-(np.arange(half, dtype=np.float32) * 2) / np.float32(ROT))
    angles = np.arange(LEN, dtype=np.float32)[:, None] * inverse.astype(np.float32)[None, :]
    table = np.zeros((2, LEN, 2, HEAD), np.float32)
    table[0] = 1.0
    table[0, :, :, :half] = np.cos(angles)[:, None]
    table[0, :, :, half:ROT] = np.cos(angles)[:, None]
    table[1, :, :, :half] = -np.sin(angles)[:, None]
    table[1, :, :, half:ROT] = np.sin(angles)[:, None]
    return jnp.asarray(table.reshape(2, LEN, 128))


def shards(
    inputs, cotangent, doc_lengths, present,
    w_qkv, m_qkv, v_qkv, w_out, m_out, v_out, w_up, m_up, v_up, w_down, m_down, v_down,
    vector, m_vector, v_vector,
):
    x_own, g_own = inputs.reshape(512, D), cotangent.reshape(512, D)
    docs = doc_lengths[:, 0]
    table = rope_table()
    vec, m_vec, v_vec = (a.reshape(104, 128) for a in (vector, m_vector, v_vector))

    (
        r, sent, h1, h2, h2t, gt, y, dh2, p0, part, wt, wo, x_oth, g_oth, live_oth, docs_oth, db0, norms,
    ) = forward(x_own, g_own, (w_qkv, w_out, w_up, w_down), vec, present, docs, table)
    u, p1, y, dh2, p0, db1 = attention(
        r, docs, docs_oth, present, live_oth, table, vec, sent, part, h2, h2t, g_own, g_oth, gt, y, dh2, p0
    )
    u = u.reshape(4, 2, 4, MB, ROWS, 128)
    y, dx, slots, vecs = backward(
        (x_own, g_own, x_oth, g_oth, h1, u, wt, wo, y, dh2, p0, p1), norms, db0, db1
    )
    masters = (
        w_qkv, m_qkv, v_qkv, w_out, m_out, v_out, w_up, m_up, v_up, w_down, m_down, v_down,
        vec, m_vec, v_vec,
    )
    new = final(y, dx, slots, vecs, masters)
    shape = (MB, 1, ROWS, D)
    return (
        new[0].reshape(shape),
        new[1].reshape(shape),
        *new[2:14],
        *(a.reshape(VEC) for a in new[14:]),
    )


def solution(mesh):
    finer = Mesh(mesh.devices.reshape(4, 2, 4, 2, 2), SEQ + FSDP)
    tokens = P(None, FSDP, SEQ, None)
    weight = P(FSDP, SEQ)
    in_specs = (tokens, tokens, P(None, FSDP, None), P(None, FSDP, None)) + (weight,) * 12 + (P(),) * 3
    out_specs = (tokens, tokens) + (weight,) * 12 + (P(),) * 3
    return jax.shard_map(
        shards, mesh=finer, in_specs=in_specs, out_specs=out_specs, check_vma=False
    )
```

```python
import math

import jax
import jax.numpy as jnp
import numpy as np
from jax import lax
from jax.experimental import pallas as pl
from jax.experimental.pallas import tpu as pltpu
from jax.sharding import Mesh
from jax.sharding import PartitionSpec as P

D = 1024
HEADS = 16
HEAD = 64
FF = 4096
ROT = 16
WINDOW = 1024
NDOC = 4
STEP = 10
VEC = 13312
MB = 2
ROWS = 256
LEN = 2048
BETA_ONE = 0.9
BETA_TWO = 0.95
ADAM_EPS = 1e-08
DECAY = 0.01
NORM_EPS = 1e-05
VECTOR_RATE = 0.5
BIG_NEG = -1e30
MESH = pl.DeviceIdType.MESH
MIB = 2**20
F32 = jnp.float32
BF16 = jnp.bfloat16

SEQ = ("x", "zl")
FSDP = ("y", "zh", "c")
LEAD = (4, 2, 4, 2)
EVEN = (
    (("x", "y", "z"), ((0, 48), (48, 32))),
    (("y", "z", "x"), ((80, 48), (128, 32))),
    (("z", "x", "y"), ((160, 48), (208, 48))),
)
ALONG_Y = (
    (("z", "x", "y"), ((0, 64), (64, 64))),
    (("x", "z", "y"), ((128, 64), (192, 64))),
)
GATHER = (EVEN, EVEN, ALONG_Y)
SCATTER = tuple((o[::-1], h, ()) for o, h in EVEN)
SCATTER_Y = tuple((("y",), h, ()) for o, h in ALONG_Y)
SCATTER_XZ = tuple((o[1::-1], h, ("y",)) for o, h in ALONG_Y)
SLOT = (256, 128)


def dot_nn(a, b):
    return lax.dot_general(a, b, (((1,), (0,)), ((), ())), preferred_element_type=F32)


def dot_nt(a, b):
    return lax.dot_general(a, b, (((1,), (1,)), ((), ())), preferred_element_type=F32)


def dot_tn(a, b):
    return lax.dot_general(a, b, (((0,), (0,)), ((), ())), preferred_element_type=F32)


def place():
    zl, zh = lax.axis_index("zl"), lax.axis_index("zh")
    return {
        "x": lax.axis_index("x"),
        "y": lax.axis_index("y"),
        "z": zh * 2 + zl,
        "c": lax.axis_index("c"),
    }


def device(at):
    return (at["x"], lax.rem(at["z"], 2), at["y"], at["z"] // 2, at["c"])


def stepped(me, axis, by):
    at = dict(me)
    at[axis] = lax.rem(me[axis] + by + 4, 4)
    return at


def slot(sel):
    z = sel["z"]
    if isinstance(z, slice):
        return (sel["x"], slice(None), sel["y"], slice(None))
    return (sel["x"], lax.rem(z, 2), sel["y"], z // 2)


def announce(targets):
    bar = pltpu.get_barrier_semaphore()
    for t in targets:
        pl.semaphore_signal(bar, inc=1, device_id=t, device_id_type=MESH)
    return lambda: pl.semaphore_wait(bar, len(targets))


def ring_neighbours(me):
    return [device(stepped(me, a, s)) for a in "xyz" for s in (1, 2, -1)]


def all_neighbours(me):
    return ring_neighbours(me) + [device(p) for k, p in enumerate(peers(me)) if k + 1 in (3, 5, 7)]


class Steps:
    def __init__(self, gens):
        self.live = list(gens)

    def step(self):
        still = []
        for g in self.live:
            if next(g, "end") != "end":
                still.append(g)
        self.live = still

    def finish(self):
        while self.live:
            self.step()


class Sems:
    def __init__(self, send, recv, at=0):
        self.send, self.recv, self.at, self.copies = send, recv, at, []

    def push(self, src, dst, to):
        k = self.at
        self.at += 1
        cp = pltpu.make_async_remote_copy(
            src_ref=src,
            dst_ref=dst,
            send_sem=self.send.at[k],
            recv_sem=self.recv.at[k],
            device_id=to,
            device_id_type=MESH,
        )
        cp.start()
        self.copies.append(cp)
        return k

    def arrived(self, k, dst, to):
        pltpu.make_async_remote_copy(
            src_ref=dst,
            dst_ref=dst,
            send_sem=self.send.at[k],
            recv_sem=self.recv.at[k],
            device_id=to,
            device_id_type=MESH,
        ).wait_recv()

    def drain(self):
        for cp in self.copies:
            cp.wait_send()
        self.copies = []


def other_core(me):
    at = dict(me)
    at["c"] = 1 - me["c"]
    return device(at)


def ring_gather(ref, order, halves, sems, me, known=()):
    h1, h2 = halves
    rows = (h1[0], h1[1] + h2[1])
    known = set(known)
    for a in order:
        i = me[a]
        up, down = device(stepped(me, a, 1)), device(stepped(me, a, -1))

        def block(v, half):
            sel = {b: (slice(None) if b in known else me[b]) for b in "xyz"}
            sel[a] = v
            return ref.at[slot(sel) + (pl.ds(*half), slice(None))]

        left, right, far = lax.rem(i + 3, 4), lax.rem(i + 1, 4), lax.rem(i + 2, 4)
        if not known:
            ks = [
                sems.push(block(i, rows), block(i, rows), device(stepped(me, a, by)))
                for by in (1, 3, 2)
            ]
            yield 0
            for k, frm in zip(ks, (left, right, far)):
                sems.arrived(k, block(frm, rows), up)
            known.add(a)
            continue
        r1 = sems.push(block(i, h1), block(i, h1), up)
        l2 = sems.push(block(i, h2), block(i, h2), down)
        r2 = sems.push(block(i, h2), block(i, h2), up)
        l1 = sems.push(block(i, h1), block(i, h1), down)
        yield 0
        sems.arrived(r1, block(left, h1), up)
        rf = sems.push(block(left, h1), block(left, h1), up)
        sems.arrived(l2, block(right, h2), down)
        lf = sems.push(block(right, h2), block(right, h2), down)
        yield 0
        sems.arrived(r2, block(left, h2), up)
        sems.arrived(l1, block(right, h1), down)
        sems.arrived(rf, block(far, h1), up)
        sems.arrived(lf, block(far, h2), down)
        known.add(a)


def free_dims(sel):
    dims = []
    for n, v in zip(LEAD, slot(sel)):
        if isinstance(v, slice):
            dims.append(n)
    return dims


def each_cell(sel, body):
    lead = slot(sel)
    dims = free_dims(sel)
    count = math.prod(dims)

    def at(n):
        free = []
        for d in reversed(dims):
            free.append(lax.rem(n, d))
            n = n // d
        free = free[::-1]
        full, k = [], 0
        for v in lead:
            if isinstance(v, slice):
                full.append(free[k])
                k += 1
            else:
                full.append(v)
        return tuple(full), tuple(free)

    if count == 1:
        body(*at(0))
    else:

        @pl.loop(0, count)
        def _(n):
            body(*at(n))


def ring_scatter(ref, order, halves, bufs, sems, me, out, done=()):
    h1, h2 = halves
    rows = (h1[0], h1[1] + h2[1])
    done = set(done)
    for n, a in enumerate(order):
        i = me[a]
        up, down = device(stepped(me, a, 1)), device(stepped(me, a, -1))

        def sel(v):
            s = {b: (me[b] if b in done else slice(None)) for b in "xyz"}
            s[a] = v
            return s

        def block(v, half):
            return ref.at[slot(sel(v)) + (pl.ds(*half), slice(None))]

        def add(v, half, terms, final):
            def body(full, free):
                rows = (pl.ds(*half), slice(None))
                total = ref[full + rows].astype(F32)
                for t in terms:
                    total += t[free].astype(F32)
                if final:
                    out[rows] = total
                else:
                    ref[full + rows] = total.astype(BF16)

            each_cell(sel(v), body)

        left, right, far = lax.rem(i + 3, 4), lax.rem(i + 1, 4), lax.rem(i + 2, 4)
        if done:
            ks = [
                sems.push(block(lax.rem(i + by, 4), rows), buf, device(stepped(me, a, by)))
                for by, buf in zip((2, 1, 3), bufs[n])
            ]
            yield 0
            for k, buf in zip(ks, bufs[n]):
                sems.arrived(k, buf, up)
            add(i, rows, bufs[n], len(done) == 2)
            done.add(a)
            continue
        ra, rb, rc, la, lb, lc = bufs[n]
        c0 = sems.push(block(far, h1), ra, up)
        c1 = sems.push(block(far, h2), la, down)
        c2 = sems.push(block(right, h2), rb, up)
        c3 = sems.push(block(left, h1), lb, down)
        yield 0
        sems.arrived(c0, ra, up)
        add(right, h1, [ra], False)
        c4 = sems.push(block(right, h1), rc, up)
        sems.arrived(c1, la, down)
        add(left, h2, [la], False)
        c5 = sems.push(block(left, h2), lc, down)
        yield 0
        sems.arrived(c3, lb, down)
        sems.arrived(c4, rc, up)
        add(i, h1, [lb, rc], False)
        sems.arrived(c2, rb, up)
        sems.arrived(c5, lc, down)
        add(i, h2, [rb, lc], False)
        done.add(a)


def scatter_shapes(order, halves, done=()):
    left = [a for a in "xyz" if a not in done]
    shapes = []
    for n, a in enumerate(order):
        left.remove(a)
        lead = [(4 if "x" in left else 0), (2 if "z" in left else 0), (4 if "y" in left else 0), (2 if "z" in left else 0)]
        n1, n2 = halves[0][1], halves[1][1]
        counts = (n1 + n2,) * 3 if n or done else (n1, n2, n1, n2, n1, n2)
        shapes.append([tuple(d for d in lead if d) + (r, 128) for r in counts])
    return shapes


def scatter_buffers(plan):
    return [
        pltpu.VMEM(s, BF16) for part in plan for stage in scatter_shapes(*part) for s in stage
    ]


def start_scatter(ref, plan, bufs, sems, me, out):
    gens, at = [], 0
    for order, halves, done in plan:
        mine = []
        for stage in scatter_shapes(order, halves, done):
            mine.append(bufs[at : at + len(stage)])
            at += len(stage)
        gens.append(ring_scatter(ref, order, halves, mine, sems, me, out, done))
    return Steps(gens)


def peers(me):
    out = []
    zl = lax.rem(me["z"], 2)
    for k in range(1, 8):
        at = dict(me)
        at["x"] = lax.rem(me["x"] + k // 2, 4)
        at["z"] = me["z"] - zl + lax.rem(zl + k % 2, 2)
        out.append(at)
    return out


def group_index(at):
    return at["x"] * 2 + lax.rem(at["z"], 2)


def own_rows(j):
    return pl.ds(pl.multiple_of(j * ROWS, ROWS), ROWS)


EXCHANGE_ORDER = ((1, 2, 6, 4, 3, 7, 5), (5, 4, 3, 7, 1, 2, 6))


class Exchange:
    def __init__(self, me, src_of, dst_of, send, recv, local):
        self.me, self.dst_of, self.send, self.recv = me, dst_of, send, recv
        self.own = pltpu.make_async_copy(src_of(me), dst_of(me), local)
        self.copies = [self.copy(k + 1, src_of(p), dst_of(me), p) for k, p in enumerate(peers(me))]

    def copy(self, k, src, dst, to):
        return pltpu.make_async_remote_copy(
            src_ref=src,
            dst_ref=dst,
            send_sem=self.send.at[k],
            recv_sem=self.recv.at[k],
            device_id=device(to),
            device_id_type=MESH,
        )

    def start(self):
        self.own.start()
        for core, order in enumerate(EXCHANGE_ORDER):

            @pl.when(self.me["c"] == core)
            def _(order=order):
                for k in order:
                    self.copies[k - 1].start()

    def wait_sent(self):
        for cp in self.copies:
            cp.wait_send()

    def wait_came(self):
        self.own.wait()
        zl = lax.rem(self.me["z"], 2)
        for k in range(1, 8):
            frm = dict(self.me)
            frm["x"] = lax.rem(self.me["x"] + 4 - k // 2, 4)
            frm["z"] = self.me["z"] - zl + lax.rem(zl + k % 2, 2)
            came = self.dst_of(frm)
            self.copy(k, came, came, frm).wait_recv()


def heads_exchange(me, src, dst, send, recv, local):
    return Exchange(
        me,
        lambda at: src.at[at["x"], lax.rem(at["z"], 2)],
        lambda at: dst.at[:, own_rows(group_index(at))],
        send,
        recv,
        local,
    )


def norm_parts(x):
    mean = jnp.mean(x, axis=-1, keepdims=True)
    cen = x - mean
    var = jnp.mean(cen * cen, axis=-1, keepdims=True)
    rstd = lax.rsqrt(var + NORM_EPS)
    return cen * rstd, rstd


def rope(v, table, sign):
    lane = lax.rem(lax.broadcasted_iota(jnp.int32, v.shape, 1), HEAD)
    turned = jnp.where(lane < ROT // 2, pltpu.roll(v, 128 - ROT // 2, 1), pltpu.roll(v, ROT // 2, 1))
    return v * table[0] + (sign * turned) * table[1]


def feed(cells, m, bias, h2, h2t, gs, gt, y_ref, dh_ref, db_ref):
    u_at = [(m, k, slice(None), slice(None), slice(0, 128)) for k in range(2)]
    d_at = [(slice(None), slice(None), m, k, slice(128, 256)) for k in range(2)]
    wu = jnp.concatenate([cells[i].reshape(D, 128) for i in u_at], axis=1)
    wd = jnp.concatenate([cells[i].reshape(D, 128) for i in d_at], axis=1)
    u = dot_nn(h2[...], wu) + bias
    ga = dot_nn(gs[...], wd)
    cdf = 0.5 + 0.5 * lax.erf(u * (0.5**0.5))
    pdf = jnp.exp(-0.5 * u * u) * ((2.0 * math.pi) ** -0.5)
    act = (u * cdf).astype(BF16)
    du = (ga * (cdf + u * pdf)).astype(BF16)
    db_ref[m] = jnp.sum(du.astype(F32), axis=0, keepdims=True)
    for k in range(4):
        rows = slice(k * 256, (k + 1) * 256)
        y_ref[rows] += dot_nt(act[rows], wd)
        dh_ref[rows] += dot_nt(du[rows], wu)
    dwu = dot_nn(h2t[...], du).astype(BF16)
    dwd = dot_nn(gt[...], act).astype(BF16)
    for k in range(2):
        lanes = slice(k * 128, (k + 1) * 128)
        cells[u_at[k]] = dwu[:, lanes].reshape(4, 2, 128, 128)
        cells[d_at[k]] = dwd[:, lanes].reshape(4, 2, 128, 128)


def up_bias(vec, core, f, m):
    at = 64 + m * 8 + core * 2 + f
    return jnp.concatenate([vec[pl.ds(at, 1)], vec[pl.ds(at + 4, 1)]], axis=1)


def forward_kernel(
    x_own, g_own, wq_in, wo_in, wu_in, wd_in, vec, live, docs, table,
    r_out, s_out, h1_out, h2_out, h2t_out, gt_out, y_out, dh_out, p_out, part_out, wt_out, wo_out,
    x_oth, g_oth, live_oth, docs_oth, db_out, norms,
    bqkv, y, dh, xs, gs, gt, h1, h2, h2t, cells, wt, wo, sent, tab, wqs, awq, awu, cwq, cwu,
    send, recv, heads_send, heads_recv, local,
):
    me = place()
    core = me["c"]
    seq = group_index(me)
    partner = other_core(me)
    ready = announce(all_neighbours(me) + [partner])

    def load(src, dst, k):
        cp = pltpu.make_async_copy(src, dst, local.at[k])
        cp.start()
        return cp

    got_x = load(x_own, xs.at[0], 0)
    got_g = load(g_own, gs.at[0:512], 1)
    got_t = load(table.at[:, own_rows(seq)], tab, 2)

    wqs[...] = wq_in[...].T.astype(BF16).reshape(3, 2, HEAD, 64)
    gone = wqs[:, 1 - core].reshape(192, 64)
    awq[...] = jnp.concatenate([gone[:96], gone[96:]], axis=1)
    wu = wu_in[...].astype(BF16)
    awu[...] = jnp.where(core == 0, wu[:, 256:], wu[:, :256])
    ready()
    sems = Sems(send, recv)
    kq = sems.push(awq, cwq, partner)
    ku = sems.push(awu, cwu, partner)
    kx = sems.push(x_own, x_oth, partner)
    kg = sems.push(g_own, g_oth, partner)
    kl = sems.push(live, live_oth, partner)
    kd = sems.push(docs, docs_oth, partner)
    own = slot(me)
    kept = wqs[:, core].reshape(192, 64)
    kept_u = jnp.where(core == 0, wu[:, :256], wu[:, 256:])
    wd = wd_in[...].T.astype(BF16)
    sems.arrived(kq, cwq, partner)
    came = jnp.concatenate([cwq[:, :64], cwq[:, 64:]], axis=0)
    cells[(0,) + own + (slice(0, 192),)] = jnp.where(
        core == 0,
        jnp.concatenate([kept, came], axis=1),
        jnp.concatenate([came, kept], axis=1),
    )
    cells[(0,) + own + (slice(192, 256),)] = wo_in[...].astype(BF16)
    sems.arrived(ku, cwu, partner)
    came_u = cwu[...]
    both = jnp.where(
        core == 0,
        jnp.concatenate([kept_u, came_u], axis=0),
        jnp.concatenate([came_u, kept_u], axis=0),
    )
    for f in range(2):
        cells[(1 + f,) + own + (slice(0, 128),)] = both[:, f * 128 : (f + 1) * 128]
        cells[(1 + f,) + own + (slice(128, 256),)] = wd[:, f * 128 : (f + 1) * 128]
    ring_sems = [Sems(send, recv, 6 + 54 * ph) for ph in range(3)]
    ring = [
        Steps(
            [
                ring_gather(cells.at[ph], o[: 3 if ph < 2 else 2], h, ring_sems[ph], me)
                for o, h in GATHER[ph]
            ]
        )
        for ph in range(3)
    ]

    for i in range(4):
        for j in range(8):
            norms[i : i + 1, j * 128 : (j + 1) * 128] = vec[i * 8 + j : i * 8 + j + 1]
    for j in range(8):
        norms[4:5, j * 128 : (j + 1) * 128] = vec[56 + j : 57 + j] + vec[96 + j : 97 + j]
    for i in range(12):
        one, two = vec[32 + 2 * i : 33 + 2 * i], vec[33 + 2 * i : 34 + 2 * i]
        bqkv[:, i * 128 : (i + 1) * 128] = jnp.where(
            core == 0,
            jnp.concatenate([one[:, :64], two[:, :64]], axis=1),
            jnp.concatenate([one[:, 64:], two[:, 64:]], axis=1),
        )

    def normalise(s):
        @pl.loop(0, 4)
        def _(k):
            rows = pl.ds(pl.multiple_of(k * 128, 128), 128)
            at = pl.ds(pl.multiple_of(s * 512 + k * 128, 128), 128)
            xhat, _ = norm_parts(xs[s, rows].astype(F32))
            h1[at] = (xhat * norms[0:1] + norms[1:2]).astype(BF16)
            h2[at] = (xhat * norms[2:3] + norms[3:4]).astype(BF16)

    def turn(src, dst):
        @pl.loop(0, 4)
        def _(k):
            at = pl.ds(pl.multiple_of(k * 256, 256), 256)
            dst[:, at] = src[at].T

    for ph in range(3):
        ring[ph].step()
    got_x.wait()
    normalise(0)
    for ph in range(3):
        ring[ph].step()
    sems.arrived(kx, x_oth, partner)
    got_x = load(x_oth, xs.at[1], 0)
    for ph in range(3):
        ring[ph].step()
    ring[0].step()
    sems.arrived(kg, g_oth, partner)
    got_g.wait()
    got_g = load(g_oth, gs.at[512:1024], 1)
    got_x.wait()
    normalise(1)
    ring[0].step()
    ring[1].step()
    ring[2].finish()
    ring_sems[2].drain()
    turn(h2, h2t)
    ring[0].finish()

    for k in range(8):
        for r in range(8):
            cell = cells[0, k // 2, k % 2, r // 2, r % 2]
            wt[k * 192 : (k + 1) * 192, r * 128 : (r + 1) * 128] = cell[:192]
            wo[r * 64 : (r + 1) * 64, k * 128 : (k + 1) * 128] = cell[192:]
    got_g.wait()
    got_t.wait()

    def project(s):
        rows = slice(s * 512, (s + 1) * 512)
        do = dot_nt(gs[rows], wo[...]).astype(BF16)
        turns = [jnp.concatenate([tab[i]] * MB, axis=0) for i in range(2)]
        for a in range(4):
            if a < 3:
                part = dot_nt(h1[rows], wt[a * 512 : (a + 1) * 512])
                part = (part + bqkv[:, a * 512 : (a + 1) * 512]).astype(BF16)
            else:
                part = do
            for p in range(4):
                piece = part[:, p * 128 : (p + 1) * 128]
                if a < 2:
                    piece = rope(piece.astype(F32), turns, 1.0).astype(BF16)
                for b in range(MB):
                    sent[b, p, s, a] = piece[b * ROWS : (b + 1) * ROWS]

    heads = heads_exchange(me, sent.at[0], r_out, heads_send, heads_recv, local.at[6])
    project(0)
    ring[1].step()
    project(1)
    heads.start()
    turn(gs, gt)
    ring[1].finish()
    ring_sems[1].drain()
    kept_h = [load(h1, h1_out, 3), load(h2, h2_out, 10)]
    kept_h.append(load(h2t, h2t_out, 11))
    kept_w = [load(wt, wt_out, 4), load(wo, wo_out, 5)]
    kept_w.append(load(sent.at[1], s_out, 9))
    kept_h.append(load(gt, gt_out, 12))
    kept_h.append(load(cells.at[2, :, :, me["y"]], part_out, 8))
    y[...] = jnp.zeros_like(y)
    dh[...] = jnp.zeros_like(dh)

    @pl.loop(0, 4)
    def _(m):
        feed(cells.at[1], m, up_bias(vec, core, 0, m), h2, h2t, gs, gt, y, dh, db_out)

    kept_w.append(load(cells.at[1], p_out, 7))
    kept_w.append(load(y, y_out, 13))
    kept_w.append(load(dh, dh_out, 14))
    heads.wait_sent()
    heads.wait_came()
    sems.arrived(kl, live_oth, partner)
    sems.arrived(kd, docs_oth, partner)
    ring_sems[0].drain()
    sems.drain()
    for cp in kept_h + kept_w:
        cp.wait()


def forward(x, g, weights, vec, live, docs, table):
    any_spec = pl.BlockSpec(memory_space=pl.ANY)
    vmem = pl.BlockSpec(memory_space=pltpu.VMEM)
    n = 3 * 3 * 18 + 6
    return pl.pallas_call(
        forward_kernel,
        name="forward",
        out_shape=(
            jax.ShapeDtypeStruct((4, LEN, 128), BF16),
            jax.ShapeDtypeStruct((4, 2, 4, ROWS, 128), BF16),
            jax.ShapeDtypeStruct((1024, D), BF16),
            jax.ShapeDtypeStruct((1024, D), BF16),
            jax.ShapeDtypeStruct((D, 1024), BF16),
            jax.ShapeDtypeStruct((D, 1024), BF16),
            jax.ShapeDtypeStruct((1024, D), F32),
            jax.ShapeDtypeStruct((1024, D), F32),
            jax.ShapeDtypeStruct(LEAD + SLOT, BF16),
            jax.ShapeDtypeStruct((4, 2, 2) + SLOT, BF16),
            jax.ShapeDtypeStruct((1536, D), BF16),
            jax.ShapeDtypeStruct((512, D), BF16),
            jax.ShapeDtypeStruct((512, D), BF16),
            jax.ShapeDtypeStruct((512, D), BF16),
            jax.ShapeDtypeStruct(live.shape, jnp.int32),
            jax.ShapeDtypeStruct(docs.shape, jnp.int32),
            jax.ShapeDtypeStruct((4, 1, 256), F32),
            jax.ShapeDtypeStruct((5, D), F32),
        ),
        in_specs=[any_spec] * 2 + [vmem] * 5 + [any_spec] * 3,
        out_specs=[any_spec] * 16 + [vmem] * 2,
        scratch_shapes=[
            pltpu.VMEM((1, 1536), F32),
            pltpu.VMEM((1024, D), F32),
            pltpu.VMEM((1024, D), F32),
            pltpu.VMEM((2, 512, D), BF16),
            pltpu.VMEM((1024, D), BF16),
            pltpu.VMEM((D, 1024), BF16),
            pltpu.VMEM((1024, D), BF16),
            pltpu.VMEM((1024, D), BF16),
            pltpu.VMEM((D, 1024), BF16),
            pltpu.VMEM((3,) + LEAD + SLOT, BF16),
            pltpu.VMEM((1536, D), BF16),
            pltpu.VMEM((512, D), BF16),
            pltpu.VMEM((MB, 4, 2, 4, ROWS, 128), BF16),
            pltpu.VMEM((2, ROWS, 128), F32),
            pltpu.VMEM((3, 2, HEAD, 64), BF16),
            pltpu.VMEM((96, 128), BF16),
            pltpu.VMEM((64, 256), BF16),
            pltpu.VMEM((96, 128), BF16),
            pltpu.VMEM((64, 256), BF16),
            pltpu.SemaphoreType.DMA((n,)),
            pltpu.SemaphoreType.DMA((n,)),
            pltpu.SemaphoreType.DMA((8,)),
            pltpu.SemaphoreType.DMA((8,)),
            pltpu.SemaphoreType.DMA((15,)),
        ],
        compiler_params=pltpu.CompilerParams(
            collective_id=0, has_side_effects=True, vmem_limit_bytes=62 * MIB
        ),
    )(x, g, *weights, vec, live, docs, table)


def attention_kernel(
    r_ref, docs_own, docs_oth, live_own, live_oth, table_ref, vec,
    s_hbm, part_in, h2_in, h2t_in, g_own, g_oth, gt_in, y_in, dh_in, p0_in,
    u_out, p_out, y_out, dh_out, p0_out, db_out,
    r_next, t_ref, dk, dv, cells, cells0, y, dh, h2, h2t, gs, gt, *rest,
):
    bufs, (send, recv, heads_send, heads_recv, local) = rest[:-5], rest[-5:]
    me = place()
    ready = announce(all_neighbours(me))
    zl = lax.rem(me["z"], 2)

    def load(src, dst, k):
        cp = pltpu.make_async_copy(src, dst, local.at[k])
        cp.start()
        return cp

    got = load(part_in, cells.at[:, :, me["y"]], 0)
    got0 = load(p0_in, cells0, 11)
    ready()
    heads = heads_exchange(me, s_hbm, r_next, heads_send.at[0], heads_recv.at[0], local.at[3])
    heads.start()
    got.wait()
    ring_sems = Sems(send, recv)
    ring = Steps(
        [ring_gather(cells, o[2:], h, ring_sems, me, o[:2]) for o, h in GATHER[2]]
    )
    ring.step()
    scatter_sems = Sems(send, recv, 12)
    scatter = start_scatter(cells0, SCATTER_Y, bufs, scatter_sems, me, None)
    scale = HEAD**-0.5
    lane = lax.broadcasted_iota(jnp.int32, (ROWS, 128), 1)
    first = lane < HEAD

    def pair(v):
        zero = jnp.zeros_like(v)
        return jnp.concatenate([jnp.where(first, v, zero), jnp.where(first, zero, v)], axis=0)

    def merge(v):
        return jnp.where(first, v[:ROWS], v[ROWS:])

    def one(b, q0, k0, width):
        qs, ks = pl.ds(q0, ROWS), pl.ds(k0, width)
        r = r_next if b else r_ref
        q, do = pair(r[0, qs] * jnp.asarray(scale, BF16)), pair(r[3, qs])
        k, v = r[1, ks], r[2, ks]
        row = q0 + lax.broadcasted_iota(jnp.int32, (1, ROWS), 1)
        lo, end = row - (WINDOW - 1), 0
        for d in range(NDOC - 1):
            end = end + jnp.where(zl == 0, docs_own[b, d], docs_oth[b, d])
            lo = jnp.where(row >= end, jnp.maximum(lo, end), lo)
        live = jnp.where(zl == 0, live_own[b, :, ks], live_oth[b, :, ks])
        col = k0 + lax.broadcasted_iota(jnp.int32, (width, 1), 0)
        jeff = jnp.where(live.reshape(width, 1) > 0, col, LEN)
        i = q0 + lax.broadcasted_iota(jnp.int32, (width, ROWS), 1)
        j = k0 + lax.broadcasted_iota(jnp.int32, (width, ROWS), 0)
        ok = ((jeff <= i) & (jeff >= lo)) | (i == j)
        s = jnp.where(jnp.concatenate([ok, ok], axis=1), dot_nt(k, q), BIG_NEG)
        e = jnp.exp(s - jnp.max(s, axis=0, keepdims=True))
        prob = e * (1.0 / jnp.sum(e, axis=0, keepdims=True))
        low = prob.astype(BF16)
        dp = dot_nt(v, do)
        ds = (prob * (dp - jnp.sum(dp * prob, axis=0, keepdims=True))).astype(BF16)
        t_ref[0, b, qs] = merge(dot_tn(v, low).T).astype(BF16)
        dq = merge(dot_tn(k, ds).T) * scale
        table = [table_ref[n, qs] for n in range(2)]
        t_ref[1, b, qs] = rope(dq, table, -1.0).astype(BF16)
        dk[ks] += dot_nn(ds, q)
        dv[ks] += dot_nn(low, do)

    def ship(b):
        out = Exchange(
            me,
            lambda at: t_ref.at[:, b, own_rows(group_index(at))],
            lambda at: u_out.at[group_index(at), :, b],
            heads_send.at[1 + b],
            heads_recv.at[1 + b],
            local.at[1 + b],
        )
        out.start()
        return out

    shipped = []
    for b in range(MB):
        if b == 1:
            heads.wait_came()
        dk[...] = jnp.zeros_like(dk)
        dv[...] = jnp.zeros_like(dv)
        for n in range(4):
            one(b, n * ROWS, 0, (n + 1) * ROWS)
        if b == 0:
            ring.step()
            got0.wait()
            scatter.step()
            loads = [
                load(src, dst, 4 + k)
                for k, (src, dst) in enumerate(
                    (
                        (h2_in, h2),
                        (h2t_in, h2t),
                        (g_own, gs.at[0:512]),
                        (g_oth, gs.at[512:1024]),
                        (gt_in, gt),
                        (y_in, y),
                        (dh_in, dh),
                    )
                )
            ]

        @pl.loop(4, 8)
        def _(n):
            one(
                b,
                pl.multiple_of(n * ROWS, ROWS),
                pl.multiple_of((n - 4) * ROWS, ROWS),
                5 * ROWS,
            )

        table = [table_ref[n] for n in range(2)]
        t_ref[2, b] = rope(dk[...], table, -1.0).astype(BF16)
        t_ref[3, b] = dv[...].astype(BF16)
        shipped.append(ship(b))
    heads.wait_sent()
    scatter.step()
    ring.finish()
    ring_sems.drain()
    for cp in loads:
        cp.wait()

    @pl.loop(0, 4)
    def _(m):
        feed(cells, m, up_bias(vec, me["c"], 1, m), h2, h2t, gs, gt, y, dh, db_out)

    kept = [load(cells, p_out, 4), load(y, y_out, 5), load(dh, dh_out, 6)]
    scatter.finish()
    scatter_sems.drain()
    kept.append(load(cells0.at[:, :, me["y"]], p0_out, 7))
    for out in shipped:
        out.wait_came()
        out.wait_sent()
    for cp in kept:
        cp.wait()


def attention(r, docs, docs_oth, live, live_oth, table, vec, *streamed):
    vmem = pl.BlockSpec(memory_space=pltpu.VMEM)
    smem = pl.BlockSpec(memory_space=pltpu.SMEM)
    any_spec = pl.BlockSpec(memory_space=pl.ANY)
    n = 12 + 12
    return pl.pallas_call(
        attention_kernel,
        name="attention",
        out_shape=(
            jax.ShapeDtypeStruct((8, 4, MB, ROWS, 128), BF16),
            jax.ShapeDtypeStruct(LEAD + SLOT, BF16),
            jax.ShapeDtypeStruct((1024, D), F32),
            jax.ShapeDtypeStruct((1024, D), F32),
            jax.ShapeDtypeStruct((4, 2, 2) + SLOT, BF16),
            jax.ShapeDtypeStruct((4, 1, 256), F32),
        ),
        in_specs=[vmem, smem, smem, vmem, vmem, vmem, vmem] + [any_spec] * 10,
        out_specs=[any_spec] * 5 + [vmem],
        scratch_shapes=[
            pltpu.VMEM((4, LEN, 128), BF16),
            pltpu.VMEM((4, MB, LEN, 128), BF16),
            pltpu.VMEM((LEN, 128), F32),
            pltpu.VMEM((LEN, 128), F32),
            pltpu.VMEM(LEAD + SLOT, BF16),
            pltpu.VMEM(LEAD + SLOT, BF16),
            pltpu.VMEM((1024, D), F32),
            pltpu.VMEM((1024, D), F32),
            pltpu.VMEM((1024, D), BF16),
            pltpu.VMEM((D, 1024), BF16),
            pltpu.VMEM((1024, D), BF16),
            pltpu.VMEM((D, 1024), BF16),
        ]
        + scatter_buffers(SCATTER_Y)
        + [
            pltpu.SemaphoreType.DMA((n,)),
            pltpu.SemaphoreType.DMA((n,)),
            pltpu.SemaphoreType.DMA((3, 8)),
            pltpu.SemaphoreType.DMA((3, 8)),
            pltpu.SemaphoreType.DMA((12,)),
        ],
        compiler_params=pltpu.CompilerParams(
            collective_id=1, has_side_effects=True, vmem_limit_bytes=63 * MIB
        ),
    )(r, docs, docs_oth, live, live_oth, table, vec, *streamed)


def vector_sum(vecs, sems, me):
    for n, a in enumerate("xyz"):
        i = me[a]
        ks = []
        for by in (1, 2, 3):
            ks.append(sems.push(vecs.at[n, i], vecs.at[n, i], device(stepped(me, a, by))))
        yield 0
        for k, by in zip(ks, (1, 2, 3)):
            frm = stepped(me, a, -by)
            sems.arrived(k, vecs.at[n, frm[a]], device(frm))
        total = vecs[n, 0] + vecs[n, 1] + vecs[n, 2] + vecs[n, 3]
        if n < 2:
            vecs[n + 1, me["xyz"[n + 1]]] = total
        else:
            vecs[3, me["c"]] = total


def backward_kernel(
    x_own, g_own, x_oth, g_oth, h_in, u_in, wt_in, wo_in, y_in, dh_in, p0_in, p1_in, norms, db0, db1,
    y_out, dx_out, slots, v_out,
    xs, gs, hs, us, wt, wo, ys, dhs, dqkv, os, cells, e_send, e_came, vecs, *rest,
):
    bufs, (send, recv, local) = rest[:-3], rest[-3:]
    me = place()
    core = me["c"]
    partner = other_core(me)
    ready = announce(ring_neighbours(me) + [partner])

    def load(src, dst, k):
        cp = pltpu.make_async_copy(src, dst, local.at[k])
        cp.start()
        return cp

    zeroth = [load(p1_in, cells.at[2], 1), load(p0_in, cells.at[1, :, :, me["y"]], 0)]
    first = [
        load(u_in, us, 2),
        load(h_in, hs, 3),
        load(g_own, gs.at[0:512], 4),
        load(g_oth, gs.at[512:1024], 5),
    ]
    ready()
    sems = Sems(send, recv)
    for cp in zeroth:
        cp.wait()
    cut = len(scatter_buffers(SCATTER))
    ring_ud = start_scatter(cells.at[2], SCATTER, bufs[cut : 2 * cut], sems, me, slots.at[core, 2])
    ring_ud.live += start_scatter(
        cells.at[1], SCATTER_XZ, bufs[2 * cut :], sems, me, slots.at[core, 1]
    ).live
    ring_ud.step()
    for cp in first:
        cp.wait()
    second = [
        load(wt_in, wt, 6),
        load(wo_in, wo, 7),
        load(x_own, xs.at[0], 8),
        load(x_oth, xs.at[1], 9),
        load(dh_in.at[512:1024], dhs, 10),
        load(y_in.at[512:1024], ys, 11),
    ]
    for s in range(2):
        rows = slice(s * 512, (s + 1) * 512)
        for p in range(4):
            for a in range(4):
                piece = us[p, s, a].reshape(512, 128)
                if a == 0:
                    os[rows, p * 128 : (p + 1) * 128] = piece
                else:
                    at = (a - 1) * 512 + p * 128
                    dqkv[rows, at : at + 128] = piece
    for m in range(4):
        part = dot_tn(dqkv[:, m * 384 : (m + 1) * 384], hs[...]).astype(BF16)
        for k in range(2):
            for r in range(8):
                cells[0, m, k, r // 2, r % 2, 0:192] = part[
                    k * 192 : (k + 1) * 192, r * 128 : (r + 1) * 128
                ]
    part = dot_tn(os[...], gs[...]).astype(BF16)
    for k in range(8):
        for r in range(8):
            cells[0, k // 2, k % 2, r // 2, r % 2, 192:256] = part[
                r * 64 : (r + 1) * 64, k * 128 : (k + 1) * 128
            ]
    ring_ud.step()
    ring = start_scatter(cells.at[0], SCATTER, bufs[:cut], sems, me, slots.at[core, 0])
    ring.step()
    for cp in second:
        cp.wait()
    sums = jnp.zeros((5, D), F32)
    for s in (1, 0):
        rows = slice(s * 512, (s + 1) * 512)
        if s == 0:
            second = [load(dh_in.at[0:512], dhs, 10), load(y_in.at[0:512], ys, 11)]
        attn = dot_nn(os[rows], wo[...])
        dh1 = dot_nn(dqkv[rows], wt[...])
        if s == 0:
            for cp in second:
                cp.wait()
        y = ys[...] + attn
        dh2 = dhs[...]
        xhat, _ = norm_parts(xs[s].astype(F32))
        dx = dh1 * norms[0:1] + dh2 * norms[2:3]
        sums += jnp.concatenate(
            [
                jnp.sum(dh1 * xhat, axis=0, keepdims=True),
                jnp.sum(dh1, axis=0, keepdims=True),
                jnp.sum(dh2 * xhat, axis=0, keepdims=True),
                jnp.sum(dh2, axis=0, keepdims=True),
                jnp.sum(gs[rows].astype(F32), axis=0, keepdims=True) * (1.0 - s),
            ],
            axis=0,
        )
        if s == 1:
            e_send[0] = y.astype(BF16)
            e_send[1] = dx.astype(BF16)
            ke = sems.push(e_send, e_came, partner)
            ring_ud.step()
            ring.step()
        else:
            ys[...] = y
            dhs[...] = dx
    bias = jnp.sum(dqkv[...].astype(F32), axis=0, keepdims=True)
    vecs[0, me["x"]] = jnp.zeros((16, D), F32)
    vecs[0, me["x"], 0:5] = sums
    vecs[0, me["x"], 5:6] = bias[:, :1024]
    vecs[0, me["x"], 6:7, 0:512] = bias[:, 1024:]
    for f, db in enumerate((db0, db1)):
        for m in range(4):
            vecs[0, me["x"], 8 + f * 4 + m : 9 + f * 4 + m, 0:256] = db[m]
    line = Steps([vector_sum(vecs, sems, me)])
    line.step()
    ring_ud.step()
    ring.step()
    sems.arrived(ke, e_came, partner)

    @pl.loop(0, 4)
    def _(k):
        rows = pl.ds(pl.multiple_of(k * 128, 128), 128)
        x = xs[0, rows].astype(F32)
        ys[rows] = x + ys[rows] + e_came[0, rows].astype(F32) + norms[4:5]
        dxh = dhs[rows] + e_came[1, rows].astype(F32)
        xhat, rstd = norm_parts(x)
        dhs[rows] = gs[rows].astype(F32) + rstd * (
            dxh
            - jnp.mean(dxh, axis=-1, keepdims=True)
            - xhat * jnp.mean(dxh * xhat, axis=-1, keepdims=True)
        )

    kept = [load(ys, y_out, 0), load(dhs, dx_out, 1)]
    while ring.live or line.live or ring_ud.live:
        ring_ud.step()
        line.step()
        ring.step()
    kw = sems.push(slots.at[core], slots.at[core], partner)
    kv = sems.push(vecs.at[3, core], vecs.at[3, core], partner)
    sems.arrived(kw, slots.at[1 - core], partner)
    sems.arrived(kv, vecs.at[3, 1 - core], partner)
    for cp in kept:
        cp.wait()
    v_out[...] = vecs[3, 0:2]
    sems.drain()


def backward(streamed, norms, db0, db1):
    any_spec = pl.BlockSpec(memory_space=pl.ANY)
    vmem = pl.BlockSpec(memory_space=pltpu.VMEM)
    n = 2 * 3 * 12 + 2 * 6 + 9 + 3
    return pl.pallas_call(
        backward_kernel,
        name="backward",
        out_shape=(
            jax.ShapeDtypeStruct((512, D), F32),
            jax.ShapeDtypeStruct((512, D), F32),
            jax.ShapeDtypeStruct((2, 3) + SLOT, F32),
            jax.ShapeDtypeStruct((2, 16, D), F32),
        ),
        in_specs=[any_spec] * 12 + [vmem] * 3,
        out_specs=[any_spec] * 2 + [vmem] * 2,
        scratch_shapes=[
            pltpu.VMEM((2, 512, D), BF16),
            pltpu.VMEM((1024, D), BF16),
            pltpu.VMEM((1024, D), BF16),
            pltpu.VMEM((4, 2, 4, MB, ROWS, 128), BF16),
            pltpu.VMEM((1536, D), BF16),
            pltpu.VMEM((512, D), BF16),
            pltpu.VMEM((512, D), F32),
            pltpu.VMEM((512, D), F32),
            pltpu.VMEM((1024, 1536), BF16),
            pltpu.VMEM((1024, 512), BF16),
            pltpu.VMEM((3,) + LEAD + SLOT, BF16),
            pltpu.VMEM((2, 512, D), BF16),
            pltpu.VMEM((2, 512, D), BF16),
            pltpu.VMEM((4, 4, 16, D), F32),
        ]
        + scatter_buffers(SCATTER + SCATTER + SCATTER_XZ)
        + [
            pltpu.SemaphoreType.DMA((n,)),
            pltpu.SemaphoreType.DMA((n,)),
            pltpu.SemaphoreType.DMA((12,)),
        ],
        compiler_params=pltpu.CompilerParams(
            collective_id=2, has_side_effects=True, vmem_limit_bytes=63 * MIB
        ),
    )(*streamed, norms, db0, db1)


def adam(weight, first, second, grad, rate):
    first_new = BETA_ONE * first + (1.0 - BETA_ONE) * grad
    second_new = BETA_TWO * second + (1.0 - BETA_TWO) * grad * grad
    first_hat = first_new / (1.0 - BETA_ONE**STEP)
    second_hat = second_new / (1.0 - BETA_TWO**STEP)
    weight_new = weight - rate * (first_hat / (jnp.sqrt(second_hat) + ADAM_EPS) + DECAY * weight)
    return (first_new, second_new, weight_new)


RATES = (D**-0.5, max(1, D * 16 // LEN) ** -0.5, D**-0.5, FF**-0.5, VECTOR_RATE)


def final_kernel(y_ref, dx_ref, slots, vecs, *rest):
    masters, outs, (grad, line) = rest[:15], rest[15:-2], rest[-2:]
    core = lax.axis_index("c")
    outs[0][...] = y_ref[...]
    outs[1][...] = dx_ref[...]

    def update(k, total):
        new = adam(*[r[...] for r in masters[3 * k : 3 * k + 3]], total, RATES[k])
        for ref, value in zip(outs[2 + 3 * k : 5 + 3 * k], new):
            ref[...] = value

    step = pl.program_id(0)

    @pl.when(step == 0)
    def _():
        cols = []
        for t in range(3):
            rows = slice(t * 64, (t + 1) * 64)
            both = jnp.concatenate([slots[0, 0, rows], slots[1, 0, rows]], axis=0).T
            cols.append(jnp.where(core == 0, both[:64], both[64:]))
        update(0, jnp.concatenate(cols, axis=1))
        update(1, slots[core, 0, 192:256])

    @pl.when(step == 0)
    def _():
        rows = pl.ds(pl.multiple_of(core * 64, 64), 64)
        update(2, jnp.concatenate([slots[c, 1 + f, rows] for c in range(2) for f in range(2)], axis=1))

    @pl.when(step == 1)
    def _():
        for f in range(2):
            grad[f * 128 : (f + 1) * 128] = slots[core, 1 + f, 128:256].T
        update(3, grad[...])

    @pl.when(step == 1)
    def _():
        whole = vecs[0, 0:5] + vecs[1, 0:5]
        for i, at in ((0, 0), (1, 8), (2, 16), (3, 24), (4, 56), (4, 96)):
            for j in range(8):
                line[at + j : at + j + 1] = whole[i : i + 1, j * 128 : (j + 1) * 128]
        for i in range(12):
            lanes = slice(i % 8 * 128, (i % 8 + 1) * 128)
            zero, one = vecs[0, 5 + i // 8, lanes], vecs[1, 5 + i // 8, lanes]
            line[32 + 2 * i] = jnp.concatenate([zero[:64], one[:64]])
            line[33 + 2 * i] = jnp.concatenate([zero[64:], one[64:]])
        for n in range(8):
            for c in range(2):
                for f in range(2):
                    line[64 + n * 4 + c * 2 + f] = vecs[
                        c, 8 + f * 4 + n // 2, n % 2 * 128 : (n % 2 + 1) * 128
                    ]
        update(4, line[...])


def final(y, dx, slots, vecs, masters):
    def tok():
        return pl.BlockSpec((256, D), lambda s: (s, 0))

    def whole(a):
        return pl.BlockSpec(a.shape, lambda s: (0,) * len(a.shape))

    return pl.pallas_call(
        final_kernel,
        name="final",
        grid=(2,),
        out_shape=[jax.ShapeDtypeStruct((512, D), F32)] * 2
        + [jax.ShapeDtypeStruct(m.shape, F32) for m in masters],
        in_specs=[tok(), tok()]
        + [whole(a) for a in (slots, vecs, *masters)],
        out_specs=[tok(), tok()] + [whole(m) for m in masters],
        scratch_shapes=[pltpu.VMEM((256, 128), F32), pltpu.VMEM((104, 128), F32)],
        compiler_params=pltpu.CompilerParams(vmem_limit_bytes=63 * MIB),
    )(y, dx, slots, vecs, *masters)


def rope_table():
    half = ROT // 2
    inverse = np.float32(10000.0) ** (-(np.arange(half, dtype=np.float32) * 2) / np.float32(ROT))
    angles = np.arange(LEN, dtype=np.float32)[:, None] * inverse.astype(np.float32)[None, :]
    table = np.zeros((2, LEN, 2, HEAD), np.float32)
    table[0] = 1.0
    table[0, :, :, :half] = np.cos(angles)[:, None]
    table[0, :, :, half:ROT] = np.cos(angles)[:, None]
    table[1, :, :, :half] = -np.sin(angles)[:, None]
    table[1, :, :, half:ROT] = np.sin(angles)[:, None]
    return jnp.asarray(table.reshape(2, LEN, 128))


def shards(
    inputs, cotangent, doc_lengths, present,
    w_qkv, m_qkv, v_qkv, w_out, m_out, v_out, w_up, m_up, v_up, w_down, m_down, v_down,
    vector, m_vector, v_vector,
):
    x_own, g_own = inputs.reshape(512, D), cotangent.reshape(512, D)
    docs = doc_lengths[:, 0]
    table = rope_table()
    vec, m_vec, v_vec = (a.reshape(104, 128) for a in (vector, m_vector, v_vector))

    (
        r, sent, h1, h2, h2t, gt, y, dh2, p0, part, wt, wo, x_oth, g_oth, live_oth, docs_oth, db0, norms,
    ) = forward(x_own, g_own, (w_qkv, w_out, w_up, w_down), vec, present, docs, table)
    u, p1, y, dh2, p0, db1 = attention(
        r, docs, docs_oth, present, live_oth, table, vec, sent, part, h2, h2t, g_own, g_oth, gt, y, dh2, p0
    )
    u = u.reshape(4, 2, 4, MB, ROWS, 128)
    y, dx, slots, vecs = backward(
        (x_own, g_own, x_oth, g_oth, h1, u, wt, wo, y, dh2, p0, p1), norms, db0, db1
    )
    masters = (
        w_qkv, m_qkv, v_qkv, w_out, m_out, v_out, w_up, m_up, v_up, w_down, m_down, v_down,
        vec, m_vec, v_vec,
    )
    new = final(y, dx, slots, vecs, masters)
    shape = (MB, 1, ROWS, D)
    return (
        new[0].reshape(shape),
        new[1].reshape(shape),
        *new[2:14],
        *(a.reshape(VEC) for a in new[14:]),
    )


def solution(mesh):
    finer = Mesh(mesh.devices.reshape(4, 2, 4, 2, 2), SEQ + FSDP)
    tokens = P(None, FSDP, SEQ, None)
    weight = P(FSDP, SEQ)
    in_specs = (tokens, tokens, P(None, FSDP, None), P(None, FSDP, None)) + (weight,) * 12 + (P(),) * 3
    out_specs = (tokens, tokens) + (weight,) * 12 + (P(),) * 3
    return jax.shard_map(
        shards, mesh=finer, in_specs=in_specs, out_specs=out_specs, check_vma=False
    )
```
